32 devices in a mesh: batch: 4 (over y, x), seq: 8 (over z, core).
Axes of the slice: x: 2, y: 2, z: 4, core: 2. Of those that a mesh axis runs over, the one named last changes fastest.
Arguments:
- tokens: bfloat16 [4, 2048, 2048], P('batch', 'seq'), may hold values from -6 to 6
- prefix: bfloat16 [4, 400, 2048], P('batch', 'seq'), may hold values from -6 to 6
- seg_lengths: int32 [4, 2], P('batch'), may hold values from 0 to 2048, as said below
- attn_gain: bfloat16 [2048], P(('batch', 'seq')), may hold values from 0.5 to 1.5
- attn_shift: bfloat16 [2048], P(('batch', 'seq')), may hold values from -0.125 to 0.125
- query_weight: bfloat16 [2048, 2048], P(('batch', 'seq')), may hold values from -0.125 to 0.125
- key_weight: bfloat16 [2048, 2048], P(('batch', 'seq')), may hold values from -0.125 to 0.125
- value_weight: bfloat16 [2048, 2048], P(('batch', 'seq')), may hold values from -0.125 to 0.125
- query_bias: bfloat16 [2048], P(('batch', 'seq')), may hold values from -1.75 to 1.75
- value_bias: bfloat16 [2048], P(('batch', 'seq')), may hold values from -0.125 to 0.125
- output_weight: bfloat16 [2048, 2048], P(('batch', 'seq')), may hold values from -3 to 3
- output_bias: bfloat16 [2048], P(('batch', 'seq')), may hold values from -1.75 to 1.75
- mlp_gain: bfloat16 [2048], P(('batch', 'seq')), may hold values from 0.5 to 1.5
- mlp_shift: bfloat16 [2048], P(('batch', 'seq')), may hold values from -1.75 to 1.75
- up_weight: bfloat16 [2048, 8192], P(('batch', 'seq')), may hold values from -0.125 to 0.125
- up_bias: bfloat16 [8192], P(('batch', 'seq')), may hold values from -1.75 to 1.75
- down_weight: bfloat16 [8192, 2048], P(('batch', 'seq')), may hold values from -0.0625 to 0.0625
- down_bias: bfloat16 [2048], P(('batch', 'seq')), may hold values from -1.75 to 1.75
- cot_tokens: bfloat16 [4, 2048, 2048], P('batch', 'seq'), may hold values from -6 to 6
- cot_prefix: bfloat16 [4, 400, 2048], P('batch', 'seq'), may hold values from -6 to 6
Outputs:
- out_tokens: bfloat16 [4, 2048, 2048], P('batch', 'seq')
- out_prefix: bfloat16 [4, 400, 2048], P('batch', 'seq')
- grad_tokens: float32 [4, 2048, 2048], P('batch', 'seq')
- grad_prefix: float32 [4, 400, 2048], P('batch', 'seq')
- grad_attn_gain: float32 [2048], P(('batch', 'seq'))
- grad_attn_shift: float32 [2048], P(('batch', 'seq'))
- grad_query_weight: float32 [2048, 2048], P(('batch', 'seq'))
- grad_key_weight: float32 [2048, 2048], P(('batch', 'seq'))
- grad_value_weight: float32 [2048, 2048], P(('batch', 'seq'))
- grad_query_bias: float32 [2048], P(('batch', 'seq'))
- grad_value_bias: float32 [2048], P(('batch', 'seq'))
- grad_output_weight: float32 [2048, 2048], P(('batch', 'seq'))
- grad_output_bias: float32 [2048], P(('batch', 'seq'))
- grad_mlp_gain: float32 [2048], P(('batch', 'seq'))
- grad_mlp_shift: float32 [2048], P(('batch', 'seq'))
- grad_up_weight: float32 [2048, 8192], P(('batch', 'seq'))
- grad_up_bias: float32 [8192], P(('batch', 'seq'))
- grad_down_weight: float32 [8192, 2048], P(('batch', 'seq'))
- grad_down_bias: float32 [2048], P(('batch', 'seq'))
The draws below stay inside these ranges and needn't reach their ends.
Inputs may be any that keep to these rules, and one draw needn't show every extreme that they name: `seg_lengths`: in each item the nonzero lengths come first, each between 1024 and 2048, and they sum to at most 2048; the remaining slots are padding.
All inputs are finite; a program needn't handle non-finite values.
Results may differ from the reference program's by a relative error of at most 0.04.
Values may be sent and summed in bfloat16 or wider, within the bound.
No kernel may reach another device: no remote copies, remote signals or barrier semaphores. Data moves between devices by JAX's collectives and lax.ppermute only.
A program may use at most 448 MiB of HBM per device.

```python
import math
import jax
import jax.numpy as jnp
from jax import lax

D = 2048
FF = 8192
HEADS = 32
HEAD_DIM = 64
SEGMIN = 1024
SEGMAX = 2048
ITEMS = 4
ITEM_LEN = 2048
PREFIX = 400
SEGS = 2


def draw_seg_lengths(key, part):
    first_key, second_key = jax.random.split(key)
    drawn = jax.random.randint(first_key, (ITEMS, SEGS), SEGMIN, SEGMAX + 1)
    chosen = jax.random.randint(second_key, (), 0, ITEMS)
    item_ids = jnp.arange(ITEMS)[:, None]
    slot_ids = jnp.arange(SEGS)[None, :]
    drawn = jnp.where((item_ids == chosen) & (slot_ids == 0), SEGMAX, drawn)
    ends = jnp.cumsum(drawn, axis=1)
    return jnp.where(ends <= ITEM_LEN, drawn, 0).astype(jnp.int32)


def block_scale(rng, extent, cuts, least, top_value):
    level, own = 1.0, jax.random.fold_in(rng, 6)
    for dim, parts in cuts:
        heights = jnp.exp(jax.random.uniform(jax.random.fold_in(own, dim), (parts,), jnp.float32, least / len(cuts), top_value / len(cuts)))
        level = level * jnp.repeat(heights, extent[dim] // parts).reshape([-1 if axis == dim else 1 for axis in range(len(extent))])
    return level


def bell_draw(key, shape, width, reach, cuts=(), held_as=jnp.bfloat16):
    loudness = block_scale(key, shape, cuts, -0.22, 0.18) if cuts else 1.0
    array = jax.random.normal(key, shape, jnp.float32) * width * loudness
    return jnp.minimum(jnp.maximum(array, -reach), reach).astype(held_as)


def setup_inputs(seed: int = 0) -> dict:
    streams_of = jax.random.split(jax.random.key(seed), 21)
    tokens = bell_draw(streams_of[0], (ITEMS, ITEM_LEN, D), 1.0, 6.0, ((0, 4), (1, 8)))
    prefix = bell_draw(streams_of[1], (ITEMS, PREFIX, D), 1.0, 6.0, ((0, 4), (1, 8)))
    seg_lengths = draw_seg_lengths(jax.random.fold_in(streams_of[20], 71), 0)
    attn_gain = jnp.clip(1.0 + 0.1 * jax.random.normal(streams_of[3], (D,), jnp.float32), 0.5, 1.5).astype(jnp.bfloat16)
    attn_shift = bell_draw(streams_of[4], (D,), 0.02, 0.125, ((0, 32),))
    query_weight = bell_draw(streams_of[5], (D, D), D ** -0.5, 0.125, ((0, 32),))
    key_weight = bell_draw(streams_of[6], (D, D), D ** -0.5, 0.125, ((0, 32),))
    value_weight = bell_draw(streams_of[7], (D, D), D ** -0.5, 0.125, ((0, 32),))
    query_bias = bell_draw(streams_of[8], (D,), 0.3, 1.75, ((0, 32),))
    value_bias = bell_draw(streams_of[9], (D,), 0.02, 0.125, ((0, 32),))
    output_weight = bell_draw(streams_of[10], (D, D), 4 ** -0.5, 3.0, ((0, 32),))
    output_bias = bell_draw(streams_of[11], (D,), 0.3, 1.75, ((0, 32),))
    mlp_gain = jnp.clip(1.0 + 0.1 * jax.random.normal(streams_of[12], (D,), jnp.float32), 0.5, 1.5).astype(jnp.bfloat16)
    mlp_shift = bell_draw(streams_of[13], (D,), 0.3, 1.75, ((0, 32),))
    up_weight = bell_draw(streams_of[14], (D, FF), D ** -0.5, 0.125, ((0, 32),))
    up_bias = bell_draw(streams_of[15], (FF,), 0.3, 1.75, ((0, 32),))
    down_weight = bell_draw(streams_of[16], (FF, D), FF ** -0.5, 0.0625, ((0, 32),))
    down_bias = bell_draw(streams_of[17], (D,), 0.3, 1.75, ((0, 32),))
    cot_tokens = bell_draw(streams_of[18], (ITEMS, ITEM_LEN, D), 1.0, 6.0, ((0, 4), (1, 8)))
    cot_prefix = bell_draw(streams_of[19], (ITEMS, PREFIX, D), 1.0, 6.0, ((0, 4), (1, 8)))
    return dict(tokens=tokens, prefix=prefix, seg_lengths=seg_lengths, attn_gain=attn_gain, attn_shift=attn_shift, query_weight=query_weight, key_weight=key_weight, value_weight=value_weight, query_bias=query_bias, value_bias=value_bias, output_weight=output_weight, output_bias=output_bias, mlp_gain=mlp_gain, mlp_shift=mlp_shift, up_weight=up_weight, up_bias=up_bias, down_weight=down_weight, down_bias=down_bias, cot_tokens=cot_tokens, cot_prefix=cot_prefix)


EPS = 1e-05
HIGH = lax.Precision.HIGHEST

@jax.custom_vjp
def low(v):
    return lax.optimization_barrier(v.astype(jnp.bfloat16)).astype(jnp.float32)

@jax.custom_vjp
def low_back(v):
    return v

def low_keep(v):
    return (low(v), None)

def low_pass(kept, grad):
    return (grad,)

def back_keep(v):
    return (v, None)

def back_low(kept, grad):
    return (low(grad),)
low.defvjp(low_keep, low_pass)
low_back.defvjp(back_keep, back_low)

def matmul(left, right):
    return jnp.dot(left, right, precision=HIGH)

def layer_norm(values, gain, shift):
    center = values - lax.optimization_barrier(jnp.mean(values, axis=-1, keepdims=True))
    spread = lax.optimization_barrier(jnp.mean(center * center, axis=-1, keepdims=True))
    return center * lax.rsqrt(spread + EPS) * gain + shift

def row_labels(lengths):
    ends = jnp.cumsum(lengths)
    places = jnp.arange(ITEM_LEN, dtype=jnp.int32)
    segment = lax.optimization_barrier(jnp.sum((ends[None, :] <= places[:, None]).astype(jnp.int32), axis=1))
    validity = (places < ends[-1]).astype(jnp.float32)
    key_seg = jnp.concatenate([segment, jnp.full((PREFIX,), -1, jnp.int32)])
    key_pos = jnp.concatenate([places, jnp.arange(PREFIX, dtype=jnp.int32)])
    validity = jnp.concatenate([validity, jnp.ones((PREFIX,), jnp.float32)])
    return (key_seg, key_pos, validity)

def visible(query_seg, query_pos, key_seg, key_pos):
    same = (key_seg[None, :] == query_seg[:, None]) & (key_pos[None, :] <= query_pos[:, None])
    memory = (key_seg[None, :] < 0) & (query_seg[:, None] >= 0)
    return same | memory

def split_heads(values):
    return values.reshape(values.shape[0], HEADS, HEAD_DIM).transpose(1, 0, 2)

def attention(queries, keys, values, mask):
    count = queries.shape[0]
    scale = 1.0 / math.sqrt(HEAD_DIM)

    def one_head(operands):
        head_q, head_k, head_v = operands
        scores = low_back(matmul(head_q, head_k.T) * scale)
        scores = jnp.where(mask, scores, -jnp.inf)
        shifted = jnp.exp(scores - lax.optimization_barrier(jnp.max(scores, axis=1, keepdims=True)))
        probs = shifted / lax.optimization_barrier(jnp.sum(shifted, axis=1, keepdims=True))
        return matmul(low(probs), head_v)
    heads = lax.map(jax.checkpoint(one_head), (split_heads(queries), split_heads(keys), split_heads(values)))
    return heads.transpose(1, 0, 2).reshape(count, HEADS * HEAD_DIM)

def item_rows(params, tok, pre, lengths):
    attn_gain, attn_shift, query_weight, key_weight, value_weight, query_bias, value_bias, output_weight, output_bias, mlp_gain, mlp_shift, up_weight, up_bias, down_weight, down_bias = params
    key_seg, key_pos, validity = row_labels(lengths)
    mask = visible(key_seg, key_pos, key_seg, key_pos)
    rows_in = jnp.concatenate([tok, pre], axis=0)
    validity = validity[:, None]
    normed = low(layer_norm(rows_in, attn_gain, attn_shift))
    queries = low(low_back(matmul(normed, query_weight) + query_bias))
    keys = low(low_back(matmul(normed, key_weight)))
    values = low(low_back(matmul(normed, value_weight) + value_bias))
    mixed = low(low_back(attention(queries, keys, values, mask)))
    branch = low_back(matmul(mixed, output_weight) + output_bias)
    resid = rows_in + validity * branch
    normed_m = low(layer_norm(resid, mlp_gain, mlp_shift))
    hidden = low(jax.nn.gelu(low_back(matmul(normed_m, up_weight) + up_bias), approximate=False))
    result = low_back(matmul(hidden, down_weight) + down_bias)
    return resid + validity * result

def reference(tokens, prefix, seg_lengths, attn_gain, attn_shift, query_weight, key_weight, value_weight, query_bias, value_bias, output_weight, output_bias, mlp_gain, mlp_shift, up_weight, up_bias, down_weight, down_bias, cot_tokens, cot_prefix):
    params = tuple((arr.astype(jnp.float32) for arr in (attn_gain, attn_shift, query_weight, key_weight, value_weight, query_bias, value_bias, output_weight, output_bias, mlp_gain, mlp_shift, up_weight, up_bias, down_weight, down_bias)))

    def forward(weights, tok_all, pre_all):

        def per_item(operands):
            tok, pre, lengths = operands
            return item_rows(weights, tok, pre, lengths)
        return lax.map(jax.checkpoint(per_item), (tok_all, pre_all, seg_lengths))
    outputs, pullback = jax.vjp(forward, params, tokens.astype(jnp.float32), prefix.astype(jnp.float32))
    cotangent = jnp.concatenate([cot_tokens, cot_prefix], axis=1).astype(jnp.float32)
    grad_params, grad_tok, grad_pre = pullback(cotangent)
    outputs = outputs.astype(jnp.bfloat16)
    return (outputs[:, :ITEM_LEN], outputs[:, ITEM_LEN:], grad_tok, grad_pre, grad_params[0], grad_params[1], grad_params[2], grad_params[3], grad_params[4], grad_params[5], grad_params[6], grad_params[7], grad_params[8], grad_params[9], grad_params[10], grad_params[11], grad_params[12], grad_params[13], grad_params[14])
```

```python
import functools
import math

import jax
import jax.numpy as jnp
from jax import lax
from jax.experimental import pallas as pl
from jax.experimental.pallas import tpu as pltpu
from jax.sharding import PartitionSpec as P

HEADS = 32
HEAD_DIM = 64
EPS = 1e-05
NEGATIVE = -1e30
FAR = 1 << 20
BLOCK = 256
BF16 = jnp.bfloat16
F32 = jnp.float32


def contract(left, right, left_dim, right_dim):
    return lax.dot_general(
        left, right, (((left_dim,), (right_dim,)), ((), ())), preferred_element_type=F32
    )


def row_pieces(devices, pre, tok):
    pieces = []
    for device in range(devices):
        first = device * (pre + tok)
        pieces.append((first, device * pre, pre))
        pieces.append((first + pre, devices * pre + device * tok, tok))
    return pieces


def block_mask(place, low, high):
    return (place <= high) & ((place >= low) | (place < 0))


def forward_kernel(
    devices, pre, tok, heads, head_dim,
    qkv_ref, place_ref, low_ref, high_ref,
    o_ref, ot_ref, lse_ref,
    q_s, k_s, vt_s, acc_s, m_s, l_s,
):
    width = heads * head_dim
    blocks = devices * (pre + tok) // BLOCK
    for src, dst, cnt in row_pieces(devices, pre, tok):
        q_s[dst : dst + cnt, :] = qkv_ref[src : src + cnt, 0:width]
        k_s[dst : dst + cnt, :] = qkv_ref[src : src + cnt, width : 2 * width]
        o_ref[dst : dst + cnt, :] = qkv_ref[src : src + cnt, 2 * width : 3 * width]
    for b in range(blocks):
        rows = slice(b * BLOCK, (b + 1) * BLOCK)
        vt_s[:, rows] = o_ref[rows, :].astype(F32).T.astype(BF16)
    lane = lax.broadcasted_iota(jnp.int32, (BLOCK, width), 1) // head_dim

    def query_block(i, carry):
        qs = pl.ds(pl.multiple_of(i * BLOCK, BLOCK), BLOCK)
        q = q_s[qs, :]
        qh = [jnp.where(lane == h, q, jnp.zeros_like(q)) for h in range(heads)]
        low = low_ref[:, qs]
        high = high_ref[:, qs]
        acc_s[...] = jnp.zeros_like(acc_s)
        m_s[...] = jnp.full_like(m_s, NEGATIVE)
        l_s[...] = jnp.zeros_like(l_s)

        def key_block(j, inner):
            ks = pl.ds(pl.multiple_of(j * BLOCK, BLOCK), BLOCK)
            k = k_s[ks, :]
            bias = jnp.where(block_mask(place_ref[ks, :], low, high), 0.0, NEGATIVE)
            for h in range(heads):
                s = contract(k, qh[h], 1, 1) + bias
                old = m_s[h : h + 1, :]
                new = jnp.maximum(old, jnp.max(s, axis=0, keepdims=True))
                p = jnp.exp(s - new)
                alpha = jnp.exp(old - new)
                m_s[h : h + 1, :] = new
                l_s[h : h + 1, :] = l_s[h : h + 1, :] * alpha + jnp.sum(p, axis=0, keepdims=True)
                hs = slice(h * head_dim, (h + 1) * head_dim)
                acc_s[hs, :] = acc_s[hs, :] * alpha + contract(vt_s[hs, ks], p.astype(BF16), 1, 0)
            return inner

        lax.fori_loop(0, i + 1, key_block, 0)
        for h in range(heads):
            hs = slice(h * head_dim, (h + 1) * head_dim)
            total = l_s[h : h + 1, :]
            acc_s[hs, :] = acc_s[hs, :] / total
            lse_ref[h : h + 1, qs] = m_s[h : h + 1, :] + jnp.log(total)
        result = acc_s[...]
        ot_ref[:, qs] = result
        q_s[qs, :] = result.T.astype(BF16)
        return carry

    lax.fori_loop(0, blocks, query_block, 0)
    for src, dst, cnt in row_pieces(devices, pre, tok):
        o_ref[src : src + cnt, :] = q_s[dst : dst + cnt, :]


def attention_forward(qkv, place, low, high, devices, pre, tok, heads, head_dim):
    width = heads * head_dim
    rows = devices * (pre + tok)
    vmem = pl.BlockSpec(memory_space=pltpu.VMEM)
    pairs = rows * rows // 2 * heads
    return pl.pallas_call(
        functools.partial(forward_kernel, devices, pre, tok, heads, head_dim),
        out_shape=(
            jax.ShapeDtypeStruct((rows, width), BF16),
            jax.ShapeDtypeStruct((width, rows), F32),
            jax.ShapeDtypeStruct((8, rows), F32),
        ),
        in_specs=[vmem] * 4,
        out_specs=(vmem,) * 3,
        scratch_shapes=[
            pltpu.VMEM((rows, width), BF16),
            pltpu.VMEM((rows, width), BF16),
            pltpu.VMEM((width, rows), BF16),
            pltpu.VMEM((width, BLOCK), F32),
            pltpu.VMEM((8, BLOCK), F32),
            pltpu.VMEM((8, BLOCK), F32),
        ],
        compiler_params=pltpu.CompilerParams(vmem_limit_bytes=48 << 20),
        cost_estimate=pl.CostEstimate(
            flops=16 * pairs * head_dim, bytes_accessed=rows * width * 12, transcendentals=pairs
        ),
    )(qkv, place, low, high)


def backward_kernel(
    devices, pre, tok, heads, head_dim,
    qkv_ref, do_ref, ot_ref, lse_ref, place_ref, low_ref, high_ref,
    out_ref,
    q_s, k_s, v_s, do_s, kt_s, dk_s, dv_s, dqt_s,
):
    width = heads * head_dim
    scale = 1.0 / math.sqrt(head_dim)
    blocks = devices * (pre + tok) // BLOCK
    for src, dst, cnt in row_pieces(devices, pre, tok):
        q_s[dst : dst + cnt, :] = qkv_ref[src : src + cnt, 0:width]
        k_s[dst : dst + cnt, :] = qkv_ref[src : src + cnt, width : 2 * width]
        v_s[dst : dst + cnt, :] = qkv_ref[src : src + cnt, 2 * width : 3 * width]
        do_s[dst : dst + cnt, :] = do_ref[src : src + cnt, :]
    for b in range(blocks):
        rows = slice(b * BLOCK, (b + 1) * BLOCK)
        kt_s[:, rows] = k_s[rows, :].astype(F32).T.astype(BF16)
    dk_s[...] = jnp.zeros_like(dk_s)
    dv_s[...] = jnp.zeros_like(dv_s)
    lane = lax.broadcasted_iota(jnp.int32, (BLOCK, width), 1) // head_dim

    def query_block(i, carry):
        qs = pl.ds(pl.multiple_of(i * BLOCK, BLOCK), BLOCK)
        q = q_s[qs, :]
        do = do_s[qs, :]
        qh = [jnp.where(lane == h, q, jnp.zeros_like(q)) for h in range(heads)]
        doh = [jnp.where(lane == h, do, jnp.zeros_like(do)) for h in range(heads)]
        low = low_ref[:, qs]
        high = high_ref[:, qs]
        prod = do.astype(F32).T * ot_ref[:, qs]
        delta = [
            jnp.sum(prod[h * head_dim : (h + 1) * head_dim, :], axis=0, keepdims=True)
            for h in range(heads)
        ]
        lse = [lse_ref[h : h + 1, qs] for h in range(heads)]
        dqt_s[...] = jnp.zeros_like(dqt_s)

        def key_block(j, inner):
            ks = pl.ds(pl.multiple_of(j * BLOCK, BLOCK), BLOCK)
            k = k_s[ks, :]
            v = v_s[ks, :]
            bias = jnp.where(block_mask(place_ref[ks, :], low, high), 0.0, NEGATIVE)
            dk = None
            dv = None
            for h in range(heads):
                s = contract(k, qh[h], 1, 1)
                dp = contract(v, doh[h], 1, 1)
                p = jnp.exp(s + bias - lse[h])
                p_low = p.astype(BF16)
                ds = (p * (dp - delta[h])).astype(BF16)
                dv_h = contract(p_low, doh[h], 1, 0)
                dk_h = contract(ds, qh[h], 1, 0)
                dv = dv_h if dv is None else dv + dv_h
                dk = dk_h if dk is None else dk + dk_h
                hs = slice(h * head_dim, (h + 1) * head_dim)
                dqt_s[hs, :] += contract(kt_s[hs, ks], ds, 1, 0)
            dk_s[ks, :] += dk
            dv_s[ks, :] += dv
            return inner

        lax.fori_loop(0, i + 1, key_block, 0)
        q_s[qs, :] = (dqt_s[...] * scale).T.astype(BF16)
        return carry

    lax.fori_loop(0, blocks, query_block, 0)
    for src, dst, cnt in row_pieces(devices, pre, tok):
        out_ref[src : src + cnt, 0:width] = q_s[dst : dst + cnt, :]
        out_ref[src : src + cnt, width : 2 * width] = dk_s[dst : dst + cnt, :].astype(BF16)
        out_ref[src : src + cnt, 2 * width : 3 * width] = dv_s[dst : dst + cnt, :].astype(BF16)


def attention_backward(qkv, do, ot, lse, place, low, high, devices, pre, tok, heads, head_dim):
    width = heads * head_dim
    rows = devices * (pre + tok)
    vmem = pl.BlockSpec(memory_space=pltpu.VMEM)
    pairs = rows * rows // 2 * heads
    low_rows = pltpu.VMEM((rows, width), BF16)
    return pl.pallas_call(
        functools.partial(backward_kernel, devices, pre, tok, heads, head_dim),
        out_shape=jax.ShapeDtypeStruct((rows, 3 * width), BF16),
        in_specs=[vmem] * 7,
        out_specs=vmem,
        scratch_shapes=[
            low_rows,
            low_rows,
            low_rows,
            low_rows,
            pltpu.VMEM((width, rows), BF16),
            pltpu.VMEM((rows, width), F32),
            pltpu.VMEM((rows, width), F32),
            pltpu.VMEM((width, BLOCK), F32),
        ],
        compiler_params=pltpu.CompilerParams(vmem_limit_bytes=56 << 20),
        cost_estimate=pl.CostEstimate(
            flops=40 * pairs * head_dim, bytes_accessed=rows * width * 20, transcendentals=pairs
        ),
    )(qkv, do, ot, lse, place, low, high)


def slot_labels(lengths, devices, pre, tok, real):
    slot = jnp.arange(devices * pre, dtype=jnp.int32)
    inside = slot % pre
    place = (slot // pre) * real + inside - devices * real
    is_real = inside < real
    t = jnp.arange(devices * tok, dtype=jnp.int32)
    ends = jnp.cumsum(lengths)
    start = jnp.max(jnp.where(ends[None, :] <= t[:, None], ends[None, :], 0), axis=1)
    places = jnp.concatenate([jnp.where(is_real, place, FAR), t])
    high = jnp.concatenate([jnp.where(is_real, place, -1), t])
    low = jnp.concatenate([jnp.full((devices * pre,), FAR, jnp.int32), start])
    return places[:, None], low[None, :], high[None, :]


def normalize(values):
    center = values - jnp.mean(values, axis=-1, keepdims=True)
    spread = jnp.mean(center * center, axis=-1, keepdims=True)
    inverse = lax.rsqrt(spread + EPS)
    return center * inverse, inverse


def norm_backward(grad, hat, inverse, gain):
    e = grad * gain
    mean_e = jnp.mean(e, axis=-1, keepdims=True)
    mean_eh = jnp.mean(e * hat, axis=-1, keepdims=True)
    return inverse * (e - mean_e - hat * mean_eh)


def gelu_parts(values):
    cdf = 0.5 * (1.0 + lax.erf(values * (1.0 / math.sqrt(2.0))))
    return cdf


def pick(array, index, axis):
    return lax.dynamic_index_in_dim(array, index, axis, keepdims=False)


def build(n_batch, n_seq):
    n_z = n_seq // 2
    n_dev = n_batch * n_seq
    groups = n_dev // 4
    size_of = {"batch": n_batch, "seq": n_seq}

    def bits_of(n):
        bits = []
        bit = 1
        while bit < n:
            bits.append(bit)
            bit *= 2
        return bits

    batch_bits = [("batch", bit) for bit in bits_of(n_batch)]
    quad_bits = [("seq", 1), ("seq", 2)]
    far_bits = [("seq", bit) for bit in bits_of(n_seq) if bit >= 4]
    group_bits = list(reversed(batch_bits)) + list(reversed(far_bits))
    all_bits = list(reversed(batch_bits)) + [("seq", bit) for bit in reversed(bits_of(n_seq))]

    def swap(array, which):
        axis, bit = which
        return lax.ppermute(array, axis, [(i, i ^ bit) for i in range(size_of[axis])])

    def side(which):
        axis, bit = which
        return (lax.axis_index(axis) // bit) % 2

    def shift(array, distance):
        pairs = [
            (z * 2 + c, ((z + distance) % n_z) * 2 + c) for z in range(n_z) for c in range(2)
        ]
        return lax.ppermute(array, "seq", pairs)

    def step_right(array, first, last):
        pairs = [(z * 2 + c, z * 2 + 2 + c) for z in range(first, last) for c in range(2)]
        return lax.ppermute(array, "seq", pairs)

    def step_left(array, first, last):
        pairs = [(z * 2 + c, z * 2 - 2 + c) for z in range(first, last) for c in range(2)]
        return lax.ppermute(array, "seq", pairs)

    def join(mine, other, which, axis):
        first = side(which) == 0
        return jnp.where(
            first, jnp.stack([mine, other], axis), jnp.stack([other, mine], axis)
        )

    def gather_bits(array, order, ranked):
        taken = []
        current = array
        shape = array.shape
        for which in order:
            other = swap(current, which)
            rank = ranked.index(which)
            place = sum(1 for t in taken if ranked.index(t) < rank)
            current = join(current, other, which, place)
            taken.append(which)
        return current.reshape((2 ** len(order),) + shape)

    def scatter_bits(array, order, ranked):
        shape = array.shape[1:]
        current = array.reshape((2,) * len(ranked) + shape)
        left = list(ranked)
        for which in order:
            place = left.index(which)
            mine = side(which)
            away = pick(current, 1 - mine, place).astype(BF16)
            keep = pick(current, mine, place).astype(F32)
            current = keep + swap(away, which).astype(F32)
            left.remove(which)
        return current

    def gather_pieces(block, order, ranked):
        pieces = [(frozenset(), block)]
        for which in order:
            pieces = pieces + [(took | {which}, swap(piece, which)) for took, piece in pieces]
        placed = []
        for took, piece in pieces:
            index = 0
            for which in ranked:
                here = side(which)
                index = index * 2 + ((1 - here) if which in took else here)
            placed.append((index, piece))
        return placed

    def assemble(placed):
        rows = placed[0][1].shape[0]
        out = jnp.zeros((rows * len(placed),) + placed[0][1].shape[1:], placed[0][1].dtype)
        for index, piece in placed:
            out = lax.dynamic_update_slice_in_dim(out, piece, index * rows, 0)
        return out

    def body(
        tokens, prefix, seg_lengths, attn_gain, attn_shift, query_weight, key_weight, value_weight,
        query_bias, value_bias, output_weight, output_bias, mlp_gain, mlp_shift, up_weight, up_bias,
        down_weight, down_bias, cot_tokens, cot_prefix,
    ):
        tok = tokens.shape[1]
        real = prefix.shape[1]
        pre = -(-real // 16) * 16
        width = pre + tok
        model = tokens.shape[2]
        heads = HEADS // n_seq
        span = heads * HEAD_DIM
        part = model // n_dev
        unit = up_bias.shape[0]
        hidden_here = groups * unit
        s_here = lax.axis_index("seq")
        z_here = s_here // 2
        c_here = s_here % 2
        core = ("seq", 1)
        near = ("seq", 2)
        lengths = seg_lengths[0]

        def rows_of(pre_part, tok_part):
            return jnp.concatenate([jnp.pad(pre_part, ((0, pre - real), (0, 0))), tok_part], axis=0)

        own = rows_of(prefix[0], tokens[0])
        cot = rows_of(cot_prefix[0], cot_tokens[0])
        row = jnp.arange(width, dtype=jnp.int32)
        position = row - pre + s_here * tok
        valid = jnp.where(row < pre, row < real, position < jnp.sum(lengths))
        validity = valid.astype(F32)[:, None]

        small = jnp.concatenate(
            [attn_gain, attn_shift, query_bias, value_bias, output_bias, mlp_gain, mlp_shift, down_bias, up_bias]
        )[None]
        small = gather_bits(small, list(reversed(all_bits)), all_bits).reshape(n_dev, -1)
        vectors = [small[:, n * part : (n + 1) * part].reshape(model).astype(F32) for n in range(8)]
        gain_a, shift_a, bias_q, bias_v, bias_o, gain_m, shift_m, bias_down = vectors
        bias_up = pick(small[:, 8 * part :].reshape(groups, 4, unit), s_here % 4, 1)
        bias_up = bias_up.reshape(hidden_here).astype(F32)

        stacked = jnp.stack([query_weight, key_weight, value_weight], axis=1)
        stacked = stacked.reshape(part, 3, n_z, 2, span).transpose(2, 3, 0, 1, 4)
        stacked = stacked.reshape(n_z, 2, part, 3 * span)
        mixed = join(pick(stacked, c_here, 1), swap(pick(stacked, 1 - c_here, 1), core), core, 1)
        mixed = mixed.reshape(n_z, 2 * part, 3 * span)
        placed = [(z_here, pick(mixed, z_here, 0))]
        for d in range(1, n_z):
            piece = shift(pick(mixed, (z_here + d) % n_z, 0), d)
            placed.append(((z_here - d) % n_z, piece))
        local = assemble(placed)
        half = local.shape[0] // 2
        ranked_batch = list(reversed(batch_bits))
        weight_qkv = jnp.stack(
            [
                gather_bits(local[:half], batch_bits, ranked_batch),
                gather_bits(local[half:], ranked_batch, ranked_batch),
            ],
            axis=1,
        ).reshape(model, 3 * span)

        gathered = [own]
        from_left = []
        from_right = []
        moving_right = own
        moving_left = own
        for k in range(1, n_z):
            moving_right = step_right(moving_right, k - 1, n_z - 1)
            moving_left = step_left(moving_left, 1, n_z - k + 1)
            from_left.append(moving_right)
            from_right.append(moving_left)
        for k in range(1, n_z):
            gathered.append(jnp.where(z_here >= k, from_left[k - 1], from_right[n_z - k - 1]))

        bias_qkv = jnp.concatenate(
            [
                lax.dynamic_slice_in_dim(bias_q, s_here * span, span, 0),
                jnp.zeros((span,), F32),
                lax.dynamic_slice_in_dim(bias_v, s_here * span, span, 0),
            ]
        )
        factor = jnp.concatenate(
            [jnp.full((span,), 1.0 / math.sqrt(HEAD_DIM), F32), jnp.ones((2 * span,), F32)]
        )
        normed = jnp.zeros((n_z * 2 * width, model), BF16)
        qkv = jnp.zeros((n_z * 2 * width, 3 * span), BF16)
        for k in range(n_z):
            chunk = join(gathered[k], swap(gathered[k], core), core, 0).reshape(2 * width, model)
            hat, unused = normalize(chunk.astype(F32))
            chunk = (hat * gain_a + shift_a).astype(BF16)
            first = ((z_here - k) % n_z) * 2 * width
            normed = lax.dynamic_update_slice_in_dim(normed, chunk, first, 0)
            result = (contract(chunk, weight_qkv, 1, 0) + bias_qkv).astype(BF16).astype(F32) * factor
            qkv = lax.dynamic_update_slice_in_dim(qkv, result.astype(BF16), first, 0)

        places, low, high = slot_labels(lengths, n_seq, pre, tok, real)
        attended, attended_t, log_total = attention_forward(
            qkv, places, low, high, n_seq, pre, tok, heads, HEAD_DIM
        )

        blocks = attended.reshape(n_z, 2, width, span)
        ours = join(pick(blocks, c_here, 1), swap(pick(blocks, 1 - c_here, 1), core), core, 2)
        ours = ours.reshape(n_z, width, 2 * span)
        mixed_low = jnp.zeros((width, model), BF16)
        mixed_low = lax.dynamic_update_slice_in_dim(
            mixed_low, pick(ours, z_here, 0), z_here * 2 * span, 1
        )
        for d in range(1, n_z):
            piece = shift(pick(ours, (z_here + d) % n_z, 0), d)
            mixed_low = lax.dynamic_update_slice_in_dim(
                mixed_low, piece, ((z_here - d) % n_z) * 2 * span, 1
            )

        order_o = [near] + far_bits
        half_model = model // 2
        weight_o = []
        for n, batch_order in enumerate((batch_bits, ranked_batch)):
            columns = output_weight[:, n * half_model : (n + 1) * half_model]
            gathered_o = gather_bits(columns, order_o + batch_order + [core], all_bits)
            weight_o.append(gathered_o.reshape(model, half_model))
        weight_o = jnp.concatenate(weight_o, axis=1)

        rows_in = own.astype(F32)
        branch = contract(mixed_low, weight_o, 1, 0) + bias_o
        resid = rows_in + validity * branch
        hat_m, inverse_m = normalize(resid)
        normed_m_own = (hat_m * gain_m + shift_m).astype(BF16)

        shaped = up_weight.reshape(part, groups, 2, 2, unit)
        shaped = join(pick(shaped, c_here, 3), swap(pick(shaped, 1 - c_here, 3), core), core, 0)
        near_here = side(near)
        shaped = join(pick(shaped, near_here, 3), swap(pick(shaped, 1 - near_here, 3), near), near, 0)
        up_block = shaped.reshape(4 * part, hidden_here)
        order_up = far_bits + batch_bits
        order_down = far_bits + list(reversed(batch_bits))
        weight_up = assemble(gather_pieces(up_block, order_up, group_bits))
        weight_down = assemble(gather_pieces(down_weight, order_down, group_bits))

        def quad_gather(array):
            other = swap(array, near)
            both = join(array, other, near, 0)
            return join(both, swap(both, core), core, 1).reshape((4 * width,) + array.shape[1:])

        def quad_scatter(array):
            shaped = array.reshape(2, 2, width, model)
            mine = pick(shaped, c_here, 1)
            both = mine + swap(pick(shaped, 1 - c_here, 1).astype(BF16), core).astype(F32)
            away = pick(both, 1 - near_here, 0).astype(BF16)
            return pick(both, near_here, 0) + swap(away, near).astype(F32)

        cot_rows = cot.astype(F32)
        mlp_out_grad = (validity * cot_rows).astype(BF16)
        mlp_out_grad_quad = quad_gather(mlp_out_grad)
        normed_m = quad_gather(normed_m_own)

        hidden_pre = contract(normed_m, weight_up, 1, 0) + bias_up
        cdf = 0.5 * (1.0 + lax.erf(hidden_pre * (1.0 / math.sqrt(2.0))))
        hidden = (hidden_pre * cdf).astype(BF16)
        slope = cdf + hidden_pre * jnp.exp(-0.5 * hidden_pre * hidden_pre) * (
            1.0 / math.sqrt(2.0 * math.pi)
        )
        hidden_grad = contract(mlp_out_grad_quad, weight_down, 1, 1)
        pre_grad = (hidden_grad * slope).astype(BF16)
        normed_grad = quad_scatter(contract(pre_grad, weight_up, 1, 1))
        final = resid + validity * (quad_scatter(contract(hidden, weight_down, 1, 0)) + bias_down)
        out_rows = final.astype(BF16)
        grad_up_bias = jnp.sum(pre_grad.astype(F32), axis=0)
        grad_down_bias = jnp.sum(mlp_out_grad.astype(F32), axis=0)

        def group_scatter(left, right, order):
            first = order[0]
            place = group_bits.index(first)
            shaped = left.reshape((left.shape[0],) + (2,) * len(group_bits) + (-1,))
            rest = [which for which in group_bits if which != first]
            halves = []
            for which_side in (1 - side(first), side(first)):
                columns = pick(shaped, which_side, 1 + place).reshape(left.shape[0], -1)
                halves.append(contract(columns, right, 0, 0))
            current = halves[1] + swap(halves[0].astype(BF16), first).astype(F32)
            current = current.reshape((2 ** len(rest), -1, right.shape[1]))
            return scatter_bits(current, order[1:], rest)

        grad_down = group_scatter(hidden, mlp_out_grad_quad, list(reversed(order_down)))
        grad_up = group_scatter(normed_m, pre_grad, list(reversed(order_up)))
        grad_up = grad_up.reshape(2, 2, part, hidden_here)
        grad_up = join(
            pick(grad_up, near_here, 0).astype(BF16),
            swap(pick(grad_up, 1 - near_here, 0).astype(BF16), near),
            near,
            0,
        )
        grad_up = join(pick(grad_up, c_here, 1), swap(pick(grad_up, 1 - c_here, 1), core), core, 1)
        grad_up = grad_up.reshape(4, part, groups, unit).transpose(1, 2, 0, 3)
        grad_up = grad_up.reshape(part, n_dev * unit).astype(F32)

        grad_gain_m = jnp.sum(normed_grad * hat_m, axis=0)
        grad_shift_m = jnp.sum(normed_grad, axis=0)
        resid_grad = cot_rows + norm_backward(normed_grad, hat_m, inverse_m, gain_m)

        branch_grad = (validity * resid_grad).astype(BF16)
        grad_out_bias = jnp.sum(branch_grad.astype(F32), axis=0)
        mixed_grad = contract(branch_grad, weight_o, 1, 1).astype(BF16)
        columns = mixed_grad.reshape(width, n_z, 2 * span)
        rows_grad = jnp.zeros((n_z, width, 2 * span), BF16)
        rows_grad = lax.dynamic_update_slice_in_dim(
            rows_grad, pick(columns, z_here, 1)[None], z_here, 0
        )
        for d in range(1, n_z):
            piece = shift(pick(columns, (z_here + d) % n_z, 1), d)
            rows_grad = lax.dynamic_update_slice_in_dim(
                rows_grad, piece[None], (z_here - d) % n_z, 0
            )
        rows_grad = rows_grad.reshape(n_z, width, 2, span)
        rows_grad = join(
            pick(rows_grad, c_here, 2), swap(pick(rows_grad, 1 - c_here, 2), core), core, 1
        )
        rows_grad = rows_grad.reshape(n_z * 2 * width, span)

        grad_out = contract(mixed_low, branch_grad, 0, 0).reshape(n_dev, part, model)
        ranked_pairs = [which for which in all_bits if which != core]
        grad_out = grad_out.reshape(n_dev // 2, 2, part, model)
        grad_out = pick(grad_out, c_here, 1) + swap(
            pick(grad_out, 1 - c_here, 1).astype(BF16), core
        ).astype(F32)
        grad_out = jnp.concatenate(
            [
                scatter_bits(
                    grad_out[:, :, n * half_model : (n + 1) * half_model],
                    batch_order + far_bits + [near],
                    ranked_pairs,
                )
                for n, batch_order in enumerate((batch_bits, ranked_batch))
            ],
            axis=1,
        )

        qkv_grad = attention_backward(
            qkv, rows_grad, attended_t, log_total, places, low, high, n_seq, pre, tok, heads, HEAD_DIM
        )
        bias_sums = jnp.sum(qkv_grad.astype(F32), axis=0)

        def rows_for(r):
            first = ((z_here + r) % n_z) * 2 * width
            rows = lax.dynamic_slice_in_dim(qkv_grad, first, 2 * width, 0)
            share = contract(rows, weight_qkv, 1, 1).reshape(2, width, model)
            away = swap(pick(share, 1 - c_here, 0).astype(BF16), core)
            return pick(share, c_here, 0) + away.astype(F32)

        chunks = [rows_for(r) for r in range(n_z)]
        right = None
        left = None
        for k in range(1, n_z):
            going = jnp.where(z_here + n_z - k < n_z, chunks[n_z - k], 0.0)
            right = going if right is None else going + right.astype(F32)
            right = step_right(right.astype(BF16), 0, k)
            going = jnp.where(z_here - (n_z - k) >= 0, chunks[k], 0.0)
            left = going if left is None else going + left.astype(F32)
            left = step_left(left.astype(BF16), n_z - k, n_z)
        normed_back = chunks[0] + right.astype(F32) + left.astype(F32)

        grad_qkv = contract(normed, qkv_grad, 0, 0).reshape(n_batch, 2, -1, 3 * span)
        grad_qkv = jnp.concatenate(
            [
                scatter_bits(grad_qkv[:, n], batch_order, ranked_batch)
                for n, batch_order in enumerate((ranked_batch, batch_bits))
            ],
            axis=0,
        ).astype(BF16)
        grad_qkv = grad_qkv.reshape(n_z, 2, part, 3 * span)
        grad_qkv = join(
            pick(grad_qkv, c_here, 1), swap(pick(grad_qkv, 1 - c_here, 1), core), core, 1
        )
        shares = jnp.zeros((n_z, 2, part, 3 * span), BF16)
        shares = lax.dynamic_update_slice_in_dim(shares, pick(grad_qkv, z_here, 0)[None], z_here, 0)
        for d in range(1, n_z):
            piece = shift(pick(grad_qkv, (z_here + d) % n_z, 0), d)
            shares = lax.dynamic_update_slice_in_dim(shares, piece[None], (z_here - d) % n_z, 0)
        shares = shares.reshape(n_seq, part, 3, span).transpose(2, 1, 0, 3)
        shares = shares.reshape(3, part, model).astype(F32)

        hat_a, inverse_a = normalize(rows_in)
        grad_gain_a = jnp.sum(normed_back * hat_a, axis=0)
        grad_shift_a = jnp.sum(normed_back, axis=0)
        input_grad = resid_grad + norm_backward(normed_back, hat_a, inverse_a, gain_a)

        zero = jnp.zeros((model,), F32)
        grad_bias_q = lax.dynamic_update_slice_in_dim(zero, bias_sums[:span], s_here * span, 0)
        grad_bias_v = lax.dynamic_update_slice_in_dim(zero, bias_sums[2 * span :], s_here * span, 0)
        full_up_bias = lax.dynamic_update_slice_in_dim(
            jnp.zeros((groups, 4, unit), F32), grad_up_bias.reshape(groups, 1, unit), s_here % 4, 1
        ).reshape(n_dev, unit)
        sums = jnp.concatenate(
            [
                vector.reshape(n_dev, part)
                for vector in (
                    grad_gain_a, grad_shift_a, grad_bias_q, grad_bias_v, grad_out_bias,
                    grad_gain_m, grad_shift_m, grad_down_bias,
                )
            ]
            + [full_up_bias],
            axis=1,
        )
        current = sums.reshape((2,) * len(all_bits) + (sums.shape[1],))
        for which in all_bits:
            mine = side(which)
            current = pick(current, mine, 0) + swap(pick(current, 1 - mine, 0), which)
        small_grads = [current[n * part : (n + 1) * part] for n in range(8)]

        return (
            out_rows[pre:][None],
            out_rows[:real][None],
            input_grad[pre:][None],
            input_grad[:real][None],
            small_grads[0],
            small_grads[1],
            shares[0],
            shares[1],
            shares[2],
            small_grads[2],
            small_grads[3],
            grad_out,
            small_grads[4],
            small_grads[5],
            small_grads[6],
            grad_up,
            current[8 * part :],
            grad_down,
            small_grads[7],
        )

    return body


def solution(mesh):
    rows = P("batch", "seq", None)
    vector = P(("batch", "seq"))
    matrix = P(("batch", "seq"), None)
    return jax.shard_map(
        build(mesh.shape["batch"], mesh.shape["seq"]),
        mesh=mesh,
        in_specs=(
            rows, rows, P("batch", None), vector, vector, matrix, matrix, matrix, vector, vector,
            matrix, vector, vector, vector, matrix, vector, matrix, vector, rows, rows,
        ),
        out_specs=(
            rows, rows, rows, rows, vector, vector, matrix, matrix, matrix, vector, vector, matrix,
            vector, vector, vector, matrix, vector, matrix, vector,
        ),
        check_vma=False,
    )
```

```python
import functools
import math

import jax
import jax.numpy as jnp
from jax import lax
from jax.experimental import pallas as pl
from jax.experimental.pallas import tpu as pltpu
from jax.sharding import PartitionSpec as P

HEADS = 32
HEAD_DIM = 64
EPS = 1e-05
NEGATIVE = -1e30
FAR = 1 << 20
BLOCK = 256
BF16 = jnp.bfloat16
F32 = jnp.float32


def contract(left, right, left_dim, right_dim):
    return lax.dot_general(
        left, right, (((left_dim,), (right_dim,)), ((), ())), preferred_element_type=F32
    )


def slot_pieces(devices, pre, tok, device):
    if isinstance(device, int):
        return [(0, device * pre, pre), (pre, devices * pre + device * tok, tok)]
    return [
        (0, pl.multiple_of(device * pre, 16), pre),
        (pre, pl.multiple_of(devices * pre + device * tok, 16), tok),
    ]


def block_pieces(devices, pre, tok, place_ref, first, blocks):
    pieces = []
    for n in range(blocks):
        for i in range(2):
            core = place_ref[0] if i == 0 else 1 - place_ref[0]
            device = place_ref[first + n] * 2 + core
            for row, slot, count in slot_pieces(devices, pre, tok, device):
                pieces.append((n, i * (pre + tok) + row, slot, count))
    return pieces


def result_pieces(devices, pre, tok, place_ref):
    pieces = []
    for z in range(devices // 2):
        for i in range(2):
            core = place_ref[0] if i == 0 else 1 - place_ref[0]
            for row, slot, count in slot_pieces(devices, pre, tok, z * 2 + core):
                pieces.append(((z * 2 + i) * (pre + tok) + row, slot, count))
    return pieces


def block_mask(place, low, high):
    return (place <= high) & ((place >= low) | (place < 0))


def forward_kernel(devices, pre, tok, heads, head_dim, *refs):
    chips = devices // 2
    spot_ref, place_ref, low_ref, high_ref = refs[:4]
    chunks = refs[4 : 4 + chips]
    o_ref, ot_ref, lse_ref, q_s, k_s, v_s, vt_s, acc_s = refs[4 + chips :]
    width = heads * head_dim
    blocks = devices * (pre + tok) // BLOCK
    for n, row, slot, cnt in block_pieces(devices, pre, tok, spot_ref, 1, chips):
        q_s[pl.ds(slot, cnt), :] = chunks[n][row : row + cnt, 0:width]
        k_s[pl.ds(slot, cnt), :] = chunks[n][row : row + cnt, width : 2 * width]
        v_s[pl.ds(slot, cnt), :] = chunks[n][row : row + cnt, 2 * width : 3 * width]
    for b in range(blocks):
        rows = slice(b * BLOCK, (b + 1) * BLOCK)
        vt_s[:, rows] = v_s[rows, :].astype(F32).T.astype(BF16)
    lane = lax.broadcasted_iota(jnp.int32, (BLOCK, width), 1) // head_dim

    def query_block(i, carry):
        qs = pl.ds(pl.multiple_of(i * BLOCK, BLOCK), BLOCK)
        q = q_s[qs, :]
        qh = [jnp.where(lane == h, q, jnp.zeros_like(q)) for h in range(heads)]
        low = low_ref[:, qs]
        high = high_ref[:, qs]
        acc_s[...] = jnp.zeros_like(acc_s)
        span = [slice(h * head_dim, (h + 1) * head_dim) for h in range(heads)]

        def key_block(j, inner):
            tops, totals = inner
            ks = pl.ds(pl.multiple_of(j * BLOCK, BLOCK), BLOCK)
            k = k_s[ks, :]
            bias = jnp.where(block_mask(place_ref[ks, :], low, high), 0.0, NEGATIVE)
            s = [contract(k, qh[h], 1, 1) + bias for h in range(heads)]
            new = [
                jnp.maximum(tops[h], jnp.max(s[h], axis=0, keepdims=True)) for h in range(heads)
            ]
            p = [jnp.exp(s[h] - new[h]) for h in range(heads)]
            alpha = [jnp.exp(tops[h] - new[h]) for h in range(heads)]
            sums = [
                totals[h] * alpha[h] + jnp.sum(p[h], axis=0, keepdims=True) for h in range(heads)
            ]
            for h in range(heads):
                share = contract(vt_s[span[h], ks], p[h].astype(BF16), 1, 0)
                acc_s[span[h], :] = acc_s[span[h], :] * alpha[h] + share
            return tuple(new), tuple(sums)

        start = (
            tuple(jnp.full((1, BLOCK), NEGATIVE, F32) for h in range(heads)),
            tuple(jnp.zeros((1, BLOCK), F32) for h in range(heads)),
        )
        tops, totals = lax.fori_loop(0, i + 1, key_block, start)
        for h in range(heads):
            acc_s[span[h], :] = acc_s[span[h], :] / totals[h]
            lse_ref[h : h + 1, qs] = tops[h] + jnp.log(totals[h])
        result = acc_s[...]
        ot_ref[:, qs] = result
        q_s[qs, :] = result.T.astype(BF16)
        return carry

    lax.fori_loop(0, blocks, query_block, 0)
    for row, slot, cnt in result_pieces(devices, pre, tok, spot_ref):
        o_ref[row : row + cnt, :] = q_s[pl.ds(slot, cnt), :]


def attention_forward(chunks, spots, place, low, high, devices, pre, tok, heads, head_dim):
    width = heads * head_dim
    rows = devices * (pre + tok)
    vmem = pl.BlockSpec(memory_space=pltpu.VMEM)
    pairs = rows * rows // 2 * heads
    return pl.pallas_call(
        functools.partial(forward_kernel, devices, pre, tok, heads, head_dim),
        out_shape=(
            jax.ShapeDtypeStruct((rows, width), BF16),
            jax.ShapeDtypeStruct((width, rows), F32),
            jax.ShapeDtypeStruct((8, rows), F32),
        ),
        in_specs=[pl.BlockSpec(memory_space=pltpu.SMEM)] + [vmem] * (3 + len(chunks)),
        out_specs=(vmem,) * 3,
        scratch_shapes=[
            pltpu.VMEM((rows, width), BF16),
            pltpu.VMEM((rows, width), BF16),
            pltpu.VMEM((rows, width), BF16),
            pltpu.VMEM((width, rows), BF16),
            pltpu.VMEM((width, BLOCK), F32),
        ],
        compiler_params=pltpu.CompilerParams(vmem_limit_bytes=48 << 20),
        cost_estimate=pl.CostEstimate(
            flops=16 * pairs * head_dim, bytes_accessed=rows * width * 12, transcendentals=pairs
        ),
    )(spots, place, low, high, *chunks)


def backward_kernel(
    devices, pre, tok, heads, head_dim, first, last, carried, final, *refs
):
    chips = devices // 2
    spot_ref, ot_ref, lse_ref, place_ref, low_ref, high_ref = refs[:6]
    chunks = refs[6 : 6 + chips]
    grads = refs[6 + chips : 6 + 2 * chips]
    refs = refs[6 + 2 * chips :]
    if carried:
        dq_in, dk_in, dv_in = refs[:3]
        refs = refs[3:]
    if final:
        out_ref, near_ref = refs[:2]
        q_s, k_s, v_s, do_s, kt_s, dqt_s, dq_s, dk_s, dv_s = refs[2:]
    else:
        dq_s, dk_s, dv_s, q_s, k_s, v_s, do_s, kt_s, dqt_s = refs
    width = heads * head_dim
    scale = 1.0 / math.sqrt(head_dim)
    for n, row, slot, cnt in block_pieces(devices, pre, tok, spot_ref, 1, chips):
        q_s[pl.ds(slot, cnt), :] = chunks[n][row : row + cnt, 0:width]
        k_s[pl.ds(slot, cnt), :] = chunks[n][row : row + cnt, width : 2 * width]
        v_s[pl.ds(slot, cnt), :] = chunks[n][row : row + cnt, 2 * width : 3 * width]
    for n, row, slot, cnt in block_pieces(devices, pre, tok, spot_ref, 1 + chips, chips):
        do_s[pl.ds(slot, cnt), :] = grads[n][row : row + cnt, :]
    for b in range(last):
        rows = slice(b * BLOCK, (b + 1) * BLOCK)
        kt_s[:, rows] = k_s[rows, :].astype(F32).T.astype(BF16)
    if carried:
        dq_s[...] = dq_in[...]
        dk_s[...] = dk_in[...]
        dv_s[...] = dv_in[...]
    else:
        dk_s[...] = jnp.zeros_like(dk_s)
        dv_s[...] = jnp.zeros_like(dv_s)
    lane = lax.broadcasted_iota(jnp.int32, (BLOCK, width), 1) // head_dim

    def query_block(i, carry):
        qs = pl.ds(pl.multiple_of(i * BLOCK, BLOCK), BLOCK)
        q = q_s[qs, :]
        do = do_s[qs, :]
        qh = [jnp.where(lane == h, q, jnp.zeros_like(q)) for h in range(heads)]
        doh = [jnp.where(lane == h, do, jnp.zeros_like(do)) for h in range(heads)]
        low = low_ref[:, qs]
        high = high_ref[:, qs]
        prod = do.astype(F32).T * ot_ref[:, qs]
        delta = [
            jnp.sum(prod[h * head_dim : (h + 1) * head_dim, :], axis=0, keepdims=True)
            for h in range(heads)
        ]
        lse = [lse_ref[h : h + 1, qs] for h in range(heads)]
        dqt_s[...] = jnp.zeros_like(dqt_s)

        def key_block(j, inner):
            ks = pl.ds(pl.multiple_of(j * BLOCK, BLOCK), BLOCK)
            k = k_s[ks, :]
            v = v_s[ks, :]
            bias = jnp.where(block_mask(place_ref[ks, :], low, high), 0.0, NEGATIVE)
            s = [contract(k, qh[h], 1, 1) for h in range(heads)]
            dp = [contract(v, doh[h], 1, 1) for h in range(heads)]
            p = [jnp.exp(s[h] + bias - lse[h]) for h in range(heads)]
            ds = [(p[h] * (dp[h] - delta[h])).astype(BF16) for h in range(heads)]
            dv = sum(contract(p[h].astype(BF16), doh[h], 1, 0) for h in range(heads))
            dk = sum(contract(ds[h], qh[h], 1, 0) for h in range(heads))
            for h in range(heads):
                hs = slice(h * head_dim, (h + 1) * head_dim)
                dqt_s[hs, :] += contract(kt_s[hs, ks], ds[h], 1, 0)
            dk_s[ks, :] += dk
            dv_s[ks, :] += dv
            return inner

        lax.fori_loop(0, i + 1, key_block, 0)
        dq_s[qs, :] = (dqt_s[...] * scale).T.astype(BF16)
        return carry

    lax.fori_loop(first, last, query_block, 0)
    if final:
        for row, slot, cnt in result_pieces(devices, pre, tok, spot_ref):
            out_ref[row : row + cnt, 0:width] = dq_s[pl.ds(slot, cnt), :]
            out_ref[row : row + cnt, width : 2 * width] = dk_s[pl.ds(slot, cnt), :].astype(BF16)
            out_ref[row : row + cnt, 2 * width : 3 * width] = dv_s[pl.ds(slot, cnt), :].astype(BF16)
        both = 2 * (pre + tok)
        for n in range(chips):
            chip = pl.multiple_of(spot_ref[1 + n] * both, 16)
            near_ref[n * both : (n + 1) * both, :] = out_ref[pl.ds(chip, both), :]


def attention_backward(
    chunks, grads, spots, ot, lse, place, low, high, devices, pre, tok, heads, head_dim, first, last, carry, final
):
    width = heads * head_dim
    rows = devices * (pre + tok)
    vmem = pl.BlockSpec(memory_space=pltpu.VMEM)
    pairs = (last - first) * (last + first + 1) // 2 * BLOCK * BLOCK * heads
    low_rows = pltpu.VMEM((rows, width), BF16)
    sums = [((rows, width), BF16), ((rows, width), F32), ((rows, width), F32)]
    scratch = [
        low_rows,
        low_rows,
        low_rows,
        low_rows,
        pltpu.VMEM((width, rows), BF16),
        pltpu.VMEM((width, BLOCK), F32),
    ]
    if final:
        out_shape = (jax.ShapeDtypeStruct((rows, 3 * width), BF16),) * 2
        scratch += [pltpu.VMEM(shape, dtype) for shape, dtype in sums]
    else:
        out_shape = tuple(jax.ShapeDtypeStruct(shape, dtype) for shape, dtype in sums)
    return pl.pallas_call(
        functools.partial(
            backward_kernel, devices, pre, tok, heads, head_dim, first, last, bool(carry), final
        ),
        out_shape=out_shape,
        in_specs=[pl.BlockSpec(memory_space=pltpu.SMEM)]
        + [vmem] * (5 + len(chunks) + len(grads) + len(carry)),
        out_specs=(vmem,) * len(out_shape),
        scratch_shapes=scratch,
        compiler_params=pltpu.CompilerParams(vmem_limit_bytes=58 << 20),
        cost_estimate=pl.CostEstimate(
            flops=20 * pairs * head_dim, bytes_accessed=rows * width * 20, transcendentals=pairs
        ),
    )(spots, ot, lse, place, low, high, *chunks, *grads, *carry)


def matmul_kernel(flipped, left_ref, right_ref, out_ref):
    out_ref[...] = contract(left_ref[...], right_ref[...], 1, 1 if flipped else 0).astype(BF16)


def matmul_low(left, right, flipped):
    rows, depth = left.shape
    columns = right.shape[0] if flipped else right.shape[1]
    step = 512
    block = (step, depth) if flipped else (depth, step)
    return pl.pallas_call(
        functools.partial(matmul_kernel, flipped),
        grid=(columns // step,),
        out_shape=jax.ShapeDtypeStruct((rows, columns), BF16),
        in_specs=[
            pl.BlockSpec((rows, depth), lambda n: (0, 0)),
            pl.BlockSpec(block, (lambda n: (n, 0)) if flipped else (lambda n: (0, n))),
        ],
        out_specs=pl.BlockSpec((rows, step), lambda n: (0, n)),
        compiler_params=pltpu.CompilerParams(vmem_limit_bytes=48 << 20),
        cost_estimate=pl.CostEstimate(flops=1 << 20, bytes_accessed=1 << 16, transcendentals=0),
    )(left, right)


def transposed_kernel(left_ref, right_ref, out_ref):
    out_ref[...] = contract(left_ref[...], right_ref[...], 0, 0).astype(BF16)


def matmul_transposed(left, right):
    depth, rows = left.shape
    columns = right.shape[1]
    step = 512
    return pl.pallas_call(
        transposed_kernel,
        grid=(rows // step,),
        out_shape=jax.ShapeDtypeStruct((rows, columns), BF16),
        in_specs=[
            pl.BlockSpec((depth, step), lambda n: (0, n)),
            pl.BlockSpec((depth, columns), lambda n: (0, 0)),
        ],
        out_specs=pl.BlockSpec((step, columns), lambda n: (n, 0)),
        compiler_params=pltpu.CompilerParams(vmem_limit_bytes=56 << 20),
        cost_estimate=pl.CostEstimate(flops=1 << 20, bytes_accessed=1 << 16, transcendentals=0),
    )(left, right)


def rows_product_kernel(*refs):
    chunks, right_ref, out_ref = refs[:-2], refs[-2], refs[-1]
    rows = chunks[0].shape[0]
    total = contract(chunks[0][...], right_ref[0:rows, :], 0, 0)
    for n in range(1, len(chunks)):
        total += contract(chunks[n][...], right_ref[n * rows : (n + 1) * rows, :], 0, 0)
    out_ref[...] = total.astype(BF16)


def rows_product(chunks, right):
    rows, columns = chunks[0].shape
    step = 512
    return pl.pallas_call(
        rows_product_kernel,
        grid=(columns // step,),
        out_shape=jax.ShapeDtypeStruct((columns, right.shape[1]), BF16),
        in_specs=[pl.BlockSpec((rows, step), lambda n: (0, n))] * len(chunks)
        + [pl.BlockSpec(right.shape, lambda n: (0, 0))],
        out_specs=pl.BlockSpec((step, right.shape[1]), lambda n: (n, 0)),
        compiler_params=pltpu.CompilerParams(vmem_limit_bytes=56 << 20),
        cost_estimate=pl.CostEstimate(
            flops=right.shape[0] * columns * right.shape[1] // 2, bytes_accessed=1 << 16, transcendentals=0
        ),
    )(*chunks, right)


def slot_labels(lengths, devices, pre, tok, real):
    slot = jnp.arange(devices * pre, dtype=jnp.int32)
    inside = slot % pre
    place = (slot // pre) * real + inside - devices * real
    is_real = inside < real
    t = jnp.arange(devices * tok, dtype=jnp.int32)
    ends = jnp.cumsum(lengths)
    start = jnp.max(jnp.where(ends[None, :] <= t[:, None], ends[None, :], 0), axis=1)
    places = jnp.concatenate([jnp.where(is_real, place, FAR), t])
    high = jnp.concatenate([jnp.where(is_real, place, -1), t])
    low = jnp.concatenate([jnp.full((devices * pre,), FAR, jnp.int32), start])
    return places[:, None], low[None, :], high[None, :]


def normalize(values):
    center = values - jnp.mean(values, axis=-1, keepdims=True)
    spread = jnp.mean(center * center, axis=-1, keepdims=True)
    inverse = lax.rsqrt(spread + EPS)
    return center * inverse, inverse


def norm_backward(grad, hat, inverse, gain):
    e = grad * gain
    mean_e = jnp.mean(e, axis=-1, keepdims=True)
    mean_eh = jnp.mean(e * hat, axis=-1, keepdims=True)
    return inverse * (e - mean_e - hat * mean_eh)


def gelu_parts(values):
    cdf = 0.5 * (1.0 + lax.erf(values * (1.0 / math.sqrt(2.0))))
    return cdf


def pick(array, index, axis):
    return lax.dynamic_index_in_dim(array, index, axis, keepdims=False)


def build(n_batch, n_seq):
    n_z = n_seq // 2
    n_dev = n_batch * n_seq
    groups = n_dev // 4
    size_of = {"batch": n_batch, "seq": n_seq}

    def bits_of(n):
        bits = []
        bit = 1
        while bit < n:
            bits.append(bit)
            bit *= 2
        return bits

    core = ("seq", 1)
    near = ("seq", 2)
    up_batch = [("batch", bit) for bit in bits_of(n_batch)]
    down_batch = list(reversed(up_batch))
    far_bits = [("seq", bit) for bit in bits_of(n_seq) if bit >= 4]
    chip_bits = [near] + far_bits
    group_bits = down_batch + list(reversed(far_bits))
    all_bits = down_batch + [("seq", bit) for bit in reversed(bits_of(n_seq))]

    def swap_pairs(which):
        axis, bit = which
        return axis, [(i, i ^ bit) for i in range(size_of[axis])]

    def shift_pairs(distance):
        return "seq", [
            (z * 2 + c, ((z + distance) % n_z) * 2 + c) for z in range(n_z) for c in range(2)
        ]

    def right_pairs(first, last):
        return "seq", [(z * 2 + c, z * 2 + 2 + c) for z in range(first, last) for c in range(2)]

    def left_pairs(first, last):
        return "seq", [(z * 2 + c, z * 2 - 2 + c) for z in range(first, last) for c in range(2)]

    def side(which):
        axis, bit = which
        return (lax.axis_index(axis) // bit) % 2

    def permute(array, pairs):
        return lax.ppermute(array, pairs[0], pairs[1])

    class Clock:
        def __init__(self):
            self.gate = ()

        def hold(self, *arrays):
            if self.gate:
                arrays = lax.optimization_barrier(tuple(arrays) + tuple(self.gate))[: len(arrays)]
            return arrays[0] if len(arrays) == 1 else arrays

        def tick(self, *arrays):
            self.gate = arrays

    def join(mine, other, which, axis):
        first = side(which) == 0
        return jnp.where(first, jnp.stack([mine, other], axis), jnp.stack([other, mine], axis))

    def body(
        tokens, prefix, seg_lengths, attn_gain, attn_shift, query_weight, key_weight, value_weight,
        query_bias, value_bias, output_weight, output_bias, mlp_gain, mlp_shift, up_weight, up_bias,
        down_weight, down_bias, cot_tokens, cot_prefix,
    ):
        clock = Clock()

        def swap(array, which):
            return permute(array, swap_pairs(which))

        def gather_bits(array, order, ranked):
            taken = []
            current = array
            for which in order:
                other = swap(current, which)
                rank = ranked.index(which)
                place = sum(1 for t in taken if ranked.index(t) < rank)
                current = join(current, other, which, place)
                taken.append(which)
            return current.reshape((2 ** len(order),) + array.shape)

        def part_of(current, left, which, mine):
            return pick(current, side(which) if mine else 1 - side(which), left.index(which))

        def hop_scatter(current, left, which, last):
            other = swap(part_of(current, left, which, False).astype(BF16), which)
            total = part_of(current, left, which, True).astype(F32) + other.astype(F32)
            rest = [b for b in left if b != which]
            return (total if last else total.astype(BF16)), rest

        tok = tokens.shape[1]
        real = prefix.shape[1]
        pre = -(-real // 16) * 16
        width = pre + tok
        model = tokens.shape[2]
        heads = HEADS // n_seq
        span = heads * HEAD_DIM
        part = model // n_dev
        unit = up_bias.shape[0]
        hidden_here = groups * unit
        s_here = lax.axis_index("seq")
        z_here = s_here // 2
        c_here = s_here % 2
        near_here = side(near)
        lengths = seg_lengths[0]

        def rows_of(pre_part, tok_part):
            return jnp.concatenate([jnp.pad(pre_part, ((0, pre - real), (0, 0))), tok_part], axis=0)

        def device_rows(array, z, c):
            return lax.dynamic_slice_in_dim(array, (z * 2 + c) * width, width, 0)

        own = rows_of(prefix[0], tokens[0])
        row = jnp.arange(width, dtype=jnp.int32)
        position = row - pre + s_here * tok
        valid = jnp.where(row < pre, row < real, position < jnp.sum(lengths))
        validity = valid.astype(F32)[:, None]

        far_group = list(reversed(far_bits))
        n_far = groups // n_batch
        far_here = s_here // 4

        def afar(array, mask):
            return permute(array, ("seq", [(i, i ^ (mask * 4)) for i in range(n_seq)]))

        def batch_gather(array):
            return lax.all_gather(array, "batch", axis=0, tiled=True)

        def batch_sum(array):
            return lax.psum_scatter(array, "batch", scatter_dimension=0, tiled=True)

        def set_far(whole, blocks, index):
            blocks = blocks.reshape((n_batch, 1, -1) + blocks.shape[1:])
            return lax.dynamic_update_slice_in_dim(whole, blocks, index, 1)

        steps = [(permute(own, right_pairs(0, n_z - 1)), permute(own, left_pairs(1, n_z)))]
        small = jnp.concatenate(
            [attn_gain, attn_shift, query_bias, value_bias, output_bias, mlp_gain, mlp_shift, down_bias, up_bias]
        )
        small_bits = down_batch + [core]
        small = gather_bits(small, list(reversed(small_bits)), small_bits)
        down_gate, unused = lax.optimization_barrier((down_weight, small))
        down_own = batch_gather(down_gate)

        stacked = jnp.stack([query_weight, key_weight, value_weight], axis=1)
        stacked = stacked.reshape(part, 3, heads, n_z, 2, HEAD_DIM).transpose(3, 4, 0, 1, 2, 5)
        stacked = stacked.reshape(n_z, 2, part, 3 * span)
        mixed = join(pick(stacked, c_here, 1), swap(pick(stacked, 1 - c_here, 1), core), core, 1)
        mixed = mixed.reshape(n_z, 2 * part, 3 * span)
        flat = small.reshape(-1)
        small_rows = -(-flat.shape[0] // (3 * span * 16)) * 16
        flat = jnp.pad(flat, (0, small_rows * 3 * span - flat.shape[0]))
        flat = jnp.broadcast_to(flat.reshape(1, small_rows, 3 * span), (n_z, small_rows, 3 * span))
        mixed = jnp.concatenate([mixed, flat], axis=1)

        up_near = up_weight.reshape(part, groups, 2, 2, unit)
        up_near = join(pick(up_near, c_here, 3), swap(pick(up_near, 1 - c_here, 3), core), core, 0)

        clock.tick(*steps[0], up_near)

        def shift_out(choose):
            pieces = [choose((z_here + d) % n_z) for d in range(1, n_z)]
            pieces = clock.hold(*pieces) if len(pieces) > 1 else [clock.hold(*pieces)]
            got = [permute(piece, shift_pairs(d + 1)) for d, piece in enumerate(pieces)]
            return [(z_here, choose(z_here))] + [
                ((z_here - d - 1) % n_z, piece) for d, piece in enumerate(got)
            ]

        placed = shift_out(lambda z: pick(mixed, z, 0))
        ranked_o = far_group + [near]
        up_other = swap(clock.hold(pick(up_near, 1 - near_here, 3)), near)
        gathered_o = gather_bits(clock.hold(output_weight), far_bits, far_group)
        clock.tick(up_other, gathered_o, *[piece for unused, piece in placed[1:]])
        up_block = join(pick(up_near, near_here, 3), up_other, near, 0)
        up_block = up_block.reshape(4 * part, hidden_here)
        local = jnp.zeros((n_z, 2 * part, 3 * span), BF16)
        small_z = jnp.zeros((n_z, small_rows, 3 * span), BF16)
        for z, piece in placed:
            local = lax.dynamic_update_slice_in_dim(local, piece[None, : 2 * part], z, 0)
            small_z = lax.dynamic_update_slice_in_dim(small_z, piece[None, 2 * part :], z, 0)
        local, unused = lax.optimization_barrier((local, down_own))
        weight_qkv = batch_gather(local.reshape(n_z * 2 * part, 3 * span))
        small = small_z.reshape(n_z, -1)[:, : n_batch * 2 * (8 * part + unit)]
        small = small.reshape(n_z, n_batch, 2, 8 * part + unit).transpose(1, 0, 2, 3)
        small = small.reshape(n_dev, 8 * part + unit)
        vectors = [small[:, n * part : (n + 1) * part].reshape(model).astype(F32) for n in range(8)]
        gain_a, shift_a, bias_q, bias_v, bias_o, gain_m, shift_m, bias_down = vectors
        bias_up = pick(small[:, 8 * part :].reshape(groups, 4, unit), s_here % 4, 1)
        bias_up = bias_up.reshape(hidden_here).astype(F32)

        bias_qkv = jnp.concatenate(
            [
                pick(bias_q.reshape(heads, n_seq, HEAD_DIM), s_here, 1).reshape(span),
                jnp.zeros((span,), F32),
                pick(bias_v.reshape(heads, n_seq, HEAD_DIM), s_here, 1).reshape(span),
            ]
        )
        factor = jnp.concatenate(
            [jnp.full((span,), 1.0 / math.sqrt(HEAD_DIM), F32), jnp.ones((2 * span,), F32)]
        )

        def source(n):
            if n == 0:
                return z_here
            short = jnp.minimum(z_here, n_z - 1 - z_here)
            both = n <= 2 * short
            distance = jnp.where(both, (n + 1) // 2, n - short)
            left = jnp.where(both, n % 2 == 1, 2 * z_here >= n_z)
            return jnp.where(left, z_here - distance, z_here + distance)

        def rows_from(n):
            rows = own
            for d in range((n + 1) // 2, n + 1) if n else ():
                right, left = steps[d - 1]
                rows = jnp.where(source(n) == z_here - d, right, rows)
                rows = jnp.where(source(n) == z_here + d, left, rows)
            rows = jnp.concatenate([rows, swap(rows, core)], axis=0)
            hat, unused = normalize(rows.astype(F32))
            return (hat * gain_a + shift_a).astype(BF16)

        def qkv_of(rows):
            result = (contract(rows, weight_qkv, 1, 0) + bias_qkv).astype(BF16).astype(F32) * factor
            return result.astype(BF16)

        exact = part == HEAD_DIM and heads == n_batch
        normed = []
        for k in range(2, n_z):
            right, left = clock.hold(*steps[-1])
            steps.append(
                (permute(right, right_pairs(k - 1, n_z - 1)), permute(left, left_pairs(1, n_z - k + 1)))
            )
            normed.append(rows_from(k - 2))
            clock.tick(*steps[-1], normed[-1])
        up_gate, unused = lax.optimization_barrier((up_block, weight_qkv))
        up_own = batch_gather(up_gate)

        other = swap(clock.hold(gathered_o), near)
        gathered_o = join(gathered_o, other, near, 1)
        gathered_o, unused = lax.optimization_barrier((gathered_o, up_own))
        gathered_o = batch_gather(gathered_o.reshape(n_z * part, model))

        weight_o = gathered_o.reshape(n_batch, n_z, part, model)
        if exact:
            weight_o = weight_o.transpose(1, 0, 2, 3).reshape(n_z * span, model)
        else:
            weight_o = join(weight_o, swap(weight_o, core), core, 2)
            weight_o = weight_o.reshape(heads, n_z, 2, HEAD_DIM, model)
            weight_o = pick(weight_o, c_here, 2).transpose(1, 0, 2, 3).reshape(n_z * span, model)

        qkv = []
        for n in range(n_z):
            if n >= n_z - 2:
                normed.append(rows_from(n))
            qkv.append(qkv_of(normed[n]))
        shifted = [z_here] + [(z_here - d) % n_z for d in range(1, n_z)]
        spots = jnp.stack([c_here] + [source(n) for n in range(n_z)] + shifted).astype(jnp.int32)

        cot_rows = rows_of(cot_prefix[0], cot_tokens[0]).astype(F32)
        mlp_out_grad = (validity * cot_rows).astype(BF16)
        places, low, high = slot_labels(lengths, n_seq, pre, tok, real)
        clock.tick(other)
        *qkv, up_gate, grad_gate = clock.hold(*qkv, up_block, mlp_out_grad)
        up_far = [afar(up_gate, mask) for mask in range(1, n_far)]
        grad_far = swap(grad_gate, near)
        attended, attended_t, log_total = attention_forward(
            qkv, spots, places, low, high, n_seq, pre, tok, heads, HEAD_DIM
        )
        clock.tick(attended, grad_far, *up_far)
        up_blocks = [batch_gather(clock.hold(piece)) for piece in up_far]

        blocks = attended.reshape(n_z, 2 * width, span)
        placed = shift_out(lambda z: pick(blocks, z, 0))
        *normed, up_own, down_own, unused = lax.optimization_barrier(
            tuple(normed) + (up_own, down_own, attended)
        )
        weight_up = set_far(
            jnp.zeros((n_batch, n_far, 4 * part, hidden_here), BF16), up_own, far_here
        )
        weight_down = set_far(
            jnp.zeros((n_batch, n_far, unit, model), BF16), down_own, far_here
        )
        grad_rows = jnp.concatenate(
            [mlp_out_grad, swap(mlp_out_grad, core), grad_far, swap(grad_far, core)], axis=0
        )
        mixed_low = jnp.zeros((2 * width, n_z * span), BF16)
        for z, piece in placed:
            mixed_low = lax.dynamic_update_slice_in_dim(mixed_low, piece, z * span, 1)
        clock.tick(mixed_low, weight_up, weight_down)
        down_far = [afar(clock.hold(down_weight), mask) for mask in range(1, n_far)]
        mixed_held = clock.hold(mixed_low)
        branch_away = contract(mixed_held[width:], weight_o, 1, 0).astype(BF16)
        branch_away = swap(branch_away, core)
        branch = contract(mixed_held[:width], weight_o, 1, 0) + branch_away.astype(F32) + bias_o
        rows_in = own.astype(F32)
        resid = rows_in + validity * branch
        hat_m, inverse_m = normalize(resid)
        normed_own = (hat_m * gain_m + shift_m).astype(BF16)

        normed_near = swap(normed_own, core)
        normed_far = swap(normed_own, near)
        normed_rows = jnp.concatenate(
            [normed_own, normed_near, normed_far, swap(normed_far, core)], axis=0
        )
        *down_far, unused = lax.optimization_barrier(tuple(down_far) + (normed_own,))
        down_blocks = [batch_gather(piece) for piece in down_far]
        *up_blocks, unused = lax.optimization_barrier(tuple(up_blocks) + (normed_own,))
        for mask, piece in enumerate(up_blocks):
            weight_up = set_far(weight_up, piece, far_here ^ (mask + 1))
        weight_up = weight_up.reshape(model, hidden_here)

        before = contract(normed_rows, weight_up, 1, 0) + bias_up
        cdf = 0.5 * (1.0 + lax.erf(before * (1.0 / math.sqrt(2.0))))
        hidden = (before * cdf).astype(BF16)
        slope = cdf + before * jnp.exp(-0.5 * before * before) * (1.0 / math.sqrt(2.0 * math.pi))
        *down_blocks, unused = lax.optimization_barrier(tuple(down_blocks) + (hidden,))
        for mask, piece in enumerate(down_blocks):
            weight_down = set_far(weight_down, piece, far_here ^ (mask + 1))
        weight_down = weight_down.reshape(hidden_here, model)
        grad_down = contract(hidden, grad_rows, 0, 0).astype(BF16)
        grad_down, grad_held = lax.optimization_barrier((grad_down, grad_rows))
        grad_down = batch_sum(grad_down)
        hidden_grad = contract(grad_held, weight_down, 1, 1)
        pre_grad = (hidden_grad * slope).astype(BF16)

        share_f = contract(pre_grad[2 * width :], weight_up, 1, 1).astype(BF16)
        back = swap(share_f[width:], core)
        back = (share_f[:width].astype(F32) + back.astype(F32)).astype(BF16)
        pre_held, hidden_held, back_held = lax.optimization_barrier((pre_grad, hidden, back))
        back = swap(back_held, near)
        share_n = matmul_low(pre_held[: 2 * width], weight_up, True)
        out_share = matmul_low(hidden_held, weight_down, False)
        here = swap(share_n[width:], core)
        back, out_share, here = lax.optimization_barrier((back, out_share, here))
        normed_grad = share_n[:width].astype(F32) + here.astype(F32) + back.astype(F32)

        grad_up_bias = jnp.sum(pre_grad.astype(F32), axis=0)
        grad_down_bias = jnp.sum(mlp_out_grad.astype(F32), axis=0)
        grad_gain_m = jnp.sum(normed_grad * hat_m, axis=0)
        grad_shift_m = jnp.sum(normed_grad, axis=0)
        resid_grad = cot_rows + norm_backward(normed_grad, hat_m, inverse_m, gain_m)

        branch_grad = (validity * resid_grad).astype(BF16)
        grad_out_bias = jnp.sum(branch_grad.astype(F32), axis=0)
        branch_grad = jnp.concatenate([branch_grad, swap(branch_grad, core)], axis=0)
        mixed_grad = contract(branch_grad, weight_o, 1, 1).astype(BF16)
        clock.tick(mixed_grad)
        placed = shift_out(lambda z: lax.dynamic_slice_in_dim(mixed_grad, z * span, span, 1))
        grad_gate, branch_gate, mixed_gate, unused = lax.optimization_barrier(
            (pre_grad, branch_grad, mixed_low, mixed_grad)
        )
        grad_up = matmul_transposed(normed_rows, grad_gate)
        grad_out = matmul_transposed(mixed_gate, branch_gate)
        if exact:
            grad_out = grad_out.reshape(n_z, n_batch, part, model).transpose(1, 0, 2, 3)
        else:
            full = jnp.zeros((heads, n_z, 2, HEAD_DIM, model), BF16)
            grad_out = grad_out.reshape(n_z, heads, 1, HEAD_DIM, model).transpose(1, 0, 2, 3, 4)
            grad_out = lax.dynamic_update_slice_in_dim(full, grad_out, c_here, 2)
            grad_out = grad_out.reshape(n_batch, n_z, 2, part, model)
            grad_out = pick(grad_out, c_here, 2).astype(F32) + swap(
                pick(grad_out, 1 - c_here, 2), core
            ).astype(F32)
            grad_out = grad_out.astype(BF16)
        rows_grad = [piece for unused, piece in placed]
        grad_up, grad_out, *rows_grad = lax.optimization_barrier((grad_up, grad_out, *rows_grad))
        grad_up = batch_sum(grad_up)
        grad_out = batch_sum(grad_out.reshape(n_batch * n_z * part, model))

        out_back = swap(out_share[3 * width :], core)
        out_back = (out_share[2 * width : 3 * width].astype(F32) + out_back.astype(F32)).astype(BF16)
        out_here = swap(out_share[width : 2 * width], core)
        clock.tick(*rows_grad, grad_down, out_share)
        down_gate, out_away, *rows_grad = clock.hold(grad_down, out_back, *rows_grad)
        down_sum = down_gate.reshape((2,) * len(far_bits) + (unit, model))
        rest_down = list(far_group)
        for n, which in enumerate(far_bits):
            down_sum, rest_down = hop_scatter(
                down_sum, rest_down, which, n == len(far_bits) - 1
            )
        grad_down = down_sum
        out_back = swap(out_away, near)
        blocks = n_seq * width // BLOCK
        qkv_grad, relative = attention_backward(
            qkv, rows_grad, spots, attended_t, log_total, places, low, high,
            n_seq, pre, tok, heads, HEAD_DIM, 0, blocks, (), True,
        )
        qkv_grad, relative, grad_down, out_back = lax.optimization_barrier(
            (qkv_grad, relative, grad_down, out_back)
        )
        bias_sums = jnp.sum(qkv_grad.astype(F32), axis=0)
        clock.tick(qkv_grad, grad_down, out_back)

        chunks = [None] * n_z
        order = []
        for k in range(1, n_z):
            for r in (n_z - k, k):
                if r not in order:
                    order.append(r)
        for r in order + [0]:
            z = (z_here + r) % n_z
            away = contract(device_rows(qkv_grad, z, 1), weight_qkv, 1, 1).astype(BF16)
            away = swap(away, core)
            keep = contract(device_rows(qkv_grad, z, 0), weight_qkv, 1, 1)
            chunks[r] = keep + away.astype(F32)
        right = None
        left = None
        for k in range(1, n_z):
            going_r = jnp.where(z_here + n_z - k < n_z, chunks[n_z - k], 0.0)
            going_l = jnp.where(z_here - (n_z - k) >= 0, chunks[k], 0.0)
            if k > 1:
                going_r = going_r + right.astype(F32)
                going_l = going_l + left.astype(F32)
            going_r, going_l = clock.hold(going_r.astype(BF16), going_l.astype(BF16))
            right = permute(going_r, right_pairs(0, k))
            left = permute(going_l, left_pairs(n_z - k, n_z))
            started = [right, left]
            if k == 1:
                up_sum = clock.hold(grad_up).reshape((2,) * len(far_bits) + (4 * part, hidden_here))
                rest_up = list(far_group)
                for which in far_bits:
                    up_sum, rest_up = hop_scatter(up_sum, rest_up, which, False)
                relative, unused = lax.optimization_barrier((relative, going_r))
                grad_qkv = rows_product(normed, relative)
                grad_qkv, right, left, up_sum, grad_out = lax.optimization_barrier(
                    (grad_qkv, right, left, up_sum, grad_out)
                )
                grad_qkv = batch_sum(grad_qkv)
                started = [right, left, up_sum]
            if k == 2:
                grad_up = up_sum.reshape(2, 2, part, hidden_here)
                up_other = swap(clock.hold(pick(grad_up, 1 - near_here, 0)), near)
                grad_up = join(pick(grad_up, near_here, 0), up_other, near, 0)
                rest_o = list(ranked_o)
                grad_out = clock.hold(grad_out).reshape((2,) * len(ranked_o) + (part, model))
                grad_out, rest_o = hop_scatter(grad_out, rest_o, near, False)
                started += [up_other, grad_out]
            if k == n_z - 1:
                grad_qkv = grad_qkv.reshape(n_z, 2, part, 3 * span)
                grad_qkv = join(
                    pick(grad_qkv, c_here, 1), swap(pick(grad_qkv, 1 - c_here, 1), core), core, 1
                )
                placed = shift_out(lambda z: pick(grad_qkv, z, 0))
                grad_out = clock.hold(grad_out)
                for n, which in enumerate(far_bits):
                    grad_out, rest_o = hop_scatter(grad_out, rest_o, which, n == len(far_bits) - 1)
            clock.tick(*started)
        right, left, unused = lax.optimization_barrier(
            (right, left, tuple(piece for unused, piece in placed[1:]))
        )
        normed_back = chunks[0] + right.astype(F32) + left.astype(F32)

        grad_up = join(pick(grad_up, c_here, 1), swap(pick(grad_up, 1 - c_here, 1), core), core, 1)
        grad_up = grad_up.reshape(4, part, groups, unit).transpose(1, 2, 0, 3)
        grad_up = grad_up.reshape(part, n_dev * unit).astype(F32)

        final = out_share[:width].astype(F32) + out_here.astype(F32) + out_back.astype(F32)
        final = resid + validity * (final + bias_down)
        out_rows = final.astype(BF16)

        shares = jnp.zeros((n_z, 2, part, 3 * span), BF16)
        for z, piece in placed:
            shares = lax.dynamic_update_slice_in_dim(shares, piece[None], z, 0)
        shares = shares.reshape(n_seq, part, 3, heads, HEAD_DIM)
        shares = [
            shares[:, :, n].transpose(1, 2, 0, 3).reshape(part, model).astype(F32) for n in range(3)
        ]

        hat_a, inverse_a = normalize(rows_in)
        grad_gain_a = jnp.sum(normed_back * hat_a, axis=0)
        grad_shift_a = jnp.sum(normed_back, axis=0)
        input_grad = resid_grad + norm_backward(normed_back, hat_a, inverse_a, gain_a)

        zero = jnp.zeros((heads, n_seq, HEAD_DIM), F32)

        def spread(sums):
            sums = sums.reshape(heads, 1, HEAD_DIM)
            return lax.dynamic_update_slice_in_dim(zero, sums, s_here, 1).reshape(model)

        full_up_bias = lax.dynamic_update_slice_in_dim(
            jnp.zeros((groups, 4, unit), F32), grad_up_bias.reshape(groups, 1, unit), s_here % 4, 1
        ).reshape(n_dev, unit)
        sums = jnp.concatenate(
            [
                vector.reshape(n_dev, part)
                for vector in (
                    grad_gain_a, grad_shift_a, spread(bias_sums[:span]), spread(bias_sums[2 * span :]),
                    grad_out_bias, grad_gain_m, grad_shift_m, grad_down_bias,
                )
            ]
            + [full_up_bias],
            axis=1,
        )
        sums, unused = lax.optimization_barrier((sums, tuple(shares)))
        current = jnp.sum(lax.all_to_all(sums, ("batch", "seq"), 0, 0, tiled=True), axis=0)
        small_grads = [current[n * part : (n + 1) * part] for n in range(8)]

        return (
            out_rows[pre:][None],
            out_rows[:real][None],
            input_grad[pre:][None],
            input_grad[:real][None],
            small_grads[0],
            small_grads[1],
            shares[0],
            shares[1],
            shares[2],
            small_grads[2],
            small_grads[3],
            grad_out,
            small_grads[4],
            small_grads[5],
            small_grads[6],
            grad_up,
            current[8 * part :],
            grad_down,
            small_grads[7],
        )

    return body


def solution(mesh):
    rows = P("batch", "seq", None)
    vector = P(("batch", "seq"))
    matrix = P(("batch", "seq"), None)
    return jax.shard_map(
        build(mesh.shape["batch"], mesh.shape["seq"]),
        mesh=mesh,
        in_specs=(
            rows, rows, P("batch", None), vector, vector, matrix, matrix, matrix, vector, vector,
            matrix, vector, vector, vector, matrix, vector, matrix, vector, rows, rows,
        ),
        out_specs=(
            rows, rows, rows, rows, vector, vector, matrix, matrix, matrix, vector, vector, matrix,
            vector, vector, vector, matrix, vector, matrix, vector,
        ),
        check_vma=False,
    )
```

```python
import functools
import math

import jax
import jax.numpy as jnp
from jax import lax
from jax.experimental import pallas as pl
from jax.experimental.pallas import tpu as pltpu
from jax.sharding import PartitionSpec as P

HEADS = 32
HEAD_DIM = 64
EPS = 1e-05
NEGATIVE = -1e30
FAR = 1 << 20
BLOCK = 256
BF16 = jnp.bfloat16
F32 = jnp.float32


def contract(left, right, left_dim, right_dim):
    return lax.dot_general(
        left, right, (((left_dim,), (right_dim,)), ((), ())), preferred_element_type=F32
    )


def slot_pieces(devices, pre, tok, device):
    if isinstance(device, int):
        return [(0, device * pre, pre), (pre, devices * pre + device * tok, tok)]
    return [
        (0, pl.multiple_of(device * pre, 16), pre),
        (pre, pl.multiple_of(devices * pre + device * tok, 16), tok),
    ]


def block_pieces(devices, pre, tok, place_ref, first, blocks):
    pieces = []
    for n in range(blocks):
        for i in range(2):
            core = place_ref[0] if i == 0 else 1 - place_ref[0]
            device = place_ref[first + n] * 2 + core
            for row, slot, count in slot_pieces(devices, pre, tok, device):
                pieces.append((n, i * (pre + tok) + row, slot, count))
    return pieces


def result_pieces(devices, pre, tok, place_ref):
    pieces = []
    for z in range(devices // 2):
        for i in range(2):
            core = place_ref[0] if i == 0 else 1 - place_ref[0]
            for row, slot, count in slot_pieces(devices, pre, tok, z * 2 + core):
                pieces.append(((z * 2 + i) * (pre + tok) + row, slot, count))
    return pieces


def block_mask(place, low, high):
    return (place <= high) & ((place >= low) | (place < 0))


def forward_kernel(devices, pre, tok, heads, head_dim, *refs):
    chips = devices // 2
    spot_ref, place_ref, low_ref, high_ref = refs[:4]
    chunks = refs[4 : 4 + chips]
    o_ref, ot_ref, lse_ref, q_s, k_s, v_s, vt_s, acc_s = refs[4 + chips :]
    width = heads * head_dim
    blocks = devices * (pre + tok) // BLOCK
    for n, row, slot, cnt in block_pieces(devices, pre, tok, spot_ref, 1, chips):
        q_s[pl.ds(slot, cnt), :] = chunks[n][row : row + cnt, 0:width]
        k_s[pl.ds(slot, cnt), :] = chunks[n][row : row + cnt, width : 2 * width]
        v_s[pl.ds(slot, cnt), :] = chunks[n][row : row + cnt, 2 * width : 3 * width]
    for b in range(blocks):
        rows = slice(b * BLOCK, (b + 1) * BLOCK)
        vt_s[:, rows] = v_s[rows, :].astype(F32).T.astype(BF16)
    lane = lax.broadcasted_iota(jnp.int32, (BLOCK, width), 1) // head_dim

    def query_block(i, carry):
        qs = pl.ds(pl.multiple_of(i * BLOCK, BLOCK), BLOCK)
        q = q_s[qs, :]
        qh = [jnp.where(lane == h, q, jnp.zeros_like(q)) for h in range(heads)]
        low = low_ref[:, qs]
        high = high_ref[:, qs]
        acc_s[...] = jnp.zeros_like(acc_s)
        span = [slice(h * head_dim, (h + 1) * head_dim) for h in range(heads)]

        def key_block(j, inner):
            tops, totals = inner
            ks = pl.ds(pl.multiple_of(j * BLOCK, BLOCK), BLOCK)
            k = k_s[ks, :]
            bias = jnp.where(block_mask(place_ref[ks, :], low, high), 0.0, NEGATIVE)
            s = [contract(k, qh[h], 1, 1) + bias for h in range(heads)]
            new = [
                jnp.maximum(tops[h], jnp.max(s[h], axis=0, keepdims=True)) for h in range(heads)
            ]
            p = [jnp.exp(s[h] - new[h]) for h in range(heads)]
            alpha = [jnp.exp(tops[h] - new[h]) for h in range(heads)]
            sums = [
                totals[h] * alpha[h] + jnp.sum(p[h], axis=0, keepdims=True) for h in range(heads)
            ]
            for h in range(heads):
                share = contract(vt_s[span[h], ks], p[h].astype(BF16), 1, 0)
                acc_s[span[h], :] = acc_s[span[h], :] * alpha[h] + share
            return tuple(new), tuple(sums)

        start = (
            tuple(jnp.full((1, BLOCK), NEGATIVE, F32) for h in range(heads)),
            tuple(jnp.zeros((1, BLOCK), F32) for h in range(heads)),
        )
        tops, totals = lax.fori_loop(0, i + 1, key_block, start)
        for h in range(heads):
            acc_s[span[h], :] = acc_s[span[h], :] / totals[h]
            lse_ref[h : h + 1, qs] = tops[h] + jnp.log(totals[h])
        result = acc_s[...]
        ot_ref[:, qs] = result
        q_s[qs, :] = result.T.astype(BF16)
        return carry

    lax.fori_loop(0, blocks, query_block, 0)
    for row, slot, cnt in result_pieces(devices, pre, tok, spot_ref):
        o_ref[row : row + cnt, :] = q_s[pl.ds(slot, cnt), :]


def attention_forward(chunks, spots, place, low, high, devices, pre, tok, heads, head_dim):
    width = heads * head_dim
    rows = devices * (pre + tok)
    vmem = pl.BlockSpec(memory_space=pltpu.VMEM)
    pairs = rows * rows // 2 * heads
    return pl.pallas_call(
        functools.partial(forward_kernel, devices, pre, tok, heads, head_dim),
        out_shape=(
            jax.ShapeDtypeStruct((rows, width), BF16),
            jax.ShapeDtypeStruct((width, rows), F32),
            jax.ShapeDtypeStruct((8, rows), F32),
        ),
        in_specs=[pl.BlockSpec(memory_space=pltpu.SMEM)] + [vmem] * (3 + len(chunks)),
        out_specs=(vmem,) * 3,
        scratch_shapes=[
            pltpu.VMEM((rows, width), BF16),
            pltpu.VMEM((rows, width), BF16),
            pltpu.VMEM((rows, width), BF16),
            pltpu.VMEM((width, rows), BF16),
            pltpu.VMEM((width, BLOCK), F32),
        ],
        compiler_params=pltpu.CompilerParams(vmem_limit_bytes=48 << 20),
        cost_estimate=pl.CostEstimate(
            flops=16 * pairs * head_dim, bytes_accessed=rows * width * 12, transcendentals=pairs
        ),
    )(spots, place, low, high, *chunks)


def backward_kernel(
    devices, pre, tok, heads, head_dim, first, last, carried, final, *refs
):
    chips = devices // 2
    spot_ref, ot_ref, lse_ref, place_ref, low_ref, high_ref = refs[:6]
    chunks = refs[6 : 6 + chips]
    grads = refs[6 + chips : 6 + 2 * chips]
    refs = refs[6 + 2 * chips :]
    if carried:
        dq_in, dk_in, dv_in = refs[:3]
        refs = refs[3:]
    if final:
        out_ref, near_ref = refs[:2]
        q_s, k_s, v_s, do_s, kt_s, dqt_s, dq_s, dk_s, dv_s = refs[2:]
    else:
        dq_s, dk_s, dv_s, q_s, k_s, v_s, do_s, kt_s, dqt_s = refs
    width = heads * head_dim
    scale = 1.0 / math.sqrt(head_dim)
    for n, row, slot, cnt in block_pieces(devices, pre, tok, spot_ref, 1, chips):
        q_s[pl.ds(slot, cnt), :] = chunks[n][row : row + cnt, 0:width]
        k_s[pl.ds(slot, cnt), :] = chunks[n][row : row + cnt, width : 2 * width]
        v_s[pl.ds(slot, cnt), :] = chunks[n][row : row + cnt, 2 * width : 3 * width]
    for n, row, slot, cnt in block_pieces(devices, pre, tok, spot_ref, 1 + chips, chips):
        do_s[pl.ds(slot, cnt), :] = grads[n][row : row + cnt, :]
    for b in range(last):
        rows = slice(b * BLOCK, (b + 1) * BLOCK)
        kt_s[:, rows] = k_s[rows, :].astype(F32).T.astype(BF16)
    if carried:
        dq_s[...] = dq_in[...]
        dk_s[...] = dk_in[...]
        dv_s[...] = dv_in[...]
    else:
        dk_s[...] = jnp.zeros_like(dk_s)
        dv_s[...] = jnp.zeros_like(dv_s)
    lane = lax.broadcasted_iota(jnp.int32, (BLOCK, width), 1) // head_dim

    def query_block(i, carry):
        qs = pl.ds(pl.multiple_of(i * BLOCK, BLOCK), BLOCK)
        q = q_s[qs, :]
        do = do_s[qs, :]
        qh = [jnp.where(lane == h, q, jnp.zeros_like(q)) for h in range(heads)]
        doh = [jnp.where(lane == h, do, jnp.zeros_like(do)) for h in range(heads)]
        low = low_ref[:, qs]
        high = high_ref[:, qs]
        prod = do.astype(F32).T * ot_ref[:, qs]
        delta = [
            jnp.sum(prod[h * head_dim : (h + 1) * head_dim, :], axis=0, keepdims=True)
            for h in range(heads)
        ]
        lse = [lse_ref[h : h + 1, qs] for h in range(heads)]
        dqt_s[...] = jnp.zeros_like(dqt_s)

        def key_block(j, inner):
            ks = pl.ds(pl.multiple_of(j * BLOCK, BLOCK), BLOCK)
            k = k_s[ks, :]
            v = v_s[ks, :]
            bias = jnp.where(block_mask(place_ref[ks, :], low, high), 0.0, NEGATIVE)
            s = [contract(k, qh[h], 1, 1) for h in range(heads)]
            dp = [contract(v, doh[h], 1, 1) for h in range(heads)]
            p = [jnp.exp(s[h] + bias - lse[h]) for h in range(heads)]
            ds = [(p[h] * (dp[h] - delta[h])).astype(BF16) for h in range(heads)]
            dv = sum(contract(p[h].astype(BF16), doh[h], 1, 0) for h in range(heads))
            dk = sum(contract(ds[h], qh[h], 1, 0) for h in range(heads))
            for h in range(heads):
                hs = slice(h * head_dim, (h + 1) * head_dim)
                dqt_s[hs, :] += contract(kt_s[hs, ks], ds[h], 1, 0)
            dk_s[ks, :] += dk
            dv_s[ks, :] += dv
            return inner

        lax.fori_loop(0, i + 1, key_block, 0)
        dq_s[qs, :] = (dqt_s[...] * scale).T.astype(BF16)
        return carry

    lax.fori_loop(first, last, query_block, 0)
    if final:
        for row, slot, cnt in result_pieces(devices, pre, tok, spot_ref):
            out_ref[row : row + cnt, 0:width] = dq_s[pl.ds(slot, cnt), :]
            out_ref[row : row + cnt, width : 2 * width] = dk_s[pl.ds(slot, cnt), :].astype(BF16)
            out_ref[row : row + cnt, 2 * width : 3 * width] = dv_s[pl.ds(slot, cnt), :].astype(BF16)
        both = 2 * (pre + tok)
        for n in range(chips):
            chip = pl.multiple_of(spot_ref[1 + n] * both, 16)
            near_ref[n * both : (n + 1) * both, :] = out_ref[pl.ds(chip, both), :]


def attention_backward(
    chunks, grads, spots, ot, lse, place, low, high, devices, pre, tok, heads, head_dim, first, last, carry, final
):
    width = heads * head_dim
    rows = devices * (pre + tok)
    vmem = pl.BlockSpec(memory_space=pltpu.VMEM)
    pairs = (last - first) * (last + first + 1) // 2 * BLOCK * BLOCK * heads
    low_rows = pltpu.VMEM((rows, width), BF16)
    sums = [((rows, width), BF16), ((rows, width), F32), ((rows, width), F32)]
    scratch = [
        low_rows,
        low_rows,
        low_rows,
        low_rows,
        pltpu.VMEM((width, rows), BF16),
        pltpu.VMEM((width, BLOCK), F32),
    ]
    if final:
        out_shape = (jax.ShapeDtypeStruct((rows, 3 * width), BF16),) * 2
        scratch += [pltpu.VMEM(shape, dtype) for shape, dtype in sums]
    else:
        out_shape = tuple(jax.ShapeDtypeStruct(shape, dtype) for shape, dtype in sums)
    return pl.pallas_call(
        functools.partial(
            backward_kernel, devices, pre, tok, heads, head_dim, first, last, bool(carry), final
        ),
        out_shape=out_shape,
        in_specs=[pl.BlockSpec(memory_space=pltpu.SMEM)]
        + [vmem] * (5 + len(chunks) + len(grads) + len(carry)),
        out_specs=(vmem,) * len(out_shape),
        scratch_shapes=scratch,
        compiler_params=pltpu.CompilerParams(vmem_limit_bytes=58 << 20),
        cost_estimate=pl.CostEstimate(
            flops=20 * pairs * head_dim, bytes_accessed=rows * width * 20, transcendentals=pairs
        ),
    )(spots, ot, lse, place, low, high, *chunks, *grads, *carry)


def matmul_kernel(flipped, left_ref, right_ref, out_ref):
    out_ref[...] = contract(left_ref[...], right_ref[...], 1, 1 if flipped else 0).astype(BF16)


def matmul_low(left, right, flipped):
    rows, depth = left.shape
    columns = right.shape[0] if flipped else right.shape[1]
    step = 512
    block = (step, depth) if flipped else (depth, step)
    return pl.pallas_call(
        functools.partial(matmul_kernel, flipped),
        grid=(columns // step,),
        out_shape=jax.ShapeDtypeStruct((rows, columns), BF16),
        in_specs=[
            pl.BlockSpec((rows, depth), lambda n: (0, 0)),
            pl.BlockSpec(block, (lambda n: (n, 0)) if flipped else (lambda n: (0, n))),
        ],
        out_specs=pl.BlockSpec((rows, step), lambda n: (0, n)),
        compiler_params=pltpu.CompilerParams(vmem_limit_bytes=48 << 20),
        cost_estimate=pl.CostEstimate(flops=1 << 20, bytes_accessed=1 << 16, transcendentals=0),
    )(left, right)


def transposed_kernel(left_ref, right_ref, out_ref):
    out_ref[...] = contract(left_ref[...], right_ref[...], 0, 0).astype(BF16)


def matmul_transposed(left, right):
    depth, rows = left.shape
    columns = right.shape[1]
    step = 512
    return pl.pallas_call(
        transposed_kernel,
        grid=(rows // step,),
        out_shape=jax.ShapeDtypeStruct((rows, columns), BF16),
        in_specs=[
            pl.BlockSpec((depth, step), lambda n: (0, n)),
            pl.BlockSpec((depth, columns), lambda n: (0, 0)),
        ],
        out_specs=pl.BlockSpec((step, columns), lambda n: (n, 0)),
        compiler_params=pltpu.CompilerParams(vmem_limit_bytes=56 << 20),
        cost_estimate=pl.CostEstimate(flops=1 << 20, bytes_accessed=1 << 16, transcendentals=0),
    )(left, right)


def rows_product_kernel(*refs):
    chunks, right_ref, out_ref = refs[:-2], refs[-2], refs[-1]
    rows = chunks[0].shape[0]
    total = contract(chunks[0][...], right_ref[0:rows, :], 0, 0)
    for n in range(1, len(chunks)):
        total += contract(chunks[n][...], right_ref[n * rows : (n + 1) * rows, :], 0, 0)
    out_ref[...] = total.astype(BF16)


def rows_product(chunks, right):
    rows, columns = chunks[0].shape
    step = 512
    return pl.pallas_call(
        rows_product_kernel,
        grid=(columns // step,),
        out_shape=jax.ShapeDtypeStruct((columns, right.shape[1]), BF16),
        in_specs=[pl.BlockSpec((rows, step), lambda n: (0, n))] * len(chunks)
        + [pl.BlockSpec(right.shape, lambda n: (0, 0))],
        out_specs=pl.BlockSpec((step, right.shape[1]), lambda n: (n, 0)),
        compiler_params=pltpu.CompilerParams(vmem_limit_bytes=56 << 20),
        cost_estimate=pl.CostEstimate(
            flops=right.shape[0] * columns * right.shape[1] // 2, bytes_accessed=1 << 16, transcendentals=0
        ),
    )(*chunks, right)


def slot_labels(lengths, devices, pre, tok, real):
    slot = jnp.arange(devices * pre, dtype=jnp.int32)
    inside = slot % pre
    place = (slot // pre) * real + inside - devices * real
    is_real = inside < real
    t = jnp.arange(devices * tok, dtype=jnp.int32)
    ends = jnp.cumsum(lengths)
    start = jnp.max(jnp.where(ends[None, :] <= t[:, None], ends[None, :], 0), axis=1)
    places = jnp.concatenate([jnp.where(is_real, place, FAR), t])
    high = jnp.concatenate([jnp.where(is_real, place, -1), t])
    low = jnp.concatenate([jnp.full((devices * pre,), FAR, jnp.int32), start])
    return places[:, None], low[None, :], high[None, :]


def normalize(values):
    center = values - jnp.mean(values, axis=-1, keepdims=True)
    spread = jnp.mean(center * center, axis=-1, keepdims=True)
    inverse = lax.rsqrt(spread + EPS)
    return center * inverse, inverse


def norm_backward(grad, hat, inverse, gain):
    e = grad * gain
    mean_e = jnp.mean(e, axis=-1, keepdims=True)
    mean_eh = jnp.mean(e * hat, axis=-1, keepdims=True)
    return inverse * (e - mean_e - hat * mean_eh)


def gelu_parts(values):
    cdf = 0.5 * (1.0 + lax.erf(values * (1.0 / math.sqrt(2.0))))
    return cdf


def pick(array, index, axis):
    return lax.dynamic_index_in_dim(array, index, axis, keepdims=False)


def build(n_batch, n_seq):
    n_z = n_seq // 2
    n_dev = n_batch * n_seq
    groups = n_dev // 4
    size_of = {"batch": n_batch, "seq": n_seq}

    def bits_of(n):
        bits = []
        bit = 1
        while bit < n:
            bits.append(bit)
            bit *= 2
        return bits

    core = ("seq", 1)
    near = ("seq", 2)
    up_batch = [("batch", bit) for bit in bits_of(n_batch)]
    down_batch = list(reversed(up_batch))
    far_bits = [("seq", bit) for bit in bits_of(n_seq) if bit >= 4]
    chip_bits = [near] + far_bits
    group_bits = down_batch + list(reversed(far_bits))
    all_bits = down_batch + [("seq", bit) for bit in reversed(bits_of(n_seq))]

    def swap_pairs(which):
        axis, bit = which
        return axis, [(i, i ^ bit) for i in range(size_of[axis])]

    def shift_pairs(distance):
        return "seq", [
            (z * 2 + c, ((z + distance) % n_z) * 2 + c) for z in range(n_z) for c in range(2)
        ]

    def right_pairs(first, last):
        return "seq", [(z * 2 + c, z * 2 + 2 + c) for z in range(first, last) for c in range(2)]

    def left_pairs(first, last):
        return "seq", [(z * 2 + c, z * 2 - 2 + c) for z in range(first, last) for c in range(2)]

    def side(which):
        axis, bit = which
        return (lax.axis_index(axis) // bit) % 2

    def permute(array, pairs):
        return lax.ppermute(array, pairs[0], pairs[1])

    class Clock:
        def __init__(self):
            self.gate = ()

        def hold(self, *arrays):
            if self.gate:
                arrays = lax.optimization_barrier(tuple(arrays) + tuple(self.gate))[: len(arrays)]
            return arrays[0] if len(arrays) == 1 else arrays

        def tick(self, *arrays):
            self.gate = arrays

    def join(mine, other, which, axis):
        first = side(which) == 0
        return jnp.where(first, jnp.stack([mine, other], axis), jnp.stack([other, mine], axis))

    def body(
        tokens, prefix, seg_lengths, attn_gain, attn_shift, query_weight, key_weight, value_weight,
        query_bias, value_bias, output_weight, output_bias, mlp_gain, mlp_shift, up_weight, up_bias,
        down_weight, down_bias, cot_tokens, cot_prefix,
    ):
        clock = Clock()

        def swap(array, which):
            return permute(array, swap_pairs(which))

        def gather_bits(array, order, ranked):
            taken = []
            current = array
            for which in order:
                other = swap(current, which)
                rank = ranked.index(which)
                place = sum(1 for t in taken if ranked.index(t) < rank)
                current = join(current, other, which, place)
                taken.append(which)
            return current.reshape((2 ** len(order),) + array.shape)

        def part_of(current, left, which, mine):
            return pick(current, side(which) if mine else 1 - side(which), left.index(which))

        def hop_scatter(current, left, which, last):
            other = swap(part_of(current, left, which, False).astype(BF16), which)
            total = part_of(current, left, which, True).astype(F32) + other.astype(F32)
            rest = [b for b in left if b != which]
            return (total if last else total.astype(BF16)), rest

        tok = tokens.shape[1]
        real = prefix.shape[1]
        pre = -(-real // 16) * 16
        width = pre + tok
        model = tokens.shape[2]
        heads = HEADS // n_seq
        span = heads * HEAD_DIM
        part = model // n_dev
        unit = up_bias.shape[0]
        hidden_here = groups * unit
        s_here = lax.axis_index("seq")
        z_here = s_here // 2
        c_here = s_here % 2
        near_here = side(near)
        lengths = seg_lengths[0]

        def rows_of(pre_part, tok_part):
            return jnp.concatenate([jnp.pad(pre_part, ((0, pre - real), (0, 0))), tok_part], axis=0)

        def device_rows(array, z, c):
            return lax.dynamic_slice_in_dim(array, (z * 2 + c) * width, width, 0)

        own = rows_of(prefix[0], tokens[0])
        row = jnp.arange(width, dtype=jnp.int32)
        position = row - pre + s_here * tok
        valid = jnp.where(row < pre, row < real, position < jnp.sum(lengths))
        validity = valid.astype(F32)[:, None]

        far_group = list(reversed(far_bits))
        n_far = groups // n_batch
        far_here = s_here // 4

        def afar(array, mask):
            return permute(array, ("seq", [(i, i ^ (mask * 4)) for i in range(n_seq)]))

        def batch_gather(array):
            return lax.all_gather(array, "batch", axis=0, tiled=True)

        def batch_sum(array):
            return lax.psum_scatter(array, "batch", scatter_dimension=0, tiled=True)

        def set_far(whole, blocks, index):
            blocks = blocks.reshape((n_batch, 1, -1) + blocks.shape[1:])
            return lax.dynamic_update_slice_in_dim(whole, blocks, index, 1)

        steps = [(permute(own, right_pairs(0, n_z - 1)), permute(own, left_pairs(1, n_z)))]
        small = jnp.concatenate(
            [attn_gain, attn_shift, query_bias, value_bias, output_bias, mlp_gain, mlp_shift, down_bias, up_bias]
        )
        small_bits = down_batch + [core]
        small = gather_bits(small, list(reversed(small_bits)), small_bits)
        down_gate, unused = lax.optimization_barrier((down_weight, small))
        down_own = batch_gather(down_gate)

        stacked = jnp.stack([query_weight, key_weight, value_weight], axis=1)
        stacked = stacked.reshape(part, 3, heads, n_z, 2, HEAD_DIM).transpose(3, 4, 0, 1, 2, 5)
        stacked = stacked.reshape(n_z, 2, part, 3 * span)
        mixed = join(pick(stacked, c_here, 1), swap(pick(stacked, 1 - c_here, 1), core), core, 1)
        mixed = mixed.reshape(n_z, 2 * part, 3 * span)
        flat = small.reshape(-1)
        small_rows = -(-flat.shape[0] // (3 * span * 16)) * 16
        flat = jnp.pad(flat, (0, small_rows * 3 * span - flat.shape[0]))
        flat = jnp.broadcast_to(flat.reshape(1, small_rows, 3 * span), (n_z, small_rows, 3 * span))
        mixed = jnp.concatenate([mixed, flat], axis=1)

        up_near = up_weight.reshape(part, groups, 2, 2, unit)
        up_near = join(pick(up_near, c_here, 3), swap(pick(up_near, 1 - c_here, 3), core), core, 0)

        clock.tick(*steps[0], up_near)

        def shift_out(choose):
            pieces = [choose((z_here + d) % n_z) for d in range(1, n_z)]
            pieces = clock.hold(*pieces) if len(pieces) > 1 else [clock.hold(*pieces)]
            got = [permute(piece, shift_pairs(d + 1)) for d, piece in enumerate(pieces)]
            return [(z_here, choose(z_here))] + [
                ((z_here - d - 1) % n_z, piece) for d, piece in enumerate(got)
            ]

        placed = shift_out(lambda z: pick(mixed, z, 0))
        ranked_o = far_group + [near]
        up_other = swap(clock.hold(pick(up_near, 1 - near_here, 3)), near)
        gathered_o = gather_bits(clock.hold(output_weight), far_bits, far_group)
        clock.tick(up_other, gathered_o, *[piece for unused, piece in placed[1:]])
        up_block = join(pick(up_near, near_here, 3), up_other, near, 0)
        up_block = up_block.reshape(4 * part, hidden_here)
        local = jnp.zeros((n_z, 2 * part, 3 * span), BF16)
        small_z = jnp.zeros((n_z, small_rows, 3 * span), BF16)
        for z, piece in placed:
            local = lax.dynamic_update_slice_in_dim(local, piece[None, : 2 * part], z, 0)
            small_z = lax.dynamic_update_slice_in_dim(small_z, piece[None, 2 * part :], z, 0)
        local, unused = lax.optimization_barrier((local, down_own))
        weight_qkv = batch_gather(local.reshape(n_z * 2 * part, 3 * span))
        small = small_z.reshape(n_z, -1)[:, : n_batch * 2 * (8 * part + unit)]
        small = small.reshape(n_z, n_batch, 2, 8 * part + unit).transpose(1, 0, 2, 3)
        small = small.reshape(n_dev, 8 * part + unit)
        vectors = [small[:, n * part : (n + 1) * part].reshape(model).astype(F32) for n in range(8)]
        gain_a, shift_a, bias_q, bias_v, bias_o, gain_m, shift_m, bias_down = vectors
        bias_up = pick(small[:, 8 * part :].reshape(groups, 4, unit), s_here % 4, 1)
        bias_up = bias_up.reshape(hidden_here).astype(F32)

        bias_qkv = jnp.concatenate(
            [
                pick(bias_q.reshape(heads, n_seq, HEAD_DIM), s_here, 1).reshape(span),
                jnp.zeros((span,), F32),
                pick(bias_v.reshape(heads, n_seq, HEAD_DIM), s_here, 1).reshape(span),
            ]
        )
        factor = jnp.concatenate(
            [jnp.full((span,), 1.0 / math.sqrt(HEAD_DIM), F32), jnp.ones((2 * span,), F32)]
        )

        def source(n):
            if n == 0:
                return z_here
            short = jnp.minimum(z_here, n_z - 1 - z_here)
            both = n <= 2 * short
            distance = jnp.where(both, (n + 1) // 2, n - short)
            left = jnp.where(both, n % 2 == 1, 2 * z_here >= n_z)
            return jnp.where(left, z_here - distance, z_here + distance)

        def rows_from(n):
            rows = own
            for d in range((n + 1) // 2, n + 1) if n else ():
                right, left = steps[d - 1]
                rows = jnp.where(source(n) == z_here - d, right, rows)
                rows = jnp.where(source(n) == z_here + d, left, rows)
            rows = jnp.concatenate([rows, swap(rows, core)], axis=0)
            hat, unused = normalize(rows.astype(F32))
            return (hat * gain_a + shift_a).astype(BF16)

        def qkv_of(rows):
            result = (contract(rows, weight_qkv, 1, 0) + bias_qkv).astype(BF16).astype(F32) * factor
            return result.astype(BF16)

        exact = part == HEAD_DIM and heads == n_batch
        normed = []
        for k in range(2, n_z):
            right, left = clock.hold(*steps[-1])
            steps.append(
                (permute(right, right_pairs(k - 1, n_z - 1)), permute(left, left_pairs(1, n_z - k + 1)))
            )
            normed.append(rows_from(k - 2))
            clock.tick(*steps[-1], normed[-1])
        up_gate, unused = lax.optimization_barrier((up_block, weight_qkv))
        up_own = batch_gather(up_gate)

        other = swap(clock.hold(gathered_o), near)
        gathered_o = join(gathered_o, other, near, 1)
        qkv = []
        for n in range(n_z):
            if n >= n_z - 2:
                normed.append(rows_from(n))
            qkv.append(qkv_of(normed[n]))
        gathered_o, unused = lax.optimization_barrier((gathered_o, (up_own, *qkv)))
        gathered_o = batch_gather(gathered_o.reshape(n_z * part, model))

        weight_o = gathered_o.reshape(n_batch, n_z, part, model)
        if exact:
            weight_o = weight_o.transpose(1, 0, 2, 3).reshape(n_z * span, model)
        else:
            weight_o = join(weight_o, swap(weight_o, core), core, 2)
            weight_o = weight_o.reshape(heads, n_z, 2, HEAD_DIM, model)
            weight_o = pick(weight_o, c_here, 2).transpose(1, 0, 2, 3).reshape(n_z * span, model)

        shifted = [z_here] + [(z_here - d) % n_z for d in range(1, n_z)]
        spots = jnp.stack([c_here] + [source(n) for n in range(n_z)] + shifted).astype(jnp.int32)

        cot_rows = rows_of(cot_prefix[0], cot_tokens[0]).astype(F32)
        mlp_out_grad = (validity * cot_rows).astype(BF16)
        places, low, high = slot_labels(lengths, n_seq, pre, tok, real)
        clock.tick(other)
        *qkv, up_gate, grad_gate = clock.hold(*qkv, up_block, mlp_out_grad)
        up_far = [afar(up_gate, mask) for mask in range(1, n_far)]
        grad_far = swap(grad_gate, near)
        attended, attended_t, log_total = attention_forward(
            qkv, spots, places, low, high, n_seq, pre, tok, heads, HEAD_DIM
        )
        clock.tick(attended, grad_far, *up_far)
        up_blocks = [batch_gather(clock.hold(piece)) for piece in up_far]

        blocks = attended.reshape(n_z, 2 * width, span)
        placed = shift_out(lambda z: pick(blocks, z, 0))
        *normed, up_own, down_own, unused = lax.optimization_barrier(
            tuple(normed) + (up_own, down_own, attended)
        )
        weight_up = set_far(
            jnp.zeros((n_batch, n_far, 4 * part, hidden_here), BF16), up_own, far_here
        )
        weight_down = set_far(
            jnp.zeros((n_batch, n_far, unit, model), BF16), down_own, far_here
        )
        grad_rows = jnp.concatenate(
            [mlp_out_grad, swap(mlp_out_grad, core), grad_far, swap(grad_far, core)], axis=0
        )
        spread_o = [piece for unused, piece in placed[1:]]
        *spread_o, weight_up, weight_down, weight_o = lax.optimization_barrier(
            (*spread_o, weight_up, weight_down, weight_o)
        )
        placed = [placed[0]] + [(z, piece) for (z, unused), piece in zip(placed[1:], spread_o)]
        mixed_low = jnp.zeros((2 * width, n_z * span), BF16)
        for z, piece in placed:
            mixed_low = lax.dynamic_update_slice_in_dim(mixed_low, piece, z * span, 1)
        clock.tick(mixed_low, weight_up, weight_down)
        down_far = [afar(clock.hold(down_weight), mask) for mask in range(1, n_far)]
        mixed_held = clock.hold(mixed_low)
        branch_away = contract(mixed_held[width:], weight_o, 1, 0).astype(BF16)
        branch_away = swap(branch_away, core)
        branch = contract(mixed_held[:width], weight_o, 1, 0) + branch_away.astype(F32) + bias_o
        rows_in = own.astype(F32)
        resid = rows_in + validity * branch
        hat_m, inverse_m = normalize(resid)
        normed_own = (hat_m * gain_m + shift_m).astype(BF16)

        normed_near = swap(normed_own, core)
        normed_far = swap(normed_own, near)
        *down_far, unused = lax.optimization_barrier(tuple(down_far) + (normed_own,))
        down_blocks = [batch_gather(piece) for piece in down_far]
        *up_blocks, unused = lax.optimization_barrier(tuple(up_blocks) + (normed_own,))
        for mask, piece in enumerate(up_blocks):
            weight_up = set_far(weight_up, piece, far_here ^ (mask + 1))
        weight_up = weight_up.reshape(model, hidden_here)
        normed_far, weight_up = lax.optimization_barrier((normed_far, weight_up))
        normed_parts = [normed_own, normed_near, normed_far, swap(normed_far, core)]
        normed_rows = jnp.concatenate(normed_parts, axis=0)

        before = contract(normed_rows, weight_up, 1, 0) + bias_up
        cdf = 0.5 * (1.0 + lax.erf(before * (1.0 / math.sqrt(2.0))))
        hidden = (before * cdf).astype(BF16)
        slope = cdf + before * jnp.exp(-0.5 * before * before) * (1.0 / math.sqrt(2.0 * math.pi))
        *down_blocks, unused = lax.optimization_barrier(tuple(down_blocks) + (hidden,))
        for mask, piece in enumerate(down_blocks):
            weight_down = set_far(weight_down, piece, far_here ^ (mask + 1))
        weight_down = weight_down.reshape(hidden_here, model)
        grad_down = contract(hidden, grad_rows, 0, 0).astype(BF16)
        grad_down, grad_held = lax.optimization_barrier((grad_down, grad_rows))
        grad_down = batch_sum(grad_down)
        hidden_grad = contract(grad_held, weight_down, 1, 1)
        pre_grad = (hidden_grad * slope).astype(BF16)

        share_f = contract(pre_grad[2 * width :], weight_up, 1, 1).astype(BF16)
        back = swap(share_f[width:], core)
        back = (share_f[:width].astype(F32) + back.astype(F32)).astype(BF16)
        pre_held, hidden_held, back_held = lax.optimization_barrier((pre_grad, hidden, back))
        back = swap(back_held, near)
        share_n = matmul_low(pre_held[: 2 * width], weight_up, True)
        out_share = matmul_low(hidden_held, weight_down, False)
        back, out_share, share_n = lax.optimization_barrier((back, out_share, share_n))
        here = swap(share_n[width:], core)
        normed_grad = share_n[:width].astype(F32) + here.astype(F32) + back.astype(F32)

        grad_up_bias = jnp.sum(pre_grad.astype(F32), axis=0)
        grad_down_bias = jnp.sum(mlp_out_grad.astype(F32), axis=0)
        grad_gain_m = jnp.sum(normed_grad * hat_m, axis=0)
        grad_shift_m = jnp.sum(normed_grad, axis=0)
        resid_grad = cot_rows + norm_backward(normed_grad, hat_m, inverse_m, gain_m)

        branch_grad = (validity * resid_grad).astype(BF16)
        grad_out_bias = jnp.sum(branch_grad.astype(F32), axis=0)
        branch_grad = jnp.concatenate([branch_grad, swap(branch_grad, core)], axis=0)
        mixed_grad = contract(branch_grad, weight_o, 1, 1).astype(BF16)
        clock.tick(mixed_grad)
        placed = shift_out(lambda z: lax.dynamic_slice_in_dim(mixed_grad, z * span, span, 1))
        grad_gate, branch_gate, mixed_gate, unused = lax.optimization_barrier(
            (pre_grad, branch_grad, mixed_low, mixed_grad)
        )
        grad_up = rows_product(normed_parts, grad_gate)
        grad_out = matmul_transposed(mixed_gate, branch_gate)
        if exact:
            grad_out = grad_out.reshape(n_z, n_batch, part, model).transpose(1, 0, 2, 3)
        else:
            full = jnp.zeros((heads, n_z, 2, HEAD_DIM, model), BF16)
            grad_out = grad_out.reshape(n_z, heads, 1, HEAD_DIM, model).transpose(1, 0, 2, 3, 4)
            grad_out = lax.dynamic_update_slice_in_dim(full, grad_out, c_here, 2)
            grad_out = grad_out.reshape(n_batch, n_z, 2, part, model)
            grad_out = pick(grad_out, c_here, 2).astype(F32) + swap(
                pick(grad_out, 1 - c_here, 2), core
            ).astype(F32)
            grad_out = grad_out.astype(BF16)
        rows_grad = [piece for unused, piece in placed]
        out_back = swap(out_share[3 * width :], core)
        out_back = (out_share[2 * width : 3 * width].astype(F32) + out_back.astype(F32)).astype(BF16)
        out_here = swap(out_share[width : 2 * width], core)
        grad_up, grad_out, out_back, *rows_grad = lax.optimization_barrier(
            (grad_up, grad_out, out_back, *rows_grad)
        )
        grad_up = batch_sum(grad_up)
        grad_out = batch_sum(grad_out.reshape(n_batch * n_z * part, model))

        clock.tick(*rows_grad, grad_down, out_share)
        down_gate, out_away, *rows_grad = clock.hold(grad_down, out_back, *rows_grad)
        down_sum = down_gate.reshape((2,) * len(far_bits) + (unit, model))
        rest_down = list(far_group)
        for n, which in enumerate(far_bits):
            down_sum, rest_down = hop_scatter(
                down_sum, rest_down, which, n == len(far_bits) - 1
            )
        grad_down = down_sum
        out_back = swap(out_away, near)
        blocks = n_seq * width // BLOCK
        qkv_grad, relative = attention_backward(
            qkv, rows_grad, spots, attended_t, log_total, places, low, high,
            n_seq, pre, tok, heads, HEAD_DIM, 0, blocks, (), True,
        )
        qkv_grad, relative, grad_down, out_back = lax.optimization_barrier(
            (qkv_grad, relative, grad_down, out_back)
        )
        bias_sums = jnp.sum(qkv_grad.astype(F32), axis=0)
        clock.tick(qkv_grad, grad_down, out_back)

        chunks = [None] * n_z
        aways = []
        order = []
        for k in range(1, n_z):
            for r in (n_z - k, k):
                if r not in order:
                    order.append(r)
        for r in order + [0]:
            z = (z_here + r) % n_z
            away = contract(device_rows(qkv_grad, z, 1), weight_qkv, 1, 1).astype(BF16)
            away = swap(away, core)
            aways.append(away)
            keep = contract(device_rows(qkv_grad, z, 0), weight_qkv, 1, 1)
            chunks[r] = keep + away.astype(F32)
        right = None
        left = None
        for k in range(1, n_z):
            going_r = jnp.where(z_here + n_z - k < n_z, chunks[n_z - k], 0.0)
            going_l = jnp.where(z_here - (n_z - k) >= 0, chunks[k], 0.0)
            if k > 1:
                going_r = going_r + right.astype(F32)
                going_l = going_l + left.astype(F32)
            going_r, going_l = clock.hold(going_r.astype(BF16), going_l.astype(BF16))
            right = permute(going_r, right_pairs(0, k))
            left = permute(going_l, left_pairs(n_z - k, n_z))
            started = [right, left]
            if k == 1:
                up_sum = clock.hold(grad_up).reshape((2,) * len(far_bits) + (4 * part, hidden_here))
                rest_up = list(far_group)
                for which in far_bits:
                    up_sum, rest_up = hop_scatter(up_sum, rest_up, which, False)
                relative, unused = lax.optimization_barrier((relative, going_r))
                grad_qkv = rows_product(normed, relative)
                grad_qkv, right, left, up_sum, grad_out, unused = lax.optimization_barrier(
                    (grad_qkv, right, left, up_sum, grad_out, tuple(aways[2:]))
                )
                grad_qkv = batch_sum(grad_qkv)
                started = [right, left, up_sum]
            if k == 2:
                grad_up = up_sum.reshape(2, 2, part, hidden_here)
                up_other = swap(clock.hold(pick(grad_up, 1 - near_here, 0)), near)
                grad_up = join(pick(grad_up, near_here, 0), up_other, near, 0)
                rest_o = list(ranked_o)
                grad_out = clock.hold(grad_out).reshape((2,) * len(ranked_o) + (part, model))
                grad_out, rest_o = hop_scatter(grad_out, rest_o, near, False)
                started += [up_other, grad_out]
            if k == n_z - 1:
                grad_qkv = grad_qkv.reshape(n_z, 2, part, 3 * span)
                grad_qkv = join(
                    pick(grad_qkv, c_here, 1), swap(pick(grad_qkv, 1 - c_here, 1), core), core, 1
                )
                placed = shift_out(lambda z: pick(grad_qkv, z, 0))
                grad_out = clock.hold(grad_out)
                for n, which in enumerate(far_bits):
                    grad_out, rest_o = hop_scatter(grad_out, rest_o, which, n == len(far_bits) - 1)
            clock.tick(*started)
        right, left, unused = lax.optimization_barrier(
            (right, left, tuple(piece for unused, piece in placed[1:]))
        )
        normed_back = chunks[0] + right.astype(F32) + left.astype(F32)

        grad_up = join(pick(grad_up, c_here, 1), swap(pick(grad_up, 1 - c_here, 1), core), core, 1)
        grad_up = grad_up.reshape(4, part, groups, unit).transpose(1, 2, 0, 3)
        grad_up = grad_up.reshape(part, n_dev * unit).astype(F32)

        final = out_share[:width].astype(F32) + out_here.astype(F32) + out_back.astype(F32)
        final = resid + validity * (final + bias_down)
        out_rows = final.astype(BF16)

        shares = jnp.zeros((n_z, 2, part, 3 * span), BF16)
        for z, piece in placed:
            shares = lax.dynamic_update_slice_in_dim(shares, piece[None], z, 0)
        shares = shares.reshape(n_seq, part, 3, heads, HEAD_DIM)
        shares = [
            shares[:, :, n].transpose(1, 2, 0, 3).reshape(part, model).astype(F32) for n in range(3)
        ]

        hat_a, inverse_a = normalize(rows_in)
        grad_gain_a = jnp.sum(normed_back * hat_a, axis=0)
        grad_shift_a = jnp.sum(normed_back, axis=0)
        input_grad = resid_grad + norm_backward(normed_back, hat_a, inverse_a, gain_a)

        zero = jnp.zeros((heads, n_seq, HEAD_DIM), F32)

        def spread(sums):
            sums = sums.reshape(heads, 1, HEAD_DIM)
            return lax.dynamic_update_slice_in_dim(zero, sums, s_here, 1).reshape(model)

        full_up_bias = lax.dynamic_update_slice_in_dim(
            jnp.zeros((groups, 4, unit), F32), grad_up_bias.reshape(groups, 1, unit), s_here % 4, 1
        ).reshape(n_dev, unit)
        sums = jnp.concatenate(
            [
                vector.reshape(n_dev, part)
                for vector in (
                    grad_gain_a, grad_shift_a, spread(bias_sums[:span]), spread(bias_sums[2 * span :]),
                    grad_out_bias, grad_gain_m, grad_shift_m, grad_down_bias,
                )
            ]
            + [full_up_bias],
            axis=1,
        )
        sums, unused = lax.optimization_barrier((sums, tuple(shares)))
        current = jnp.sum(lax.all_to_all(sums, ("batch", "seq"), 0, 0, tiled=True), axis=0)
        small_grads = [current[n * part : (n + 1) * part] for n in range(8)]

        return (
            out_rows[pre:][None],
            out_rows[:real][None],
            input_grad[pre:][None],
            input_grad[:real][None],
            small_grads[0],
            small_grads[1],
            shares[0],
            shares[1],
            shares[2],
            small_grads[2],
            small_grads[3],
            grad_out,
            small_grads[4],
            small_grads[5],
            small_grads[6],
            grad_up,
            current[8 * part :],
            grad_down,
            small_grads[7],
        )

    return body


def solution(mesh):
    rows = P("batch", "seq", None)
    vector = P(("batch", "seq"))
    matrix = P(("batch", "seq"), None)
    return jax.shard_map(
        build(mesh.shape["batch"], mesh.shape["seq"]),
        mesh=mesh,
        in_specs=(
            rows, rows, P("batch", None), vector, vector, matrix, matrix, matrix, vector, vector,
            matrix, vector, vector, vector, matrix, vector, matrix, vector, rows, rows,
        ),
        out_specs=(
            rows, rows, rows, rows, vector, vector, matrix, matrix, matrix, vector, vector, matrix,
            vector, vector, vector, matrix, vector, matrix, vector,
        ),
        check_vma=False,
    )
```

```python
import functools
import math

import jax
import jax.numpy as jnp
from jax import lax
from jax.experimental import pallas as pl
from jax.experimental.pallas import tpu as pltpu
from jax.sharding import PartitionSpec as P

HEADS = 32
HEAD_DIM = 64
EPS = 1e-05
NEGATIVE = -1e30
FAR = 1 << 20
BLOCK = 256
BF16 = jnp.bfloat16
F32 = jnp.float32


def contract(left, right, left_dim, right_dim):
    return lax.dot_general(
        left, right, (((left_dim,), (right_dim,)), ((), ())), preferred_element_type=F32
    )


def slot_pieces(devices, pre, tok, device):
    if isinstance(device, int):
        return [(0, device * pre, pre), (pre, devices * pre + device * tok, tok)]
    return [
        (0, pl.multiple_of(device * pre, 16), pre),
        (pre, pl.multiple_of(devices * pre + device * tok, 16), tok),
    ]


def block_pieces(devices, pre, tok, place_ref, first, blocks):
    pieces = []
    for n in range(blocks):
        for i in range(2):
            core = place_ref[0] if i == 0 else 1 - place_ref[0]
            device = place_ref[first + n] * 2 + core
            for row, slot, count in slot_pieces(devices, pre, tok, device):
                pieces.append((n, i * (pre + tok) + row, slot, count))
    return pieces


def result_pieces(devices, pre, tok, place_ref):
    pieces = []
    for z in range(devices // 2):
        for i in range(2):
            core = place_ref[0] if i == 0 else 1 - place_ref[0]
            for row, slot, count in slot_pieces(devices, pre, tok, z * 2 + core):
                pieces.append(((z * 2 + i) * (pre + tok) + row, slot, count))
    return pieces


def block_mask(place, low, high):
    return (place <= high) & ((place >= low) | (place < 0))


def forward_kernel(devices, pre, tok, heads, head_dim, *refs):
    chips = devices // 2
    spot_ref, place_ref, low_ref, high_ref = refs[:4]
    chunks = refs[4 : 4 + chips]
    o_ref, ot_ref, lse_ref, q_s, k_s, v_s, vt_s, acc_s = refs[4 + chips :]
    width = heads * head_dim
    blocks = devices * (pre + tok) // BLOCK
    for n, row, slot, cnt in block_pieces(devices, pre, tok, spot_ref, 1, chips):
        q_s[pl.ds(slot, cnt), :] = chunks[n][row : row + cnt, 0:width]
        k_s[pl.ds(slot, cnt), :] = chunks[n][row : row + cnt, width : 2 * width]
        v_s[pl.ds(slot, cnt), :] = chunks[n][row : row + cnt, 2 * width : 3 * width]
    for b in range(blocks):
        rows = slice(b * BLOCK, (b + 1) * BLOCK)
        vt_s[:, rows] = v_s[rows, :].astype(F32).T.astype(BF16)
    lane = lax.broadcasted_iota(jnp.int32, (BLOCK, width), 1) // head_dim

    def query_block(i, carry):
        qs = pl.ds(pl.multiple_of(i * BLOCK, BLOCK), BLOCK)
        q = q_s[qs, :]
        qh = [jnp.where(lane == h, q, jnp.zeros_like(q)) for h in range(heads)]
        low = low_ref[:, qs]
        high = high_ref[:, qs]
        acc_s[...] = jnp.zeros_like(acc_s)
        span = [slice(h * head_dim, (h + 1) * head_dim) for h in range(heads)]

        def key_block(j, inner):
            tops, totals = inner
            ks = pl.ds(pl.multiple_of(j * BLOCK, BLOCK), BLOCK)
            k = k_s[ks, :]
            bias = jnp.where(block_mask(place_ref[ks, :], low, high), 0.0, NEGATIVE)
            s = [contract(k, qh[h], 1, 1) + bias for h in range(heads)]
            new = [
                jnp.maximum(tops[h], jnp.max(s[h], axis=0, keepdims=True)) for h in range(heads)
            ]
            p = [jnp.exp(s[h] - new[h]) for h in range(heads)]
            alpha = [jnp.exp(tops[h] - new[h]) for h in range(heads)]
            sums = [
                totals[h] * alpha[h] + jnp.sum(p[h], axis=0, keepdims=True) for h in range(heads)
            ]
            for h in range(heads):
                share = contract(vt_s[span[h], ks], p[h].astype(BF16), 1, 0)
                acc_s[span[h], :] = acc_s[span[h], :] * alpha[h] + share
            return tuple(new), tuple(sums)

        start = (
            tuple(jnp.full((1, BLOCK), NEGATIVE, F32) for h in range(heads)),
            tuple(jnp.zeros((1, BLOCK), F32) for h in range(heads)),
        )
        tops, totals = lax.fori_loop(0, i + 1, key_block, start)
        for h in range(heads):
            acc_s[span[h], :] = acc_s[span[h], :] / totals[h]
            lse_ref[h : h + 1, qs] = tops[h] + jnp.log(totals[h])
        result = acc_s[...]
        ot_ref[:, qs] = result
        q_s[qs, :] = result.T.astype(BF16)
        return carry

    lax.fori_loop(0, blocks, query_block, 0)
    for row, slot, cnt in result_pieces(devices, pre, tok, spot_ref):
        o_ref[row : row + cnt, :] = q_s[pl.ds(slot, cnt), :]


def attention_forward(chunks, spots, place, low, high, devices, pre, tok, heads, head_dim):
    width = heads * head_dim
    rows = devices * (pre + tok)
    vmem = pl.BlockSpec(memory_space=pltpu.VMEM)
    pairs = rows * rows // 2 * heads
    return pl.pallas_call(
        functools.partial(forward_kernel, devices, pre, tok, heads, head_dim),
        out_shape=(
            jax.ShapeDtypeStruct((rows, width), BF16),
            jax.ShapeDtypeStruct((width, rows), F32),
            jax.ShapeDtypeStruct((8, rows), F32),
        ),
        in_specs=[pl.BlockSpec(memory_space=pltpu.SMEM)] + [vmem] * (3 + len(chunks)),
        out_specs=(vmem,) * 3,
        scratch_shapes=[
            pltpu.VMEM((rows, width), BF16),
            pltpu.VMEM((rows, width), BF16),
            pltpu.VMEM((rows, width), BF16),
            pltpu.VMEM((width, rows), BF16),
            pltpu.VMEM((width, BLOCK), F32),
        ],
        compiler_params=pltpu.CompilerParams(vmem_limit_bytes=48 << 20),
        cost_estimate=pl.CostEstimate(
            flops=16 * pairs * head_dim, bytes_accessed=rows * width * 12, transcendentals=pairs
        ),
    )(spots, place, low, high, *chunks)


def backward_kernel(
    devices, pre, tok, heads, head_dim, first, last, carried, final, *refs
):
    chips = devices // 2
    spot_ref, ot_ref, lse_ref, place_ref, low_ref, high_ref = refs[:6]
    chunks = refs[6 : 6 + chips]
    grads = refs[6 + chips : 6 + 2 * chips]
    refs = refs[6 + 2 * chips :]
    if carried:
        dq_in, dk_in, dv_in = refs[:3]
        refs = refs[3:]
    if final:
        out_ref, near_ref = refs[:2]
        q_s, k_s, v_s, do_s, kt_s, dqt_s, dq_s, dk_s, dv_s = refs[2:]
    else:
        dq_s, dk_s, dv_s, q_s, k_s, v_s, do_s, kt_s, dqt_s = refs
    width = heads * head_dim
    scale = 1.0 / math.sqrt(head_dim)
    for n, row, slot, cnt in block_pieces(devices, pre, tok, spot_ref, 1, chips):
        q_s[pl.ds(slot, cnt), :] = chunks[n][row : row + cnt, 0:width]
        k_s[pl.ds(slot, cnt), :] = chunks[n][row : row + cnt, width : 2 * width]
        v_s[pl.ds(slot, cnt), :] = chunks[n][row : row + cnt, 2 * width : 3 * width]
    for n, row, slot, cnt in block_pieces(devices, pre, tok, spot_ref, 1 + chips, chips):
        do_s[pl.ds(slot, cnt), :] = grads[n][row : row + cnt, :]
    for b in range(last):
        rows = slice(b * BLOCK, (b + 1) * BLOCK)
        kt_s[:, rows] = k_s[rows, :].astype(F32).T.astype(BF16)
    if carried:
        dq_s[...] = dq_in[...]
        dk_s[...] = dk_in[...]
        dv_s[...] = dv_in[...]
    else:
        dk_s[...] = jnp.zeros_like(dk_s)
        dv_s[...] = jnp.zeros_like(dv_s)
    lane = lax.broadcasted_iota(jnp.int32, (BLOCK, width), 1) // head_dim

    def query_block(i, carry):
        qs = pl.ds(pl.multiple_of(i * BLOCK, BLOCK), BLOCK)
        q = q_s[qs, :]
        do = do_s[qs, :]
        qh = [jnp.where(lane == h, q, jnp.zeros_like(q)) for h in range(heads)]
        doh = [jnp.where(lane == h, do, jnp.zeros_like(do)) for h in range(heads)]
        low = low_ref[:, qs]
        high = high_ref[:, qs]
        prod = do.astype(F32).T * ot_ref[:, qs]
        delta = [
            jnp.sum(prod[h * head_dim : (h + 1) * head_dim, :], axis=0, keepdims=True)
            for h in range(heads)
        ]
        lse = [lse_ref[h : h + 1, qs] for h in range(heads)]
        dqt_s[...] = jnp.zeros_like(dqt_s)

        def key_block(j, inner):
            ks = pl.ds(pl.multiple_of(j * BLOCK, BLOCK), BLOCK)
            k = k_s[ks, :]
            v = v_s[ks, :]
            bias = jnp.where(block_mask(place_ref[ks, :], low, high), 0.0, NEGATIVE)
            s = [contract(k, qh[h], 1, 1) for h in range(heads)]
            dp = [contract(v, doh[h], 1, 1) for h in range(heads)]
            p = [jnp.exp(s[h] + bias - lse[h]) for h in range(heads)]
            ds = [(p[h] * (dp[h] - delta[h])).astype(BF16) for h in range(heads)]
            dv = sum(contract(p[h].astype(BF16), doh[h], 1, 0) for h in range(heads))
            dk = sum(contract(ds[h], qh[h], 1, 0) for h in range(heads))
            for h in range(heads):
                hs = slice(h * head_dim, (h + 1) * head_dim)
                dqt_s[hs, :] += contract(kt_s[hs, ks], ds[h], 1, 0)
            dk_s[ks, :] += dk
            dv_s[ks, :] += dv
            return inner

        lax.fori_loop(0, i + 1, key_block, 0)
        dq_s[qs, :] = (dqt_s[...] * scale).T.astype(BF16)
        return carry

    lax.fori_loop(first, last, query_block, 0)
    if final:
        for row, slot, cnt in result_pieces(devices, pre, tok, spot_ref):
            out_ref[row : row + cnt, 0:width] = dq_s[pl.ds(slot, cnt), :]
            out_ref[row : row + cnt, width : 2 * width] = dk_s[pl.ds(slot, cnt), :].astype(BF16)
            out_ref[row : row + cnt, 2 * width : 3 * width] = dv_s[pl.ds(slot, cnt), :].astype(BF16)
        both = 2 * (pre + tok)
        for n in range(chips):
            chip = pl.multiple_of(spot_ref[1 + n] * both, 16)
            near_ref[n * both : (n + 1) * both, :] = out_ref[pl.ds(chip, both), :]


def attention_backward(
    chunks, grads, spots, ot, lse, place, low, high, devices, pre, tok, heads, head_dim, first, last, carry, final
):
    width = heads * head_dim
    rows = devices * (pre + tok)
    vmem = pl.BlockSpec(memory_space=pltpu.VMEM)
    pairs = (last - first) * (last + first + 1) // 2 * BLOCK * BLOCK * heads
    low_rows = pltpu.VMEM((rows, width), BF16)
    sums = [((rows, width), BF16), ((rows, width), F32), ((rows, width), F32)]
    scratch = [
        low_rows,
        low_rows,
        low_rows,
        low_rows,
        pltpu.VMEM((width, rows), BF16),
        pltpu.VMEM((width, BLOCK), F32),
    ]
    if final:
        out_shape = (jax.ShapeDtypeStruct((rows, 3 * width), BF16),) * 2
        scratch += [pltpu.VMEM(shape, dtype) for shape, dtype in sums]
    else:
        out_shape = tuple(jax.ShapeDtypeStruct(shape, dtype) for shape, dtype in sums)
    return pl.pallas_call(
        functools.partial(
            backward_kernel, devices, pre, tok, heads, head_dim, first, last, bool(carry), final
        ),
        out_shape=out_shape,
        in_specs=[pl.BlockSpec(memory_space=pltpu.SMEM)]
        + [vmem] * (5 + len(chunks) + len(grads) + len(carry)),
        out_specs=(vmem,) * len(out_shape),
        scratch_shapes=scratch,
        compiler_params=pltpu.CompilerParams(vmem_limit_bytes=58 << 20),
        cost_estimate=pl.CostEstimate(
            flops=20 * pairs * head_dim, bytes_accessed=rows * width * 20, transcendentals=pairs
        ),
    )(spots, ot, lse, place, low, high, *chunks, *grads, *carry)


def matmul_kernel(flipped, left_ref, right_ref, out_ref):
    out_ref[...] = contract(left_ref[...], right_ref[...], 1, 1 if flipped else 0).astype(BF16)


def matmul_low(left, right, flipped):
    rows, depth = left.shape
    columns = right.shape[0] if flipped else right.shape[1]
    step = 512
    block = (step, depth) if flipped else (depth, step)
    return pl.pallas_call(
        functools.partial(matmul_kernel, flipped),
        grid=(columns // step,),
        out_shape=jax.ShapeDtypeStruct((rows, columns), BF16),
        in_specs=[
            pl.BlockSpec((rows, depth), lambda n: (0, 0)),
            pl.BlockSpec(block, (lambda n: (n, 0)) if flipped else (lambda n: (0, n))),
        ],
        out_specs=pl.BlockSpec((rows, step), lambda n: (0, n)),
        compiler_params=pltpu.CompilerParams(vmem_limit_bytes=48 << 20),
        cost_estimate=pl.CostEstimate(flops=1 << 20, bytes_accessed=1 << 16, transcendentals=0),
    )(left, right)


def transposed_kernel(left_ref, right_ref, out_ref):
    out_ref[...] = contract(left_ref[...], right_ref[...], 0, 0).astype(BF16)


def matmul_transposed(left, right):
    depth, rows = left.shape
    columns = right.shape[1]
    step = 512
    return pl.pallas_call(
        transposed_kernel,
        grid=(rows // step,),
        out_shape=jax.ShapeDtypeStruct((rows, columns), BF16),
        in_specs=[
            pl.BlockSpec((depth, step), lambda n: (0, n)),
            pl.BlockSpec((depth, columns), lambda n: (0, 0)),
        ],
        out_specs=pl.BlockSpec((step, columns), lambda n: (n, 0)),
        compiler_params=pltpu.CompilerParams(vmem_limit_bytes=56 << 20),
        cost_estimate=pl.CostEstimate(flops=1 << 20, bytes_accessed=1 << 16, transcendentals=0),
    )(left, right)


def rows_product_kernel(*refs):
    chunks, right_ref, out_ref = refs[:-2], refs[-2], refs[-1]
    rows = chunks[0].shape[0]
    total = contract(chunks[0][...], right_ref[0:rows, :], 0, 0)
    for n in range(1, len(chunks)):
        total += contract(chunks[n][...], right_ref[n * rows : (n + 1) * rows, :], 0, 0)
    out_ref[...] = total.astype(BF16)


def rows_product(chunks, right):
    rows, columns = chunks[0].shape
    step = 512
    return pl.pallas_call(
        rows_product_kernel,
        grid=(columns // step,),
        out_shape=jax.ShapeDtypeStruct((columns, right.shape[1]), BF16),
        in_specs=[pl.BlockSpec((rows, step), lambda n: (0, n))] * len(chunks)
        + [pl.BlockSpec(right.shape, lambda n: (0, 0))],
        out_specs=pl.BlockSpec((step, right.shape[1]), lambda n: (n, 0)),
        compiler_params=pltpu.CompilerParams(vmem_limit_bytes=56 << 20),
        cost_estimate=pl.CostEstimate(
            flops=right.shape[0] * columns * right.shape[1] // 2, bytes_accessed=1 << 16, transcendentals=0
        ),
    )(*chunks, right)


def slot_labels(lengths, devices, pre, tok, real):
    slot = jnp.arange(devices * pre, dtype=jnp.int32)
    inside = slot % pre
    place = (slot // pre) * real + inside - devices * real
    is_real = inside < real
    t = jnp.arange(devices * tok, dtype=jnp.int32)
    ends = jnp.cumsum(lengths)
    start = jnp.max(jnp.where(ends[None, :] <= t[:, None], ends[None, :], 0), axis=1)
    places = jnp.concatenate([jnp.where(is_real, place, FAR), t])
    high = jnp.concatenate([jnp.where(is_real, place, -1), t])
    low = jnp.concatenate([jnp.full((devices * pre,), FAR, jnp.int32), start])
    return places[:, None], low[None, :], high[None, :]


def normalize(values):
    center = values - jnp.mean(values, axis=-1, keepdims=True)
    spread = jnp.mean(center * center, axis=-1, keepdims=True)
    inverse = lax.rsqrt(spread + EPS)
    return center * inverse, inverse


def norm_backward(grad, hat, inverse, gain):
    e = grad * gain
    mean_e = jnp.mean(e, axis=-1, keepdims=True)
    mean_eh = jnp.mean(e * hat, axis=-1, keepdims=True)
    return inverse * (e - mean_e - hat * mean_eh)


def gelu_parts(values):
    cdf = 0.5 * (1.0 + lax.erf(values * (1.0 / math.sqrt(2.0))))
    return cdf


def pick(array, index, axis):
    return lax.dynamic_index_in_dim(array, index, axis, keepdims=False)


def build(n_batch, n_seq):
    n_z = n_seq // 2
    n_dev = n_batch * n_seq
    groups = n_dev // 4
    size_of = {"batch": n_batch, "seq": n_seq}

    def bits_of(n):
        bits = []
        bit = 1
        while bit < n:
            bits.append(bit)
            bit *= 2
        return bits

    core = ("seq", 1)
    near = ("seq", 2)
    up_batch = [("batch", bit) for bit in bits_of(n_batch)]
    down_batch = list(reversed(up_batch))
    far_bits = [("seq", bit) for bit in bits_of(n_seq) if bit >= 4]
    chip_bits = [near] + far_bits
    group_bits = down_batch + list(reversed(far_bits))
    all_bits = down_batch + [("seq", bit) for bit in reversed(bits_of(n_seq))]

    def swap_pairs(which):
        axis, bit = which
        return axis, [(i, i ^ bit) for i in range(size_of[axis])]

    def shift_pairs(distance):
        return "seq", [
            (z * 2 + c, ((z + distance) % n_z) * 2 + c) for z in range(n_z) for c in range(2)
        ]

    def right_pairs(first, last):
        return "seq", [(z * 2 + c, z * 2 + 2 + c) for z in range(first, last) for c in range(2)]

    def left_pairs(first, last):
        return "seq", [(z * 2 + c, z * 2 - 2 + c) for z in range(first, last) for c in range(2)]

    def side(which):
        axis, bit = which
        return (lax.axis_index(axis) // bit) % 2

    def permute(array, pairs):
        return lax.ppermute(array, pairs[0], pairs[1])

    class Clock:
        def __init__(self):
            self.gate = ()

        def hold(self, *arrays):
            if self.gate:
                arrays = lax.optimization_barrier(tuple(arrays) + tuple(self.gate))[: len(arrays)]
            return arrays[0] if len(arrays) == 1 else arrays

        def tick(self, *arrays):
            self.gate = arrays

    def join(mine, other, which, axis):
        first = side(which) == 0
        return jnp.where(first, jnp.stack([mine, other], axis), jnp.stack([other, mine], axis))

    def body(
        tokens, prefix, seg_lengths, attn_gain, attn_shift, query_weight, key_weight, value_weight,
        query_bias, value_bias, output_weight, output_bias, mlp_gain, mlp_shift, up_weight, up_bias,
        down_weight, down_bias, cot_tokens, cot_prefix,
    ):
        clock = Clock()

        def swap(array, which):
            return permute(array, swap_pairs(which))

        def gather_bits(array, order, ranked):
            taken = []
            current = array
            for which in order:
                other = swap(current, which)
                rank = ranked.index(which)
                place = sum(1 for t in taken if ranked.index(t) < rank)
                current = join(current, other, which, place)
                taken.append(which)
            return current.reshape((2 ** len(order),) + array.shape)

        def part_of(current, left, which, mine):
            return pick(current, side(which) if mine else 1 - side(which), left.index(which))

        def hop_scatter(current, left, which, last):
            other = swap(part_of(current, left, which, False).astype(BF16), which)
            total = part_of(current, left, which, True).astype(F32) + other.astype(F32)
            rest = [b for b in left if b != which]
            return (total if last else total.astype(BF16)), rest

        tok = tokens.shape[1]
        real = prefix.shape[1]
        pre = -(-real // 16) * 16
        width = pre + tok
        model = tokens.shape[2]
        heads = HEADS // n_seq
        span = heads * HEAD_DIM
        part = model // n_dev
        unit = up_bias.shape[0]
        hidden_here = groups * unit
        s_here = lax.axis_index("seq")
        z_here = s_here // 2
        c_here = s_here % 2
        near_here = side(near)
        lengths = seg_lengths[0]

        def rows_of(pre_part, tok_part):
            return jnp.concatenate([jnp.pad(pre_part, ((0, pre - real), (0, 0))), tok_part], axis=0)

        def device_rows(array, z, c):
            return lax.dynamic_slice_in_dim(array, (z * 2 + c) * width, width, 0)

        own = rows_of(prefix[0], tokens[0])
        row = jnp.arange(width, dtype=jnp.int32)
        position = row - pre + s_here * tok
        valid = jnp.where(row < pre, row < real, position < jnp.sum(lengths))
        validity = valid.astype(F32)[:, None]

        far_group = list(reversed(far_bits))
        n_far = groups // n_batch
        far_here = s_here // 4

        def afar(array, mask):
            return permute(array, ("seq", [(i, i ^ (mask * 4)) for i in range(n_seq)]))

        def batch_gather(array):
            return lax.all_gather(array, "batch", axis=0, tiled=True)

        def batch_sum(array):
            return lax.psum_scatter(array, "batch", scatter_dimension=0, tiled=True)

        def set_far(whole, blocks, index):
            blocks = blocks.reshape((n_batch, 1, -1) + blocks.shape[1:])
            return lax.dynamic_update_slice_in_dim(whole, blocks, index, 1)

        steps = [(permute(own, right_pairs(0, n_z - 1)), permute(own, left_pairs(1, n_z)))]
        small = jnp.concatenate(
            [attn_gain, attn_shift, query_bias, value_bias, output_bias, mlp_gain, mlp_shift, down_bias, up_bias]
        )
        small_bits = down_batch + [core]
        small = gather_bits(small, list(reversed(small_bits)), small_bits)
        down_gate, unused = lax.optimization_barrier((down_weight, small))
        down_own = batch_gather(down_gate)

        stacked = jnp.stack([query_weight, key_weight, value_weight], axis=1)
        stacked = stacked.reshape(part, 3, heads, n_z, 2, HEAD_DIM).transpose(3, 4, 0, 1, 2, 5)
        stacked = stacked.reshape(n_z, 2, part, 3 * span)
        mixed = join(pick(stacked, c_here, 1), swap(pick(stacked, 1 - c_here, 1), core), core, 1)
        mixed = mixed.reshape(n_z, 2 * part, 3 * span)
        flat = small.reshape(-1)
        small_rows = -(-flat.shape[0] // (3 * span * 16)) * 16
        flat = jnp.pad(flat, (0, small_rows * 3 * span - flat.shape[0]))
        flat = jnp.broadcast_to(flat.reshape(1, small_rows, 3 * span), (n_z, small_rows, 3 * span))
        mixed = jnp.concatenate([mixed, flat], axis=1)

        up_near = up_weight.reshape(part, groups, 2, 2, unit)
        up_near = join(pick(up_near, c_here, 3), swap(pick(up_near, 1 - c_here, 3), core), core, 0)

        clock.tick(*steps[0], up_near)

        def shift_out(choose):
            pieces = [choose((z_here + d) % n_z) for d in range(1, n_z)]
            pieces = clock.hold(*pieces) if len(pieces) > 1 else [clock.hold(*pieces)]
            got = [permute(piece, shift_pairs(d + 1)) for d, piece in enumerate(pieces)]
            return [(z_here, choose(z_here))] + [
                ((z_here - d - 1) % n_z, piece) for d, piece in enumerate(got)
            ]

        placed = shift_out(lambda z: pick(mixed, z, 0))
        ranked_o = far_group + [near]
        up_other = swap(clock.hold(pick(up_near, 1 - near_here, 3)), near)
        gathered_o = gather_bits(clock.hold(output_weight), far_bits, far_group)
        clock.tick(up_other, gathered_o, *[piece for unused, piece in placed[1:]])
        up_block = join(pick(up_near, near_here, 3), up_other, near, 0)
        up_block = up_block.reshape(4 * part, hidden_here)
        local = jnp.zeros((n_z, 2 * part, 3 * span), BF16)
        small_z = jnp.zeros((n_z, small_rows, 3 * span), BF16)
        for z, piece in placed:
            local = lax.dynamic_update_slice_in_dim(local, piece[None, : 2 * part], z, 0)
            small_z = lax.dynamic_update_slice_in_dim(small_z, piece[None, 2 * part :], z, 0)
        local, unused = lax.optimization_barrier((local, down_own))
        weight_qkv = batch_gather(local.reshape(n_z * 2 * part, 3 * span))
        small = small_z.reshape(n_z, -1)[:, : n_batch * 2 * (8 * part + unit)]
        small = small.reshape(n_z, n_batch, 2, 8 * part + unit).transpose(1, 0, 2, 3)
        small = small.reshape(n_dev, 8 * part + unit)
        vectors = [small[:, n * part : (n + 1) * part].reshape(model).astype(F32) for n in range(8)]
        gain_a, shift_a, bias_q, bias_v, bias_o, gain_m, shift_m, bias_down = vectors
        bias_up = pick(small[:, 8 * part :].reshape(groups, 4, unit), s_here % 4, 1)
        bias_up = bias_up.reshape(hidden_here).astype(F32)

        bias_qkv = jnp.concatenate(
            [
                pick(bias_q.reshape(heads, n_seq, HEAD_DIM), s_here, 1).reshape(span),
                jnp.zeros((span,), F32),
                pick(bias_v.reshape(heads, n_seq, HEAD_DIM), s_here, 1).reshape(span),
            ]
        )
        factor = jnp.concatenate(
            [jnp.full((span,), 1.0 / math.sqrt(HEAD_DIM), F32), jnp.ones((2 * span,), F32)]
        )

        def source(n):
            if n == 0:
                return z_here
            short = jnp.minimum(z_here, n_z - 1 - z_here)
            both = n <= 2 * short
            distance = jnp.where(both, (n + 1) // 2, n - short)
            left = jnp.where(both, n % 2 == 1, 2 * z_here >= n_z)
            return jnp.where(left, z_here - distance, z_here + distance)

        def rows_from(n):
            rows = own
            for d in range((n + 1) // 2, n + 1) if n else ():
                right, left = steps[d - 1]
                rows = jnp.where(source(n) == z_here - d, right, rows)
                rows = jnp.where(source(n) == z_here + d, left, rows)
            rows = jnp.concatenate([rows, swap(rows, core)], axis=0)
            hat, unused = normalize(rows.astype(F32))
            return (hat * gain_a + shift_a).astype(BF16)

        def qkv_of(rows):
            result = (contract(rows, weight_qkv, 1, 0) + bias_qkv).astype(BF16).astype(F32) * factor
            return result.astype(BF16)

        exact = part == HEAD_DIM and heads == n_batch
        normed = []
        for k in range(2, n_z):
            right, left = clock.hold(*steps[-1])
            steps.append(
                (permute(right, right_pairs(k - 1, n_z - 1)), permute(left, left_pairs(1, n_z - k + 1)))
            )
            normed.append(rows_from(k - 2))
            clock.tick(*steps[-1], normed[-1])
        up_gate, unused = lax.optimization_barrier((up_block, weight_qkv))
        up_own = batch_gather(up_gate)

        other = swap(clock.hold(gathered_o), near)
        gathered_o = join(gathered_o, other, near, 1)
        gathered_o, unused = lax.optimization_barrier((gathered_o, up_own))
        gathered_o = batch_gather(gathered_o.reshape(n_z * part, model))

        weight_o = gathered_o.reshape(n_batch, n_z, part, model)
        if exact:
            weight_o = weight_o.transpose(1, 0, 2, 3).reshape(n_z * span, model)
        else:
            weight_o = join(weight_o, swap(weight_o, core), core, 2)
            weight_o = weight_o.reshape(heads, n_z, 2, HEAD_DIM, model)
            weight_o = pick(weight_o, c_here, 2).transpose(1, 0, 2, 3).reshape(n_z * span, model)

        qkv = []
        for n in range(n_z):
            if n >= n_z - 2:
                normed.append(rows_from(n))
            qkv.append(qkv_of(normed[n]))
        shifted = [z_here] + [(z_here - d) % n_z for d in range(1, n_z)]
        spots = jnp.stack([c_here] + [source(n) for n in range(n_z)] + shifted).astype(jnp.int32)

        cot_rows = rows_of(cot_prefix[0], cot_tokens[0]).astype(F32)
        mlp_out_grad = (validity * cot_rows).astype(BF16)
        places, low, high = slot_labels(lengths, n_seq, pre, tok, real)
        clock.tick(other)
        *qkv, up_gate, grad_gate = clock.hold(*qkv, up_block, mlp_out_grad)
        up_far = [afar(up_gate, mask) for mask in range(1, n_far)]
        grad_far = swap(grad_gate, near)
        attended, attended_t, log_total = attention_forward(
            qkv, spots, places, low, high, n_seq, pre, tok, heads, HEAD_DIM
        )
        clock.tick(attended, grad_far, *up_far)
        up_blocks = [batch_gather(clock.hold(piece)) for piece in up_far]

        blocks = attended.reshape(n_z, 2 * width, span)
        placed = shift_out(lambda z: pick(blocks, z, 0))
        *normed, up_own, down_own, unused = lax.optimization_barrier(
            tuple(normed) + (up_own, down_own, attended)
        )
        weight_up = set_far(
            jnp.zeros((n_batch, n_far, 4 * part, hidden_here), BF16), up_own, far_here
        )
        weight_down = set_far(
            jnp.zeros((n_batch, n_far, unit, model), BF16), down_own, far_here
        )
        grad_rows = jnp.concatenate(
            [mlp_out_grad, swap(mlp_out_grad, core), grad_far, swap(grad_far, core)], axis=0
        )
        spread_o = [piece for unused, piece in placed[1:]]
        *spread_o, weight_up, weight_down, weight_o = lax.optimization_barrier(
            (*spread_o, weight_up, weight_down, weight_o)
        )
        placed = [placed[0]] + [(z, piece) for (z, unused), piece in zip(placed[1:], spread_o)]
        mixed_low = jnp.zeros((2 * width, n_z * span), BF16)
        for z, piece in placed:
            mixed_low = lax.dynamic_update_slice_in_dim(mixed_low, piece, z * span, 1)
        clock.tick(mixed_low, weight_up, weight_down)
        down_far = [afar(clock.hold(down_weight), mask) for mask in range(1, n_far)]
        mixed_held = clock.hold(mixed_low)
        branch_away = contract(mixed_held[width:], weight_o, 1, 0).astype(BF16)
        branch_away = swap(branch_away, core)
        branch = contract(mixed_held[:width], weight_o, 1, 0) + branch_away.astype(F32) + bias_o
        rows_in = own.astype(F32)
        resid = rows_in + validity * branch
        hat_m, inverse_m = normalize(resid)
        normed_own = (hat_m * gain_m + shift_m).astype(BF16)

        normed_near = swap(normed_own, core)
        normed_far = swap(normed_own, near)
        *down_far, unused = lax.optimization_barrier(tuple(down_far) + (normed_own,))
        down_blocks = [batch_gather(piece) for piece in down_far]
        *up_blocks, unused = lax.optimization_barrier(tuple(up_blocks) + (normed_own,))
        for mask, piece in enumerate(up_blocks):
            weight_up = set_far(weight_up, piece, far_here ^ (mask + 1))
        weight_up = weight_up.reshape(model, hidden_here)
        normed_far, weight_up = lax.optimization_barrier((normed_far, weight_up))
        normed_parts = [normed_own, normed_near, normed_far, swap(normed_far, core)]
        normed_rows = jnp.concatenate(normed_parts, axis=0)

        before = contract(normed_rows, weight_up, 1, 0) + bias_up
        cdf = 0.5 * (1.0 + lax.erf(before * (1.0 / math.sqrt(2.0))))
        hidden = (before * cdf).astype(BF16)
        slope = cdf + before * jnp.exp(-0.5 * before * before) * (1.0 / math.sqrt(2.0 * math.pi))
        *down_blocks, unused = lax.optimization_barrier(tuple(down_blocks) + (hidden,))
        for mask, piece in enumerate(down_blocks):
            weight_down = set_far(weight_down, piece, far_here ^ (mask + 1))
        weight_down = weight_down.reshape(hidden_here, model)
        grad_down = contract(hidden, grad_rows, 0, 0).astype(BF16)
        grad_down, grad_held = lax.optimization_barrier((grad_down, grad_rows))
        grad_down = batch_sum(grad_down)
        hidden_grad = contract(grad_held, weight_down, 1, 1)
        pre_grad = (hidden_grad * slope).astype(BF16)

        share_f = contract(pre_grad[2 * width :], weight_up, 1, 1).astype(BF16)
        back = swap(share_f[width:], core)
        back = (share_f[:width].astype(F32) + back.astype(F32)).astype(BF16)
        pre_held, hidden_held, back_held = lax.optimization_barrier((pre_grad, hidden, back))
        back = swap(back_held, near)
        share_n = matmul_low(pre_held[: 2 * width], weight_up, True)
        out_share = matmul_low(hidden_held, weight_down, False)
        *normed_late, unused = lax.optimization_barrier((*normed_parts, back_held))
        normed_late = jnp.concatenate(normed_late, axis=0)
        back, out_share, share_n, normed_late = lax.optimization_barrier(
            (back, out_share, share_n, normed_late)
        )
        here = swap(share_n[width:], core)
        normed_grad = share_n[:width].astype(F32) + here.astype(F32) + back.astype(F32)

        grad_up_bias = jnp.sum(pre_grad.astype(F32), axis=0)
        grad_down_bias = jnp.sum(mlp_out_grad.astype(F32), axis=0)
        grad_gain_m = jnp.sum(normed_grad * hat_m, axis=0)
        grad_shift_m = jnp.sum(normed_grad, axis=0)
        resid_grad = cot_rows + norm_backward(normed_grad, hat_m, inverse_m, gain_m)

        branch_grad = (validity * resid_grad).astype(BF16)
        grad_out_bias = jnp.sum(branch_grad.astype(F32), axis=0)
        branch_grad = jnp.concatenate([branch_grad, swap(branch_grad, core)], axis=0)
        mixed_grad = contract(branch_grad, weight_o, 1, 1).astype(BF16)
        clock.tick(mixed_grad)
        placed = shift_out(lambda z: lax.dynamic_slice_in_dim(mixed_grad, z * span, span, 1))
        grad_gate, branch_gate, mixed_gate, unused = lax.optimization_barrier(
            (pre_grad, branch_grad, mixed_low, mixed_grad)
        )
        grad_up = matmul_transposed(normed_late, grad_gate)
        grad_out = matmul_transposed(mixed_gate, branch_gate)
        if exact:
            grad_out = grad_out.reshape(n_z, n_batch, part, model).transpose(1, 0, 2, 3)
        else:
            full = jnp.zeros((heads, n_z, 2, HEAD_DIM, model), BF16)
            grad_out = grad_out.reshape(n_z, heads, 1, HEAD_DIM, model).transpose(1, 0, 2, 3, 4)
            grad_out = lax.dynamic_update_slice_in_dim(full, grad_out, c_here, 2)
            grad_out = grad_out.reshape(n_batch, n_z, 2, part, model)
            grad_out = pick(grad_out, c_here, 2).astype(F32) + swap(
                pick(grad_out, 1 - c_here, 2), core
            ).astype(F32)
            grad_out = grad_out.astype(BF16)
        rows_grad = [piece for unused, piece in placed]
        out_back = swap(out_share[3 * width :], core)
        out_back = (out_share[2 * width : 3 * width].astype(F32) + out_back.astype(F32)).astype(BF16)
        grad_up, grad_out, out_back, *rows_grad = lax.optimization_barrier(
            (grad_up, grad_out, out_back, *rows_grad)
        )
        grad_up = batch_sum(grad_up)
        grad_out = batch_sum(grad_out.reshape(n_batch * n_z * part, model))

        clock.tick(*rows_grad, grad_down, out_share)
        down_gate, out_away, *rows_grad = clock.hold(grad_down, out_back, *rows_grad)
        down_sum = down_gate.reshape((2,) * len(far_bits) + (unit, model))
        rest_down = list(far_group)
        for n, which in enumerate(far_bits):
            down_sum, rest_down = hop_scatter(
                down_sum, rest_down, which, n == len(far_bits) - 1
            )
        grad_down = down_sum
        out_back = swap(out_away, near)
        blocks = n_seq * width // BLOCK
        qkv_grad, relative = attention_backward(
            qkv, rows_grad, spots, attended_t, log_total, places, low, high,
            n_seq, pre, tok, heads, HEAD_DIM, 0, blocks, (), True,
        )
        qkv_grad, relative, grad_down, out_back = lax.optimization_barrier(
            (qkv_grad, relative, grad_down, out_back)
        )
        clock.tick(qkv_grad, grad_down, out_back)

        chunks = [None] * n_z
        aways = []
        order = []
        for k in range(1, n_z):
            for r in (n_z - k, k):
                if r not in order:
                    order.append(r)
        for r in order + [0]:
            z = (z_here + r) % n_z
            away = contract(device_rows(qkv_grad, z, 1), weight_qkv, 1, 1).astype(BF16)
            away = swap(away, core)
            aways.append(away)
            keep = contract(device_rows(qkv_grad, z, 0), weight_qkv, 1, 1)
            chunks[r] = keep + away.astype(F32)
        right = None
        left = None
        for k in range(1, n_z):
            going_r = jnp.where(z_here + n_z - k < n_z, chunks[n_z - k], 0.0)
            going_l = jnp.where(z_here - (n_z - k) >= 0, chunks[k], 0.0)
            if k > 1:
                going_r = going_r + right.astype(F32)
                going_l = going_l + left.astype(F32)
            going_r, going_l = clock.hold(going_r.astype(BF16), going_l.astype(BF16))
            right = permute(going_r, right_pairs(0, k))
            left = permute(going_l, left_pairs(n_z - k, n_z))
            started = [right, left]
            if k == 1:
                up_sum = clock.hold(grad_up).reshape((2,) * len(far_bits) + (4 * part, hidden_here))
                rest_up = list(far_group)
                for which in far_bits:
                    up_sum, rest_up = hop_scatter(up_sum, rest_up, which, False)
                relative, unused = lax.optimization_barrier((relative, going_r))
                grad_qkv = rows_product(normed, relative)
                grad_qkv, right, left, up_sum, grad_out, unused = lax.optimization_barrier(
                    (grad_qkv, right, left, up_sum, grad_out, tuple(aways[2:]))
                )
                grad_qkv = batch_sum(grad_qkv)
                started = [right, left, up_sum]
            if k == 2:
                grad_up = up_sum.reshape(2, 2, part, hidden_here)
                up_other = swap(clock.hold(pick(grad_up, 1 - near_here, 0)), near)
                grad_up = join(pick(grad_up, near_here, 0), up_other, near, 0)
                rest_o = list(ranked_o)
                grad_out = clock.hold(grad_out).reshape((2,) * len(ranked_o) + (part, model))
                grad_out, rest_o = hop_scatter(grad_out, rest_o, near, False)
                started += [up_other, grad_out]
            if k == n_z - 1:
                grad_qkv = grad_qkv.reshape(n_z, 2, part, 3 * span)
                grad_qkv = join(
                    pick(grad_qkv, c_here, 1), swap(pick(grad_qkv, 1 - c_here, 1), core), core, 1
                )
                placed = shift_out(lambda z: pick(grad_qkv, z, 0))
                out_share, out_back, grads_late = clock.hold(out_share, out_back, qkv_grad)
                out_here = swap(out_share[width : 2 * width], core)
                final = out_share[:width].astype(F32) + out_here.astype(F32) + out_back.astype(F32)
                final = resid + validity * (final + bias_down)
                out_rows = final.astype(BF16)
                bias_sums = jnp.sum(grads_late.astype(F32), axis=0)
                grad_out = clock.hold(grad_out)
                for n, which in enumerate(far_bits):
                    grad_out, rest_o = hop_scatter(grad_out, rest_o, which, n == len(far_bits) - 1)
            clock.tick(*started)
        right, left, unused = lax.optimization_barrier(
            (right, left, (out_rows, bias_sums, *[piece for unused, piece in placed[1:]]))
        )
        normed_back = chunks[0] + right.astype(F32) + left.astype(F32)

        grad_up = join(pick(grad_up, c_here, 1), swap(pick(grad_up, 1 - c_here, 1), core), core, 1)
        grad_up = grad_up.reshape(4, part, groups, unit).transpose(1, 2, 0, 3)
        grad_up = grad_up.reshape(part, n_dev * unit).astype(F32)


        shares = jnp.zeros((n_z, 2, part, 3 * span), BF16)
        for z, piece in placed:
            shares = lax.dynamic_update_slice_in_dim(shares, piece[None], z, 0)
        shares = shares.reshape(n_seq, part, 3, heads, HEAD_DIM)
        shares = [
            shares[:, :, n].transpose(1, 2, 0, 3).reshape(part, model).astype(F32) for n in range(3)
        ]

        hat_a, inverse_a = normalize(rows_in)
        grad_gain_a = jnp.sum(normed_back * hat_a, axis=0)
        grad_shift_a = jnp.sum(normed_back, axis=0)
        input_grad = resid_grad + norm_backward(normed_back, hat_a, inverse_a, gain_a)

        zero = jnp.zeros((heads, n_seq, HEAD_DIM), F32)

        def spread(sums):
            sums = sums.reshape(heads, 1, HEAD_DIM)
            return lax.dynamic_update_slice_in_dim(zero, sums, s_here, 1).reshape(model)

        full_up_bias = lax.dynamic_update_slice_in_dim(
            jnp.zeros((groups, 4, unit), F32), grad_up_bias.reshape(groups, 1, unit), s_here % 4, 1
        ).reshape(n_dev, unit)
        sums = jnp.concatenate(
            [
                vector.reshape(n_dev, part)
                for vector in (
                    grad_gain_a, grad_shift_a, spread(bias_sums[:span]), spread(bias_sums[2 * span :]),
                    grad_out_bias, grad_gain_m, grad_shift_m, grad_down_bias,
                )
            ]
            + [full_up_bias],
            axis=1,
        )
        sums, unused = lax.optimization_barrier((sums, tuple(shares)))
        current = jnp.sum(lax.all_to_all(sums, ("batch", "seq"), 0, 0, tiled=True), axis=0)
        small_grads = [current[n * part : (n + 1) * part] for n in range(8)]

        return (
            out_rows[pre:][None],
            out_rows[:real][None],
            input_grad[pre:][None],
            input_grad[:real][None],
            small_grads[0],
            small_grads[1],
            shares[0],
            shares[1],
            shares[2],
            small_grads[2],
            small_grads[3],
            grad_out,
            small_grads[4],
            small_grads[5],
            small_grads[6],
            grad_up,
            current[8 * part :],
            grad_down,
            small_grads[7],
        )

    return body


def solution(mesh):
    rows = P("batch", "seq", None)
    vector = P(("batch", "seq"))
    matrix = P(("batch", "seq"), None)
    return jax.shard_map(
        build(mesh.shape["batch"], mesh.shape["seq"]),
        mesh=mesh,
        in_specs=(
            rows, rows, P("batch", None), vector, vector, matrix, matrix, matrix, vector, vector,
            matrix, vector, vector, vector, matrix, vector, matrix, vector, rows, rows,
        ),
        out_specs=(
            rows, rows, rows, rows, vector, vector, matrix, matrix, matrix, vector, vector, matrix,
            vector, vector, vector, matrix, vector, matrix, vector,
        ),
        check_vma=False,
    )
```

```python
import functools
import math

import jax
import jax.numpy as jnp
from jax import lax
from jax.experimental import pallas as pl
from jax.experimental.pallas import tpu as pltpu
from jax.sharding import PartitionSpec as P

HEADS = 32
HEAD_DIM = 64
EPS = 1e-05
NEGATIVE = -1e30
FAR = 1 << 20
BLOCK = 256
BF16 = jnp.bfloat16
F32 = jnp.float32


def contract(left, right, left_dim, right_dim):
    return lax.dot_general(
        left, right, (((left_dim,), (right_dim,)), ((), ())), preferred_element_type=F32
    )


def slot_pieces(devices, pre, tok, device):
    if isinstance(device, int):
        return [(0, device * pre, pre), (pre, devices * pre + device * tok, tok)]
    return [
        (0, pl.multiple_of(device * pre, 16), pre),
        (pre, pl.multiple_of(devices * pre + device * tok, 16), tok),
    ]


def block_pieces(devices, pre, tok, place_ref, first, blocks):
    pieces = []
    for n in range(blocks):
        for i in range(2):
            core = place_ref[0] if i == 0 else 1 - place_ref[0]
            device = place_ref[first + n] * 2 + core
            for row, slot, count in slot_pieces(devices, pre, tok, device):
                pieces.append((n, i * (pre + tok) + row, slot, count))
    return pieces


def result_pieces(devices, pre, tok, place_ref):
    pieces = []
    for z in range(devices // 2):
        for i in range(2):
            core = place_ref[0] if i == 0 else 1 - place_ref[0]
            for row, slot, count in slot_pieces(devices, pre, tok, z * 2 + core):
                pieces.append(((z * 2 + i) * (pre + tok) + row, slot, count))
    return pieces


def block_mask(place, low, high):
    return (place <= high) & ((place >= low) | (place < 0))


def forward_kernel(devices, pre, tok, heads, head_dim, *refs):
    chips = devices // 2
    spot_ref, place_ref, low_ref, high_ref = refs[:4]
    chunks = refs[4 : 4 + chips]
    o_ref, ot_ref, lse_ref, q_s, k_s, v_s, vt_s, acc_s = refs[4 + chips :]
    width = heads * head_dim
    blocks = devices * (pre + tok) // BLOCK
    for n, row, slot, cnt in block_pieces(devices, pre, tok, spot_ref, 1, chips):
        q_s[pl.ds(slot, cnt), :] = chunks[n][row : row + cnt, 0:width]
        k_s[pl.ds(slot, cnt), :] = chunks[n][row : row + cnt, width : 2 * width]
        v_s[pl.ds(slot, cnt), :] = chunks[n][row : row + cnt, 2 * width : 3 * width]
    for b in range(blocks):
        rows = slice(b * BLOCK, (b + 1) * BLOCK)
        vt_s[:, rows] = v_s[rows, :].astype(F32).T.astype(BF16)
    lane = lax.broadcasted_iota(jnp.int32, (BLOCK, width), 1) // head_dim

    def query_block(i, carry):
        qs = pl.ds(pl.multiple_of(i * BLOCK, BLOCK), BLOCK)
        q = q_s[qs, :]
        qh = [jnp.where(lane == h, q, jnp.zeros_like(q)) for h in range(heads)]
        low = low_ref[:, qs]
        high = high_ref[:, qs]
        acc_s[...] = jnp.zeros_like(acc_s)
        span = [slice(h * head_dim, (h + 1) * head_dim) for h in range(heads)]

        def key_block(j, inner):
            tops, totals = inner
            ks = pl.ds(pl.multiple_of(j * BLOCK, BLOCK), BLOCK)
            k = k_s[ks, :]
            bias = jnp.where(block_mask(place_ref[ks, :], low, high), 0.0, NEGATIVE)
            s = [contract(k, qh[h], 1, 1) + bias for h in range(heads)]
            new = [
                jnp.maximum(tops[h], jnp.max(s[h], axis=0, keepdims=True)) for h in range(heads)
            ]
            p = [jnp.exp(s[h] - new[h]) for h in range(heads)]
            alpha = [jnp.exp(tops[h] - new[h]) for h in range(heads)]
            sums = [
                totals[h] * alpha[h] + jnp.sum(p[h], axis=0, keepdims=True) for h in range(heads)
            ]
            for h in range(heads):
                share = contract(vt_s[span[h], ks], p[h].astype(BF16), 1, 0)
                acc_s[span[h], :] = acc_s[span[h], :] * alpha[h] + share
            return tuple(new), tuple(sums)

        start = (
            tuple(jnp.full((1, BLOCK), NEGATIVE, F32) for h in range(heads)),
            tuple(jnp.zeros((1, BLOCK), F32) for h in range(heads)),
        )
        start = lax.fori_loop(
            0, (i + 1) // 2, lambda j, inner: key_block(2 * j + 1, key_block(2 * j, inner)), start
        )
        tops, totals = lax.fori_loop((i + 1) // 2 * 2, i + 1, key_block, start)
        for h in range(heads):
            acc_s[span[h], :] = acc_s[span[h], :] / totals[h]
            lse_ref[h : h + 1, qs] = tops[h] + jnp.log(totals[h])
        result = acc_s[...]
        ot_ref[:, qs] = result
        q_s[qs, :] = result.T.astype(BF16)
        return carry

    lax.fori_loop(0, blocks, query_block, 0)
    for row, slot, cnt in result_pieces(devices, pre, tok, spot_ref):
        o_ref[row : row + cnt, :] = q_s[pl.ds(slot, cnt), :]


def attention_forward(chunks, spots, place, low, high, devices, pre, tok, heads, head_dim):
    width = heads * head_dim
    rows = devices * (pre + tok)
    vmem = pl.BlockSpec(memory_space=pltpu.VMEM)
    pairs = rows * rows // 2 * heads
    return pl.pallas_call(
        functools.partial(forward_kernel, devices, pre, tok, heads, head_dim),
        out_shape=(
            jax.ShapeDtypeStruct((rows, width), BF16),
            jax.ShapeDtypeStruct((width, rows), F32),
            jax.ShapeDtypeStruct((8, rows), F32),
        ),
        in_specs=[pl.BlockSpec(memory_space=pltpu.SMEM)] + [vmem] * (3 + len(chunks)),
        out_specs=(vmem,) * 3,
        scratch_shapes=[
            pltpu.VMEM((rows, width), BF16),
            pltpu.VMEM((rows, width), BF16),
            pltpu.VMEM((rows, width), BF16),
            pltpu.VMEM((width, rows), BF16),
            pltpu.VMEM((width, BLOCK), F32),
        ],
        compiler_params=pltpu.CompilerParams(vmem_limit_bytes=48 << 20),
        cost_estimate=pl.CostEstimate(
            flops=16 * pairs * head_dim, bytes_accessed=rows * width * 12, transcendentals=pairs
        ),
    )(spots, place, low, high, *chunks)


def backward_kernel(
    devices, pre, tok, heads, head_dim, first, last, carried, final, *refs
):
    chips = devices // 2
    spot_ref, ot_ref, lse_ref, place_ref, low_ref, high_ref = refs[:6]
    chunks = refs[6 : 6 + chips]
    grads = refs[6 + chips : 6 + 2 * chips]
    refs = refs[6 + 2 * chips :]
    if carried:
        dq_in, dk_in, dv_in = refs[:3]
        refs = refs[3:]
    if final:
        out_ref, near_ref = refs[:2]
        q_s, k_s, v_s, do_s, kt_s, dqt_s, dq_s, dk_s, dv_s = refs[2:]
    else:
        dq_s, dk_s, dv_s, q_s, k_s, v_s, do_s, kt_s, dqt_s = refs
    width = heads * head_dim
    scale = 1.0 / math.sqrt(head_dim)
    for n, row, slot, cnt in block_pieces(devices, pre, tok, spot_ref, 1, chips):
        q_s[pl.ds(slot, cnt), :] = chunks[n][row : row + cnt, 0:width]
        k_s[pl.ds(slot, cnt), :] = chunks[n][row : row + cnt, width : 2 * width]
        v_s[pl.ds(slot, cnt), :] = chunks[n][row : row + cnt, 2 * width : 3 * width]
    for n, row, slot, cnt in block_pieces(devices, pre, tok, spot_ref, 1 + chips, chips):
        do_s[pl.ds(slot, cnt), :] = grads[n][row : row + cnt, :]
    for b in range(last):
        rows = slice(b * BLOCK, (b + 1) * BLOCK)
        kt_s[:, rows] = k_s[rows, :].astype(F32).T.astype(BF16)
    if carried:
        dq_s[...] = dq_in[...]
        dk_s[...] = dk_in[...]
        dv_s[...] = dv_in[...]
    else:
        dk_s[...] = jnp.zeros_like(dk_s)
        dv_s[...] = jnp.zeros_like(dv_s)
    lane = lax.broadcasted_iota(jnp.int32, (BLOCK, width), 1) // head_dim

    def query_block(i, carry):
        qs = pl.ds(pl.multiple_of(i * BLOCK, BLOCK), BLOCK)
        q = q_s[qs, :]
        do = do_s[qs, :]
        qh = [jnp.where(lane == h, q, jnp.zeros_like(q)) for h in range(heads)]
        doh = [jnp.where(lane == h, do, jnp.zeros_like(do)) for h in range(heads)]
        qh_all = jnp.concatenate(qh, axis=0)
        doh_all = jnp.concatenate(doh, axis=0)
        low = low_ref[:, qs]
        high = high_ref[:, qs]
        prod = do.astype(F32).T * ot_ref[:, qs]
        delta = [
            jnp.sum(prod[h * head_dim : (h + 1) * head_dim, :], axis=0, keepdims=True)
            for h in range(heads)
        ]
        lse = [lse_ref[h : h + 1, qs] for h in range(heads)]
        dqt_s[...] = jnp.zeros_like(dqt_s)

        def key_block(j, inner):
            ks = pl.ds(pl.multiple_of(j * BLOCK, BLOCK), BLOCK)
            k = k_s[ks, :]
            v = v_s[ks, :]
            bias = jnp.where(block_mask(place_ref[ks, :], low, high), 0.0, NEGATIVE)
            s = [contract(k, qh[h], 1, 1) for h in range(heads)]
            dp = [contract(v, doh[h], 1, 1) for h in range(heads)]
            p = [jnp.exp(s[h] + (bias - lse[h])) for h in range(heads)]
            ds = [(p[h] * (dp[h] - delta[h])).astype(BF16) for h in range(heads)]
            dv = contract(jnp.concatenate([p[h].astype(BF16) for h in range(heads)], axis=1), doh_all, 1, 0)
            dk = contract(jnp.concatenate(ds, axis=1), qh_all, 1, 0)
            for h in range(heads):
                hs = slice(h * head_dim, (h + 1) * head_dim)
                dqt_s[hs, :] += contract(kt_s[hs, ks], ds[h], 1, 0)
            dk_s[ks, :] += dk
            dv_s[ks, :] += dv
            return inner

        lax.fori_loop(
            0, (i + 1) // 2, lambda j, inner: key_block(2 * j + 1, key_block(2 * j, inner)), 0
        )
        lax.fori_loop((i + 1) // 2 * 2, i + 1, key_block, 0)
        dq_s[qs, :] = (dqt_s[...] * scale).T.astype(BF16)
        return carry

    lax.fori_loop(first, last, query_block, 0)
    if final:
        for row, slot, cnt in result_pieces(devices, pre, tok, spot_ref):
            out_ref[row : row + cnt, 0:width] = dq_s[pl.ds(slot, cnt), :]
            out_ref[row : row + cnt, width : 2 * width] = dk_s[pl.ds(slot, cnt), :].astype(BF16)
            out_ref[row : row + cnt, 2 * width : 3 * width] = dv_s[pl.ds(slot, cnt), :].astype(BF16)
        both = 2 * (pre + tok)
        for n in range(chips):
            chip = pl.multiple_of(spot_ref[1 + n] * both, 16)
            near_ref[n * both : (n + 1) * both, :] = out_ref[pl.ds(chip, both), :]


def attention_backward(
    chunks, grads, spots, ot, lse, place, low, high, devices, pre, tok, heads, head_dim, first, last, carry, final
):
    width = heads * head_dim
    rows = devices * (pre + tok)
    vmem = pl.BlockSpec(memory_space=pltpu.VMEM)
    pairs = (last - first) * (last + first + 1) // 2 * BLOCK * BLOCK * heads
    low_rows = pltpu.VMEM((rows, width), BF16)
    sums = [((rows, width), BF16), ((rows, width), F32), ((rows, width), F32)]
    scratch = [
        low_rows,
        low_rows,
        low_rows,
        low_rows,
        pltpu.VMEM((width, rows), BF16),
        pltpu.VMEM((width, BLOCK), F32),
    ]
    if final:
        out_shape = (jax.ShapeDtypeStruct((rows, 3 * width), BF16),) * 2
        scratch += [pltpu.VMEM(shape, dtype) for shape, dtype in sums]
    else:
        out_shape = tuple(jax.ShapeDtypeStruct(shape, dtype) for shape, dtype in sums)
    return pl.pallas_call(
        functools.partial(
            backward_kernel, devices, pre, tok, heads, head_dim, first, last, bool(carry), final
        ),
        out_shape=out_shape,
        in_specs=[pl.BlockSpec(memory_space=pltpu.SMEM)]
        + [vmem] * (5 + len(chunks) + len(grads) + len(carry)),
        out_specs=(vmem,) * len(out_shape),
        scratch_shapes=scratch,
        compiler_params=pltpu.CompilerParams(vmem_limit_bytes=58 << 20),
        cost_estimate=pl.CostEstimate(
            flops=20 * pairs * head_dim, bytes_accessed=rows * width * 20, transcendentals=pairs
        ),
    )(spots, ot, lse, place, low, high, *chunks, *grads, *carry)


def matmul_kernel(flipped, left_ref, right_ref, out_ref):
    out_ref[...] = contract(left_ref[...], right_ref[...], 1, 1 if flipped else 0).astype(BF16)


def matmul_low(left, right, flipped):
    rows, depth = left.shape
    columns = right.shape[0] if flipped else right.shape[1]
    step = 512
    block = (step, depth) if flipped else (depth, step)
    return pl.pallas_call(
        functools.partial(matmul_kernel, flipped),
        grid=(columns // step,),
        out_shape=jax.ShapeDtypeStruct((rows, columns), BF16),
        in_specs=[
            pl.BlockSpec((rows, depth), lambda n: (0, 0)),
            pl.BlockSpec(block, (lambda n: (n, 0)) if flipped else (lambda n: (0, n))),
        ],
        out_specs=pl.BlockSpec((rows, step), lambda n: (0, n)),
        compiler_params=pltpu.CompilerParams(vmem_limit_bytes=48 << 20),
        cost_estimate=pl.CostEstimate(flops=1 << 20, bytes_accessed=1 << 16, transcendentals=0),
    )(left, right)


def transposed_kernel(left_ref, right_ref, out_ref):
    out_ref[...] = contract(left_ref[...], right_ref[...], 0, 0).astype(BF16)


def matmul_transposed(left, right):
    depth, rows = left.shape
    columns = right.shape[1]
    step = 512
    return pl.pallas_call(
        transposed_kernel,
        grid=(rows // step,),
        out_shape=jax.ShapeDtypeStruct((rows, columns), BF16),
        in_specs=[
            pl.BlockSpec((depth, step), lambda n: (0, n)),
            pl.BlockSpec((depth, columns), lambda n: (0, 0)),
        ],
        out_specs=pl.BlockSpec((step, columns), lambda n: (n, 0)),
        compiler_params=pltpu.CompilerParams(vmem_limit_bytes=56 << 20),
        cost_estimate=pl.CostEstimate(flops=1 << 20, bytes_accessed=1 << 16, transcendentals=0),
    )(left, right)


def rows_product_kernel(*refs):
    chunks, right_ref, out_ref = refs[:-2], refs[-2], refs[-1]
    rows = chunks[0].shape[0]
    total = contract(chunks[0][...], right_ref[0:rows, :], 0, 0)
    for n in range(1, len(chunks)):
        total += contract(chunks[n][...], right_ref[n * rows : (n + 1) * rows, :], 0, 0)
    out_ref[...] = total.astype(BF16)


def rows_product(chunks, right):
    rows, columns = chunks[0].shape
    step = 512
    return pl.pallas_call(
        rows_product_kernel,
        grid=(columns // step,),
        out_shape=jax.ShapeDtypeStruct((columns, right.shape[1]), BF16),
        in_specs=[pl.BlockSpec((rows, step), lambda n: (0, n))] * len(chunks)
        + [pl.BlockSpec(right.shape, lambda n: (0, 0))],
        out_specs=pl.BlockSpec((step, right.shape[1]), lambda n: (n, 0)),
        compiler_params=pltpu.CompilerParams(vmem_limit_bytes=56 << 20),
        cost_estimate=pl.CostEstimate(
            flops=right.shape[0] * columns * right.shape[1] // 2, bytes_accessed=1 << 16, transcendentals=0
        ),
    )(*chunks, right)


def slot_labels(lengths, devices, pre, tok, real):
    slot = jnp.arange(devices * pre, dtype=jnp.int32)
    inside = slot % pre
    place = (slot // pre) * real + inside - devices * real
    is_real = inside < real
    t = jnp.arange(devices * tok, dtype=jnp.int32)
    ends = jnp.cumsum(lengths)
    start = jnp.max(jnp.where(ends[None, :] <= t[:, None], ends[None, :], 0), axis=1)
    places = jnp.concatenate([jnp.where(is_real, place, FAR), t])
    high = jnp.concatenate([jnp.where(is_real, place, -1), t])
    low = jnp.concatenate([jnp.full((devices * pre,), FAR, jnp.int32), start])
    return places[:, None], low[None, :], high[None, :]


def normalize(values):
    center = values - jnp.mean(values, axis=-1, keepdims=True)
    spread = jnp.mean(center * center, axis=-1, keepdims=True)
    inverse = lax.rsqrt(spread + EPS)
    return center * inverse, inverse


def norm_backward(grad, hat, inverse, gain):
    e = grad * gain
    mean_e = jnp.mean(e, axis=-1, keepdims=True)
    mean_eh = jnp.mean(e * hat, axis=-1, keepdims=True)
    return inverse * (e - mean_e - hat * mean_eh)


def gelu_parts(values):
    cdf = 0.5 * (1.0 + lax.erf(values * (1.0 / math.sqrt(2.0))))
    return cdf


def pick(array, index, axis):
    return lax.dynamic_index_in_dim(array, index, axis, keepdims=False)


def build(n_batch, n_seq):
    n_z = n_seq // 2
    n_dev = n_batch * n_seq
    groups = n_dev // 4
    size_of = {"batch": n_batch, "seq": n_seq}

    def bits_of(n):
        bits = []
        bit = 1
        while bit < n:
            bits.append(bit)
            bit *= 2
        return bits

    core = ("seq", 1)
    near = ("seq", 2)
    up_batch = [("batch", bit) for bit in bits_of(n_batch)]
    down_batch = list(reversed(up_batch))
    far_bits = [("seq", bit) for bit in bits_of(n_seq) if bit >= 4]
    chip_bits = [near] + far_bits
    group_bits = down_batch + list(reversed(far_bits))
    all_bits = down_batch + [("seq", bit) for bit in reversed(bits_of(n_seq))]

    def swap_pairs(which):
        axis, bit = which
        return axis, [(i, i ^ bit) for i in range(size_of[axis])]

    def shift_pairs(distance):
        return "seq", [
            (z * 2 + c, ((z + distance) % n_z) * 2 + c) for z in range(n_z) for c in range(2)
        ]

    def right_pairs(first, last):
        return "seq", [(z * 2 + c, z * 2 + 2 + c) for z in range(first, last) for c in range(2)]

    def left_pairs(first, last):
        return "seq", [(z * 2 + c, z * 2 - 2 + c) for z in range(first, last) for c in range(2)]

    def side(which):
        axis, bit = which
        return (lax.axis_index(axis) // bit) % 2

    def permute(array, pairs):
        return lax.ppermute(array, pairs[0], pairs[1])

    class Clock:
        def __init__(self):
            self.gate = ()

        def hold(self, *arrays):
            if self.gate:
                arrays = lax.optimization_barrier(tuple(arrays) + tuple(self.gate))[: len(arrays)]
            return arrays[0] if len(arrays) == 1 else arrays

        def tick(self, *arrays):
            self.gate = arrays

    def join(mine, other, which, axis):
        first = side(which) == 0
        return jnp.where(first, jnp.stack([mine, other], axis), jnp.stack([other, mine], axis))

    def body(
        tokens, prefix, seg_lengths, attn_gain, attn_shift, query_weight, key_weight, value_weight,
        query_bias, value_bias, output_weight, output_bias, mlp_gain, mlp_shift, up_weight, up_bias,
        down_weight, down_bias, cot_tokens, cot_prefix,
    ):
        clock = Clock()

        def swap(array, which):
            return permute(array, swap_pairs(which))

        def gather_bits(array, order, ranked):
            taken = []
            current = array
            for which in order:
                other = swap(current, which)
                rank = ranked.index(which)
                place = sum(1 for t in taken if ranked.index(t) < rank)
                current = join(current, other, which, place)
                taken.append(which)
            return current.reshape((2 ** len(order),) + array.shape)

        def part_of(current, left, which, mine):
            return pick(current, side(which) if mine else 1 - side(which), left.index(which))

        def hop_scatter(current, left, which, last):
            other = swap(part_of(current, left, which, False).astype(BF16), which)
            total = part_of(current, left, which, True).astype(F32) + other.astype(F32)
            rest = [b for b in left if b != which]
            return (total if last else total.astype(BF16)), rest

        tok = tokens.shape[1]
        real = prefix.shape[1]
        pre = -(-real // 16) * 16
        width = pre + tok
        model = tokens.shape[2]
        heads = HEADS // n_seq
        span = heads * HEAD_DIM
        part = model // n_dev
        unit = up_bias.shape[0]
        hidden_here = groups * unit
        s_here = lax.axis_index("seq")
        z_here = s_here // 2
        c_here = s_here % 2
        near_here = side(near)
        lengths = seg_lengths[0]

        def rows_of(pre_part, tok_part):
            return jnp.concatenate([jnp.pad(pre_part, ((0, pre - real), (0, 0))), tok_part], axis=0)

        def device_rows(array, z, c):
            return lax.dynamic_slice_in_dim(array, (z * 2 + c) * width, width, 0)

        own = rows_of(prefix[0], tokens[0])
        row = jnp.arange(width, dtype=jnp.int32)
        position = row - pre + s_here * tok
        valid = jnp.where(row < pre, row < real, position < jnp.sum(lengths))
        validity = valid.astype(F32)[:, None]

        far_group = list(reversed(far_bits))
        n_far = groups // n_batch
        far_here = s_here // 4

        def afar(array, mask):
            return permute(array, ("seq", [(i, i ^ (mask * 4)) for i in range(n_seq)]))

        def batch_gather(array):
            return lax.all_gather(array, "batch", axis=0, tiled=True)

        def batch_sum(array):
            return lax.psum_scatter(array, "batch", scatter_dimension=0, tiled=True)

        def set_far(whole, blocks, index):
            blocks = blocks.reshape((n_batch, 1, -1) + blocks.shape[1:])
            return lax.dynamic_update_slice_in_dim(whole, blocks, index, 1)

        steps = [(permute(own, right_pairs(0, n_z - 1)), permute(own, left_pairs(1, n_z)))]
        small = jnp.concatenate(
            [attn_gain, attn_shift, query_bias, value_bias, output_bias, mlp_gain, mlp_shift, down_bias, up_bias]
        )
        small_bits = down_batch + [core]
        small = gather_bits(small, list(reversed(small_bits)), small_bits)
        down_gate, unused = lax.optimization_barrier((down_weight, small))
        down_own = batch_gather(down_gate)

        stacked = jnp.stack([query_weight, key_weight, value_weight], axis=1)
        stacked = stacked.reshape(part, 3, heads, n_z, 2, HEAD_DIM).transpose(3, 4, 0, 1, 2, 5)
        stacked = stacked.reshape(n_z, 2, part, 3 * span)
        mixed = join(pick(stacked, c_here, 1), swap(pick(stacked, 1 - c_here, 1), core), core, 1)
        mixed = mixed.reshape(n_z, 2 * part, 3 * span)
        flat = small.reshape(-1)
        small_rows = -(-flat.shape[0] // (3 * span * 16)) * 16
        flat = jnp.pad(flat, (0, small_rows * 3 * span - flat.shape[0]))
        flat = jnp.broadcast_to(flat.reshape(1, small_rows, 3 * span), (n_z, small_rows, 3 * span))
        mixed = jnp.concatenate([mixed, flat], axis=1)

        up_near = up_weight.reshape(part, groups, 2, 2, unit)
        up_near = join(pick(up_near, c_here, 3), swap(pick(up_near, 1 - c_here, 3), core), core, 0)

        clock.tick(*steps[0], up_near)

        def shift_out(choose):
            pieces = [choose((z_here + d) % n_z) for d in range(1, n_z)]
            pieces = clock.hold(*pieces) if len(pieces) > 1 else [clock.hold(*pieces)]
            got = [permute(piece, shift_pairs(d + 1)) for d, piece in enumerate(pieces)]
            return [(z_here, choose(z_here))] + [
                ((z_here - d - 1) % n_z, piece) for d, piece in enumerate(got)
            ]

        placed = shift_out(lambda z: pick(mixed, z, 0))
        ranked_o = far_group + [near]
        up_other = swap(clock.hold(pick(up_near, 1 - near_here, 3)), near)
        gathered_o = gather_bits(clock.hold(output_weight), far_bits, far_group)
        clock.tick(up_other, gathered_o, *[piece for unused, piece in placed[1:]])
        up_block = join(pick(up_near, near_here, 3), up_other, near, 0)
        up_block = up_block.reshape(4 * part, hidden_here)
        local = jnp.zeros((n_z, 2 * part, 3 * span), BF16)
        small_z = jnp.zeros((n_z, small_rows, 3 * span), BF16)
        for z, piece in placed:
            local = lax.dynamic_update_slice_in_dim(local, piece[None, : 2 * part], z, 0)
            small_z = lax.dynamic_update_slice_in_dim(small_z, piece[None, 2 * part :], z, 0)
        local, unused = lax.optimization_barrier((local, down_own))
        weight_qkv = batch_gather(local.reshape(n_z * 2 * part, 3 * span))
        small = small_z.reshape(n_z, -1)[:, : n_batch * 2 * (8 * part + unit)]
        small = small.reshape(n_z, n_batch, 2, 8 * part + unit).transpose(1, 0, 2, 3)
        small = small.reshape(n_dev, 8 * part + unit)
        vectors = [small[:, n * part : (n + 1) * part].reshape(model).astype(F32) for n in range(8)]
        gain_a, shift_a, bias_q, bias_v, bias_o, gain_m, shift_m, bias_down = vectors
        bias_up = pick(small[:, 8 * part :].reshape(groups, 4, unit), s_here % 4, 1)
        bias_up = bias_up.reshape(hidden_here).astype(F32)

        bias_qkv = jnp.concatenate(
            [
                pick(bias_q.reshape(heads, n_seq, HEAD_DIM), s_here, 1).reshape(span),
                jnp.zeros((span,), F32),
                pick(bias_v.reshape(heads, n_seq, HEAD_DIM), s_here, 1).reshape(span),
            ]
        )
        factor = jnp.concatenate(
            [jnp.full((span,), 1.0 / math.sqrt(HEAD_DIM), F32), jnp.ones((2 * span,), F32)]
        )

        def source(n):
            if n == 0:
                return z_here
            short = jnp.minimum(z_here, n_z - 1 - z_here)
            both = n <= 2 * short
            distance = jnp.where(both, (n + 1) // 2, n - short)
            left = jnp.where(both, n % 2 == 1, 2 * z_here >= n_z)
            return jnp.where(left, z_here - distance, z_here + distance)

        def rows_from(n):
            rows = own
            for d in range((n + 1) // 2, n + 1) if n else ():
                right, left = steps[d - 1]
                rows = jnp.where(source(n) == z_here - d, right, rows)
                rows = jnp.where(source(n) == z_here + d, left, rows)
            rows = jnp.concatenate([rows, swap(rows, core)], axis=0)
            hat, unused = normalize(rows.astype(F32))
            return (hat * gain_a + shift_a).astype(BF16)

        def qkv_of(rows):
            result = (contract(rows, weight_qkv, 1, 0) + bias_qkv).astype(BF16).astype(F32) * factor
            return result.astype(BF16)

        exact = part == HEAD_DIM and heads == n_batch
        normed = []
        for k in range(2, n_z):
            right, left = clock.hold(*steps[-1])
            steps.append(
                (permute(right, right_pairs(k - 1, n_z - 1)), permute(left, left_pairs(1, n_z - k + 1)))
            )
            normed.append(rows_from(k - 2))
            clock.tick(*steps[-1], normed[-1])
        up_gate, unused = lax.optimization_barrier((up_block, weight_qkv))
        up_own = batch_gather(up_gate)

        other = swap(clock.hold(gathered_o), near)
        gathered_o = join(gathered_o, other, near, 1)
        gathered_o, unused = lax.optimization_barrier((gathered_o, up_own))
        gathered_o = batch_gather(gathered_o.reshape(n_z * part, model))

        weight_o = gathered_o.reshape(n_batch, n_z, part, model)
        if exact:
            weight_o = weight_o.transpose(1, 0, 2, 3).reshape(n_z * span, model)
        else:
            weight_o = join(weight_o, swap(weight_o, core), core, 2)
            weight_o = weight_o.reshape(heads, n_z, 2, HEAD_DIM, model)
            weight_o = pick(weight_o, c_here, 2).transpose(1, 0, 2, 3).reshape(n_z * span, model)

        qkv = []
        for n in range(n_z):
            if n >= n_z - 2:
                normed.append(rows_from(n))
            qkv.append(qkv_of(normed[n]))
        shifted = [z_here] + [(z_here - d) % n_z for d in range(1, n_z)]
        spots = jnp.stack([c_here] + [source(n) for n in range(n_z)] + shifted).astype(jnp.int32)

        cot_rows = rows_of(cot_prefix[0], cot_tokens[0]).astype(F32)
        mlp_out_grad = (validity * cot_rows).astype(BF16)
        places, low, high = slot_labels(lengths, n_seq, pre, tok, real)
        clock.tick(other)
        *qkv, up_gate, grad_gate = clock.hold(*qkv, up_block, mlp_out_grad)
        up_far = [afar(up_gate, mask) for mask in range(1, n_far)]
        grad_far = swap(grad_gate, near)
        attended, attended_t, log_total = attention_forward(
            qkv, spots, places, low, high, n_seq, pre, tok, heads, HEAD_DIM
        )
        clock.tick(attended, grad_far, *up_far)
        up_blocks = [batch_gather(clock.hold(piece)) for piece in up_far]

        blocks = attended.reshape(n_z, 2 * width, span)
        placed = shift_out(lambda z: pick(blocks, z, 0))
        *normed, up_own, down_own, unused = lax.optimization_barrier(
            tuple(normed) + (up_own, down_own, attended)
        )
        weight_up = set_far(
            jnp.zeros((n_batch, n_far, 4 * part, hidden_here), BF16), up_own, far_here
        )
        weight_down = set_far(
            jnp.zeros((n_batch, n_far, unit, model), BF16), down_own, far_here
        )
        grad_rows = jnp.concatenate(
            [mlp_out_grad, swap(mlp_out_grad, core), grad_far, swap(grad_far, core)], axis=0
        )
        spread_o = [piece for unused, piece in placed[1:]]
        *spread_o, weight_up, weight_down, weight_o = lax.optimization_barrier(
            (*spread_o, weight_up, weight_down, weight_o)
        )
        placed = [placed[0]] + [(z, piece) for (z, unused), piece in zip(placed[1:], spread_o)]
        mixed_low = jnp.zeros((2 * width, n_z * span), BF16)
        for z, piece in placed:
            mixed_low = lax.dynamic_update_slice_in_dim(mixed_low, piece, z * span, 1)
        clock.tick(mixed_low, weight_up, weight_down)
        down_far = [afar(clock.hold(down_weight), mask) for mask in range(1, n_far)]
        mixed_held = clock.hold(mixed_low)
        branch_away = contract(mixed_held[width:], weight_o, 1, 0).astype(BF16)
        branch_away = swap(branch_away, core)
        branch = contract(mixed_held[:width], weight_o, 1, 0) + branch_away.astype(F32) + bias_o
        rows_in = own.astype(F32)
        resid = rows_in + validity * branch
        hat_m, inverse_m = normalize(resid)
        normed_own = (hat_m * gain_m + shift_m).astype(BF16)

        normed_near = swap(normed_own, core)
        normed_far = swap(normed_own, near)
        *down_far, unused = lax.optimization_barrier(tuple(down_far) + (normed_own,))
        down_blocks = [batch_gather(piece) for piece in down_far]
        *up_blocks, unused = lax.optimization_barrier(tuple(up_blocks) + (normed_own,))
        for mask, piece in enumerate(up_blocks):
            weight_up = set_far(weight_up, piece, far_here ^ (mask + 1))
        weight_up = weight_up.reshape(model, hidden_here)
        normed_far, weight_up = lax.optimization_barrier((normed_far, weight_up))
        normed_parts = [normed_own, normed_near, normed_far, swap(normed_far, core)]
        normed_rows = jnp.concatenate(normed_parts, axis=0)

        before = contract(normed_rows, weight_up, 1, 0) + bias_up
        cdf = 0.5 * (1.0 + lax.erf(before * (1.0 / math.sqrt(2.0))))
        hidden = (before * cdf).astype(BF16)
        slope = cdf + before * jnp.exp(-0.5 * before * before) * (1.0 / math.sqrt(2.0 * math.pi))
        *down_blocks, unused = lax.optimization_barrier(tuple(down_blocks) + (hidden,))
        for mask, piece in enumerate(down_blocks):
            weight_down = set_far(weight_down, piece, far_here ^ (mask + 1))
        weight_down = weight_down.reshape(hidden_here, model)
        grad_down = contract(hidden, grad_rows, 0, 0).astype(BF16)
        grad_down, grad_held = lax.optimization_barrier((grad_down, grad_rows))
        grad_down = batch_sum(grad_down)
        hidden_grad = contract(grad_held, weight_down, 1, 1)
        pre_grad = (hidden_grad * slope).astype(BF16)

        share_f = contract(pre_grad[2 * width :], weight_up, 1, 1).astype(BF16)
        back = swap(share_f[width:], core)
        back = (share_f[:width].astype(F32) + back.astype(F32)).astype(BF16)
        pre_held, hidden_held, back_held = lax.optimization_barrier((pre_grad, hidden, back))
        back = swap(back_held, near)
        share_n = matmul_low(pre_held[: 2 * width], weight_up, True)
        out_share = matmul_low(hidden_held, weight_down, False)
        *normed_late, unused = lax.optimization_barrier((*normed_parts, back_held))
        normed_late = jnp.concatenate(normed_late, axis=0)
        back, out_share, share_n, normed_late = lax.optimization_barrier(
            (back, out_share, share_n, normed_late)
        )
        here = swap(share_n[width:], core)
        normed_grad = share_n[:width].astype(F32) + here.astype(F32) + back.astype(F32)

        grad_up_bias = jnp.sum(pre_grad.astype(F32), axis=0)
        grad_down_bias = jnp.sum(mlp_out_grad.astype(F32), axis=0)
        grad_gain_m = jnp.sum(normed_grad * hat_m, axis=0)
        grad_shift_m = jnp.sum(normed_grad, axis=0)
        resid_grad = cot_rows + norm_backward(normed_grad, hat_m, inverse_m, gain_m)

        branch_grad = (validity * resid_grad).astype(BF16)
        grad_out_bias = jnp.sum(branch_grad.astype(F32), axis=0)
        branch_grad = jnp.concatenate([branch_grad, swap(branch_grad, core)], axis=0)
        mixed_grad = contract(branch_grad, weight_o, 1, 1).astype(BF16)
        clock.tick(mixed_grad)
        placed = shift_out(lambda z: lax.dynamic_slice_in_dim(mixed_grad, z * span, span, 1))
        grad_gate, branch_gate, mixed_gate, unused = lax.optimization_barrier(
            (pre_grad, branch_grad, mixed_low, mixed_grad)
        )
        grad_up = matmul_transposed(normed_late, grad_gate)
        grad_out = matmul_transposed(mixed_gate, branch_gate)
        if exact:
            grad_out = grad_out.reshape(n_z, n_batch, part, model).transpose(1, 0, 2, 3)
        else:
            full = jnp.zeros((heads, n_z, 2, HEAD_DIM, model), BF16)
            grad_out = grad_out.reshape(n_z, heads, 1, HEAD_DIM, model).transpose(1, 0, 2, 3, 4)
            grad_out = lax.dynamic_update_slice_in_dim(full, grad_out, c_here, 2)
            grad_out = grad_out.reshape(n_batch, n_z, 2, part, model)
            grad_out = pick(grad_out, c_here, 2).astype(F32) + swap(
                pick(grad_out, 1 - c_here, 2), core
            ).astype(F32)
            grad_out = grad_out.astype(BF16)
        rows_grad = [piece for unused, piece in placed]
        out_back = swap(out_share[3 * width :], core)
        out_back = (out_share[2 * width : 3 * width].astype(F32) + out_back.astype(F32)).astype(BF16)
        grad_up, grad_out, out_back, *rows_grad = lax.optimization_barrier(
            (grad_up, grad_out, out_back, *rows_grad)
        )
        grad_up = batch_sum(grad_up)
        grad_out = batch_sum(grad_out.reshape(n_batch * n_z * part, model))

        clock.tick(*rows_grad, grad_down, out_share)
        down_gate, out_away, *rows_grad = clock.hold(grad_down, out_back, *rows_grad)
        down_sum = down_gate.reshape((2,) * len(far_bits) + (unit, model))
        rest_down = list(far_group)
        for n, which in enumerate(far_bits):
            down_sum, rest_down = hop_scatter(
                down_sum, rest_down, which, n == len(far_bits) - 1
            )
        grad_down = down_sum
        out_back = swap(out_away, near)
        blocks = n_seq * width // BLOCK
        qkv_grad, relative = attention_backward(
            qkv, rows_grad, spots, attended_t, log_total, places, low, high,
            n_seq, pre, tok, heads, HEAD_DIM, 0, blocks, (), True,
        )
        qkv_grad, relative, grad_down, out_back = lax.optimization_barrier(
            (qkv_grad, relative, grad_down, out_back)
        )
        clock.tick(qkv_grad, grad_down, out_back)

        chunks = [None] * n_z
        aways = []
        order = []
        for k in range(1, n_z):
            for r in (n_z - k, k):
                if r not in order:
                    order.append(r)
        for r in order + [0]:
            z = (z_here + r) % n_z
            away = contract(device_rows(qkv_grad, z, 1), weight_qkv, 1, 1).astype(BF16)
            away = swap(away, core)
            aways.append(away)
            keep = contract(device_rows(qkv_grad, z, 0), weight_qkv, 1, 1)
            chunks[r] = keep + away.astype(F32)
        right = None
        left = None
        for k in range(1, n_z):
            going_r = jnp.where(z_here + n_z - k < n_z, chunks[n_z - k], 0.0)
            going_l = jnp.where(z_here - (n_z - k) >= 0, chunks[k], 0.0)
            if k > 1:
                going_r = going_r + right.astype(F32)
                going_l = going_l + left.astype(F32)
            going_r, going_l = clock.hold(going_r.astype(BF16), going_l.astype(BF16))
            right = permute(going_r, right_pairs(0, k))
            left = permute(going_l, left_pairs(n_z - k, n_z))
            started = [right, left]
            if k == 1:
                up_sum = clock.hold(grad_up).reshape((2,) * len(far_bits) + (4 * part, hidden_here))
                rest_up = list(far_group)
                for which in far_bits:
                    up_sum, rest_up = hop_scatter(up_sum, rest_up, which, False)
                relative, unused = lax.optimization_barrier((relative, going_r))
                grad_qkv = rows_product(normed, relative)
                grad_qkv, right, left, up_sum, grad_out, unused = lax.optimization_barrier(
                    (grad_qkv, right, left, up_sum, grad_out, tuple(aways[2:]))
                )
                grad_qkv = batch_sum(grad_qkv)
                started = [right, left, up_sum]
            if k == 2:
                grad_up = up_sum.reshape(2, 2, part, hidden_here)
                up_other = swap(clock.hold(pick(grad_up, 1 - near_here, 0)), near)
                grad_up = join(pick(grad_up, near_here, 0), up_other, near, 0)
                rest_o = list(ranked_o)
                grad_out = clock.hold(grad_out).reshape((2,) * len(ranked_o) + (part, model))
                grad_out, rest_o = hop_scatter(grad_out, rest_o, near, False)
                started += [up_other, grad_out]
            if k == n_z - 1:
                grad_qkv = grad_qkv.reshape(n_z, 2, part, 3 * span)
                grad_qkv = join(
                    pick(grad_qkv, c_here, 1), swap(pick(grad_qkv, 1 - c_here, 1), core), core, 1
                )
                placed = shift_out(lambda z: pick(grad_qkv, z, 0))
                out_share, out_back, grads_late = clock.hold(out_share, out_back, qkv_grad)
                out_here = swap(out_share[width : 2 * width], core)
                final = out_share[:width].astype(F32) + out_here.astype(F32) + out_back.astype(F32)
                final = resid + validity * (final + bias_down)
                out_rows = final.astype(BF16)
                bias_sums = jnp.sum(grads_late.astype(F32), axis=0)
                grad_out = clock.hold(grad_out)
                for n, which in enumerate(far_bits):
                    grad_out, rest_o = hop_scatter(grad_out, rest_o, which, n == len(far_bits) - 1)
            clock.tick(*started)
        right, left, unused = lax.optimization_barrier(
            (right, left, (out_rows, bias_sums, *[piece for unused, piece in placed[1:]]))
        )
        normed_back = chunks[0] + right.astype(F32) + left.astype(F32)

        grad_up = join(pick(grad_up, c_here, 1), swap(pick(grad_up, 1 - c_here, 1), core), core, 1)
        grad_up = grad_up.reshape(4, part, groups, unit).transpose(1, 2, 0, 3)
        grad_up = grad_up.reshape(part, n_dev * unit).astype(F32)


        shares = jnp.zeros((n_z, 2, part, 3 * span), BF16)
        for z, piece in placed:
            shares = lax.dynamic_update_slice_in_dim(shares, piece[None], z, 0)
        shares = shares.reshape(n_seq, part, 3, heads, HEAD_DIM)
        shares = [
            shares[:, :, n].transpose(1, 2, 0, 3).reshape(part, model).astype(F32) for n in range(3)
        ]

        hat_a, inverse_a = normalize(rows_in)
        grad_gain_a = jnp.sum(normed_back * hat_a, axis=0)
        grad_shift_a = jnp.sum(normed_back, axis=0)
        input_grad = resid_grad + norm_backward(normed_back, hat_a, inverse_a, gain_a)

        zero = jnp.zeros((heads, n_seq, HEAD_DIM), F32)

        def spread(sums):
            sums = sums.reshape(heads, 1, HEAD_DIM)
            return lax.dynamic_update_slice_in_dim(zero, sums, s_here, 1).reshape(model)

        full_up_bias = lax.dynamic_update_slice_in_dim(
            jnp.zeros((groups, 4, unit), F32), grad_up_bias.reshape(groups, 1, unit), s_here % 4, 1
        ).reshape(n_dev, unit)
        sums = jnp.concatenate(
            [
                vector.reshape(n_dev, part)
                for vector in (
                    grad_gain_a, grad_shift_a, spread(bias_sums[:span]), spread(bias_sums[2 * span :]),
                    grad_out_bias, grad_gain_m, grad_shift_m, grad_down_bias,
                )
            ]
            + [full_up_bias],
            axis=1,
        )
        sums, unused = lax.optimization_barrier((sums, tuple(shares)))
        current = jnp.sum(lax.all_to_all(sums, ("batch", "seq"), 0, 0, tiled=True), axis=0)
        small_grads = [current[n * part : (n + 1) * part] for n in range(8)]

        return (
            out_rows[pre:][None],
            out_rows[:real][None],
            input_grad[pre:][None],
            input_grad[:real][None],
            small_grads[0],
            small_grads[1],
            shares[0],
            shares[1],
            shares[2],
            small_grads[2],
            small_grads[3],
            grad_out,
            small_grads[4],
            small_grads[5],
            small_grads[6],
            grad_up,
            current[8 * part :],
            grad_down,
            small_grads[7],
        )

    return body


def solution(mesh):
    rows = P("batch", "seq", None)
    vector = P(("batch", "seq"))
    matrix = P(("batch", "seq"), None)
    return jax.shard_map(
        build(mesh.shape["batch"], mesh.shape["seq"]),
        mesh=mesh,
        in_specs=(
            rows, rows, P("batch", None), vector, vector, matrix, matrix, matrix, vector, vector,
            matrix, vector, vector, vector, matrix, vector, matrix, vector, rows, rows,
        ),
        out_specs=(
            rows, rows, rows, rows, vector, vector, matrix, matrix, matrix, vector, vector, matrix,
            vector, vector, vector, matrix, vector, matrix, vector,
        ),
        check_vma=False,
    )
```

```python
import functools
import math

import jax
import jax.numpy as jnp
from jax import lax
from jax.experimental import pallas as pl
from jax.experimental.pallas import tpu as pltpu
from jax.sharding import PartitionSpec as P

HEADS = 32
HEAD_DIM = 64
EPS = 1e-05
NEGATIVE = -1e30
FAR = 1 << 20
BLOCK = 256
BF16 = jnp.bfloat16
F32 = jnp.float32


def contract(left, right, left_dim, right_dim):
    return lax.dot_general(
        left, right, (((left_dim,), (right_dim,)), ((), ())), preferred_element_type=F32
    )


def slot_pieces(devices, pre, tok, device):
    if isinstance(device, int):
        return [(0, device * pre, pre), (pre, devices * pre + device * tok, tok)]
    return [
        (0, pl.multiple_of(device * pre, 16), pre),
        (pre, pl.multiple_of(devices * pre + device * tok, 16), tok),
    ]


def block_pieces(devices, pre, tok, place_ref, first, blocks):
    pieces = []
    for n in range(blocks):
        for i in range(2):
            core = place_ref[0] if i == 0 else 1 - place_ref[0]
            device = place_ref[first + n] * 2 + core
            for row, slot, count in slot_pieces(devices, pre, tok, device):
                pieces.append((n, i * (pre + tok) + row, slot, count))
    return pieces


def result_pieces(devices, pre, tok, place_ref):
    pieces = []
    for z in range(devices // 2):
        for i in range(2):
            core = place_ref[0] if i == 0 else 1 - place_ref[0]
            for row, slot, count in slot_pieces(devices, pre, tok, z * 2 + core):
                pieces.append(((z * 2 + i) * (pre + tok) + row, slot, count))
    return pieces


def block_mask(place, low, high):
    return (place <= high) & ((place >= low) | (place < 0))


def forward_kernel(devices, pre, tok, heads, head_dim, *refs):
    chips = devices // 2
    spot_ref, place_ref, low_ref, high_ref = refs[:4]
    chunks = refs[4 : 4 + chips]
    o_ref, ot_ref, lse_ref, q_s, k_s, v_s, vt_s, acc_s = refs[4 + chips :]
    width = heads * head_dim
    blocks = devices * (pre + tok) // BLOCK
    for n, row, slot, cnt in block_pieces(devices, pre, tok, spot_ref, 1, chips):
        q_s[pl.ds(slot, cnt), :] = chunks[n][row : row + cnt, 0:width]
        k_s[pl.ds(slot, cnt), :] = chunks[n][row : row + cnt, width : 2 * width]
        v_s[pl.ds(slot, cnt), :] = chunks[n][row : row + cnt, 2 * width : 3 * width]
    for b in range(blocks):
        rows = slice(b * BLOCK, (b + 1) * BLOCK)
        vt_s[:, rows] = v_s[rows, :].astype(F32).T.astype(BF16)
    lane = lax.broadcasted_iota(jnp.int32, (BLOCK, width), 1) // head_dim

    def query_block(i, carry):
        qs = pl.ds(pl.multiple_of(i * BLOCK, BLOCK), BLOCK)
        q = q_s[qs, :]
        qh = [jnp.where(lane == h, q, jnp.zeros_like(q)) for h in range(heads)]
        low = low_ref[:, qs]
        high = high_ref[:, qs]
        acc_s[...] = jnp.zeros_like(acc_s)
        span = [slice(h * head_dim, (h + 1) * head_dim) for h in range(heads)]

        def key_block(j, inner):
            tops, totals = inner
            ks = pl.ds(pl.multiple_of(j * BLOCK, BLOCK), BLOCK)
            k = k_s[ks, :]
            bias = jnp.where(block_mask(place_ref[ks, :], low, high), 0.0, NEGATIVE)
            s = [contract(k, qh[h], 1, 1) + bias for h in range(heads)]
            new = [
                jnp.maximum(tops[h], jnp.max(s[h], axis=0, keepdims=True)) for h in range(heads)
            ]
            p = [jnp.exp(s[h] - new[h]) for h in range(heads)]
            alpha = [jnp.exp(tops[h] - new[h]) for h in range(heads)]
            sums = [
                totals[h] * alpha[h] + jnp.sum(p[h], axis=0, keepdims=True) for h in range(heads)
            ]
            for h in range(heads):
                share = contract(vt_s[span[h], ks], p[h].astype(BF16), 1, 0)
                acc_s[span[h], :] = acc_s[span[h], :] * alpha[h] + share
            return tuple(new), tuple(sums)

        start = (
            tuple(jnp.full((1, BLOCK), NEGATIVE, F32) for h in range(heads)),
            tuple(jnp.zeros((1, BLOCK), F32) for h in range(heads)),
        )
        start = lax.fori_loop(
            0, (i + 1) // 4, lambda j, inner: key_block(4 * j + 3, key_block(4 * j + 2, key_block(4 * j + 1, key_block(4 * j, inner)))), start
        )
        tops, totals = lax.fori_loop((i + 1) // 4 * 4, i + 1, key_block, start)
        for h in range(heads):
            acc_s[span[h], :] = acc_s[span[h], :] / totals[h]
            lse_ref[h : h + 1, qs] = tops[h] + jnp.log(totals[h])
        result = acc_s[...]
        ot_ref[:, qs] = result
        q_s[qs, :] = result.T.astype(BF16)
        return carry

    lax.fori_loop(0, blocks, query_block, 0)
    for row, slot, cnt in result_pieces(devices, pre, tok, spot_ref):
        o_ref[row : row + cnt, :] = q_s[pl.ds(slot, cnt), :]


def attention_forward(chunks, spots, place, low, high, devices, pre, tok, heads, head_dim):
    width = heads * head_dim
    rows = devices * (pre + tok)
    vmem = pl.BlockSpec(memory_space=pltpu.VMEM)
    pairs = rows * rows // 2 * heads
    return pl.pallas_call(
        functools.partial(forward_kernel, devices, pre, tok, heads, head_dim),
        out_shape=(
            jax.ShapeDtypeStruct((rows, width), BF16),
            jax.ShapeDtypeStruct((width, rows), F32),
            jax.ShapeDtypeStruct((8, rows), F32),
        ),
        in_specs=[pl.BlockSpec(memory_space=pltpu.SMEM)] + [vmem] * (3 + len(chunks)),
        out_specs=(vmem,) * 3,
        scratch_shapes=[
            pltpu.VMEM((rows, width), BF16),
            pltpu.VMEM((rows, width), BF16),
            pltpu.VMEM((rows, width), BF16),
            pltpu.VMEM((width, rows), BF16),
            pltpu.VMEM((width, BLOCK), F32),
        ],
        compiler_params=pltpu.CompilerParams(vmem_limit_bytes=48 << 20),
        cost_estimate=pl.CostEstimate(
            flops=16 * pairs * head_dim, bytes_accessed=rows * width * 12, transcendentals=pairs
        ),
    )(spots, place, low, high, *chunks)


def backward_kernel(
    devices, pre, tok, heads, head_dim, first, last, carried, final, *refs
):
    chips = devices // 2
    spot_ref, ot_ref, lse_ref, place_ref, low_ref, high_ref = refs[:6]
    chunks = refs[6 : 6 + chips]
    grads = refs[6 + chips : 6 + 2 * chips]
    refs = refs[6 + 2 * chips :]
    if carried:
        dq_in, dk_in, dv_in = refs[:3]
        refs = refs[3:]
    if final:
        out_ref, near_ref = refs[:2]
        q_s, k_s, v_s, do_s, kt_s, dqt_s, dq_s, dk_s, dv_s = refs[2:]
    else:
        dq_s, dk_s, dv_s, q_s, k_s, v_s, do_s, kt_s, dqt_s = refs
    width = heads * head_dim
    scale = 1.0 / math.sqrt(head_dim)
    for n, row, slot, cnt in block_pieces(devices, pre, tok, spot_ref, 1, chips):
        q_s[pl.ds(slot, cnt), :] = chunks[n][row : row + cnt, 0:width]
        k_s[pl.ds(slot, cnt), :] = chunks[n][row : row + cnt, width : 2 * width]
        v_s[pl.ds(slot, cnt), :] = chunks[n][row : row + cnt, 2 * width : 3 * width]
    for n, row, slot, cnt in block_pieces(devices, pre, tok, spot_ref, 1 + chips, chips):
        do_s[pl.ds(slot, cnt), :] = grads[n][row : row + cnt, :]
    for b in range(last):
        rows = slice(b * BLOCK, (b + 1) * BLOCK)
        kt_s[:, rows] = k_s[rows, :].astype(F32).T.astype(BF16)
    if carried:
        dq_s[...] = dq_in[...]
        dk_s[...] = dk_in[...]
        dv_s[...] = dv_in[...]
    else:
        dk_s[...] = jnp.zeros_like(dk_s)
        dv_s[...] = jnp.zeros_like(dv_s)
    lane = lax.broadcasted_iota(jnp.int32, (BLOCK, width), 1) // head_dim

    def query_block(i, carry):
        qs = pl.ds(pl.multiple_of(i * BLOCK, BLOCK), BLOCK)
        q = q_s[qs, :]
        do = do_s[qs, :]
        qh = [jnp.where(lane == h, q, jnp.zeros_like(q)) for h in range(heads)]
        doh = [jnp.where(lane == h, do, jnp.zeros_like(do)) for h in range(heads)]
        qh_all = jnp.concatenate(qh, axis=0)
        doh_all = jnp.concatenate(doh, axis=0)
        low = low_ref[:, qs]
        high = high_ref[:, qs]
        prod = do.astype(F32).T * ot_ref[:, qs]
        delta = [
            jnp.sum(prod[h * head_dim : (h + 1) * head_dim, :], axis=0, keepdims=True)
            for h in range(heads)
        ]
        lse = [lse_ref[h : h + 1, qs] for h in range(heads)]
        dqt_s[...] = jnp.zeros_like(dqt_s)

        def key_block(j, inner):
            ks = pl.ds(pl.multiple_of(j * BLOCK, BLOCK), BLOCK)
            k = k_s[ks, :]
            v = v_s[ks, :]
            bias = jnp.where(block_mask(place_ref[ks, :], low, high), 0.0, NEGATIVE)
            s = [contract(k, qh[h], 1, 1) for h in range(heads)]
            dp = [contract(v, doh[h], 1, 1) for h in range(heads)]
            p = [jnp.exp(s[h] + (bias - lse[h])) for h in range(heads)]
            ds = [(p[h] * (dp[h] - delta[h])).astype(BF16) for h in range(heads)]
            dv = contract(jnp.concatenate([p[h].astype(BF16) for h in range(heads)], axis=1), doh_all, 1, 0)
            dk = contract(jnp.concatenate(ds, axis=1), qh_all, 1, 0)
            for h in range(heads):
                hs = slice(h * head_dim, (h + 1) * head_dim)
                dqt_s[hs, :] += contract(kt_s[hs, ks], ds[h], 1, 0)
            dk_s[ks, :] += dk
            dv_s[ks, :] += dv
            return inner

        lax.fori_loop(
            0, (i + 1) // 4, lambda j, inner: key_block(4 * j + 3, key_block(4 * j + 2, key_block(4 * j + 1, key_block(4 * j, inner)))), 0
        )
        lax.fori_loop((i + 1) // 4 * 4, i + 1, key_block, 0)
        dq_s[qs, :] = (dqt_s[...] * scale).T.astype(BF16)
        return carry

    lax.fori_loop(first, last, query_block, 0)
    if final:
        for row, slot, cnt in result_pieces(devices, pre, tok, spot_ref):
            out_ref[row : row + cnt, 0:width] = dq_s[pl.ds(slot, cnt), :]
            out_ref[row : row + cnt, width : 2 * width] = dk_s[pl.ds(slot, cnt), :].astype(BF16)
            out_ref[row : row + cnt, 2 * width : 3 * width] = dv_s[pl.ds(slot, cnt), :].astype(BF16)
        both = 2 * (pre + tok)
        for n in range(chips):
            chip = pl.multiple_of(spot_ref[1 + n] * both, 16)
            near_ref[n * both : (n + 1) * both, :] = out_ref[pl.ds(chip, both), :]


def attention_backward(
    chunks, grads, spots, ot, lse, place, low, high, devices, pre, tok, heads, head_dim, first, last, carry, final
):
    width = heads * head_dim
    rows = devices * (pre + tok)
    vmem = pl.BlockSpec(memory_space=pltpu.VMEM)
    pairs = (last - first) * (last + first + 1) // 2 * BLOCK * BLOCK * heads
    low_rows = pltpu.VMEM((rows, width), BF16)
    sums = [((rows, width), BF16), ((rows, width), F32), ((rows, width), F32)]
    scratch = [
        low_rows,
        low_rows,
        low_rows,
        low_rows,
        pltpu.VMEM((width, rows), BF16),
        pltpu.VMEM((width, BLOCK), F32),
    ]
    if final:
        out_shape = (jax.ShapeDtypeStruct((rows, 3 * width), BF16),) * 2
        scratch += [pltpu.VMEM(shape, dtype) for shape, dtype in sums]
    else:
        out_shape = tuple(jax.ShapeDtypeStruct(shape, dtype) for shape, dtype in sums)
    return pl.pallas_call(
        functools.partial(
            backward_kernel, devices, pre, tok, heads, head_dim, first, last, bool(carry), final
        ),
        out_shape=out_shape,
        in_specs=[pl.BlockSpec(memory_space=pltpu.SMEM)]
        + [vmem] * (5 + len(chunks) + len(grads) + len(carry)),
        out_specs=(vmem,) * len(out_shape),
        scratch_shapes=scratch,
        compiler_params=pltpu.CompilerParams(vmem_limit_bytes=58 << 20),
        cost_estimate=pl.CostEstimate(
            flops=20 * pairs * head_dim, bytes_accessed=rows * width * 20, transcendentals=pairs
        ),
    )(spots, ot, lse, place, low, high, *chunks, *grads, *carry)


def matmul_kernel(flipped, left_ref, right_ref, out_ref):
    out_ref[...] = contract(left_ref[...], right_ref[...], 1, 1 if flipped else 0).astype(BF16)


def matmul_low(left, right, flipped):
    rows, depth = left.shape
    columns = right.shape[0] if flipped else right.shape[1]
    step = 512
    block = (step, depth) if flipped else (depth, step)
    return pl.pallas_call(
        functools.partial(matmul_kernel, flipped),
        grid=(columns // step,),
        out_shape=jax.ShapeDtypeStruct((rows, columns), BF16),
        in_specs=[
            pl.BlockSpec((rows, depth), lambda n: (0, 0)),
            pl.BlockSpec(block, (lambda n: (n, 0)) if flipped else (lambda n: (0, n))),
        ],
        out_specs=pl.BlockSpec((rows, step), lambda n: (0, n)),
        compiler_params=pltpu.CompilerParams(vmem_limit_bytes=48 << 20),
        cost_estimate=pl.CostEstimate(flops=1 << 20, bytes_accessed=1 << 16, transcendentals=0),
    )(left, right)


def transposed_kernel(left_ref, right_ref, out_ref):
    out_ref[...] = contract(left_ref[...], right_ref[...], 0, 0).astype(BF16)


def matmul_transposed(left, right):
    depth, rows = left.shape
    columns = right.shape[1]
    step = 512
    return pl.pallas_call(
        transposed_kernel,
        grid=(rows // step,),
        out_shape=jax.ShapeDtypeStruct((rows, columns), BF16),
        in_specs=[
            pl.BlockSpec((depth, step), lambda n: (0, n)),
            pl.BlockSpec((depth, columns), lambda n: (0, 0)),
        ],
        out_specs=pl.BlockSpec((step, columns), lambda n: (n, 0)),
        compiler_params=pltpu.CompilerParams(vmem_limit_bytes=56 << 20),
        cost_estimate=pl.CostEstimate(flops=1 << 20, bytes_accessed=1 << 16, transcendentals=0),
    )(left, right)


def rows_product_kernel(*refs):
    chunks, right_ref, out_ref = refs[:-2], refs[-2], refs[-1]
    rows = chunks[0].shape[0]
    total = contract(chunks[0][...], right_ref[0:rows, :], 0, 0)
    for n in range(1, len(chunks)):
        total += contract(chunks[n][...], right_ref[n * rows : (n + 1) * rows, :], 0, 0)
    out_ref[...] = total.astype(BF16)


def rows_product(chunks, right):
    rows, columns = chunks[0].shape
    step = 512
    return pl.pallas_call(
        rows_product_kernel,
        grid=(columns // step,),
        out_shape=jax.ShapeDtypeStruct((columns, right.shape[1]), BF16),
        in_specs=[pl.BlockSpec((rows, step), lambda n: (0, n))] * len(chunks)
        + [pl.BlockSpec(right.shape, lambda n: (0, 0))],
        out_specs=pl.BlockSpec((step, right.shape[1]), lambda n: (n, 0)),
        compiler_params=pltpu.CompilerParams(vmem_limit_bytes=56 << 20),
        cost_estimate=pl.CostEstimate(
            flops=right.shape[0] * columns * right.shape[1] // 2, bytes_accessed=1 << 16, transcendentals=0
        ),
    )(*chunks, right)


def slot_labels(lengths, devices, pre, tok, real):
    slot = jnp.arange(devices * pre, dtype=jnp.int32)
    inside = slot % pre
    place = (slot // pre) * real + inside - devices * real
    is_real = inside < real
    t = jnp.arange(devices * tok, dtype=jnp.int32)
    ends = jnp.cumsum(lengths)
    start = jnp.max(jnp.where(ends[None, :] <= t[:, None], ends[None, :], 0), axis=1)
    places = jnp.concatenate([jnp.where(is_real, place, FAR), t])
    high = jnp.concatenate([jnp.where(is_real, place, -1), t])
    low = jnp.concatenate([jnp.full((devices * pre,), FAR, jnp.int32), start])
    return places[:, None], low[None, :], high[None, :]


def normalize(values):
    center = values - jnp.mean(values, axis=-1, keepdims=True)
    spread = jnp.mean(center * center, axis=-1, keepdims=True)
    inverse = lax.rsqrt(spread + EPS)
    return center * inverse, inverse


def norm_backward(grad, hat, inverse, gain):
    e = grad * gain
    mean_e = jnp.mean(e, axis=-1, keepdims=True)
    mean_eh = jnp.mean(e * hat, axis=-1, keepdims=True)
    return inverse * (e - mean_e - hat * mean_eh)


def gelu_parts(values):
    cdf = 0.5 * (1.0 + lax.erf(values * (1.0 / math.sqrt(2.0))))
    return cdf


def pick(array, index, axis):
    return lax.dynamic_index_in_dim(array, index, axis, keepdims=False)


def build(n_batch, n_seq):
    n_z = n_seq // 2
    n_dev = n_batch * n_seq
    groups = n_dev // 4
    size_of = {"batch": n_batch, "seq": n_seq}

    def bits_of(n):
        bits = []
        bit = 1
        while bit < n:
            bits.append(bit)
            bit *= 2
        return bits

    core = ("seq", 1)
    near = ("seq", 2)
    up_batch = [("batch", bit) for bit in bits_of(n_batch)]
    down_batch = list(reversed(up_batch))
    far_bits = [("seq", bit) for bit in bits_of(n_seq) if bit >= 4]
    chip_bits = [near] + far_bits
    group_bits = down_batch + list(reversed(far_bits))
    all_bits = down_batch + [("seq", bit) for bit in reversed(bits_of(n_seq))]

    def swap_pairs(which):
        axis, bit = which
        return axis, [(i, i ^ bit) for i in range(size_of[axis])]

    def shift_pairs(distance):
        return "seq", [
            (z * 2 + c, ((z + distance) % n_z) * 2 + c) for z in range(n_z) for c in range(2)
        ]

    def right_pairs(first, last):
        return "seq", [(z * 2 + c, z * 2 + 2 + c) for z in range(first, last) for c in range(2)]

    def left_pairs(first, last):
        return "seq", [(z * 2 + c, z * 2 - 2 + c) for z in range(first, last) for c in range(2)]

    def side(which):
        axis, bit = which
        return (lax.axis_index(axis) // bit) % 2

    def permute(array, pairs):
        return lax.ppermute(array, pairs[0], pairs[1])

    class Clock:
        def __init__(self):
            self.gate = ()

        def hold(self, *arrays):
            if self.gate:
                arrays = lax.optimization_barrier(tuple(arrays) + tuple(self.gate))[: len(arrays)]
            return arrays[0] if len(arrays) == 1 else arrays

        def tick(self, *arrays):
            self.gate = arrays

    def join(mine, other, which, axis):
        first = side(which) == 0
        return jnp.where(first, jnp.stack([mine, other], axis), jnp.stack([other, mine], axis))

    def body(
        tokens, prefix, seg_lengths, attn_gain, attn_shift, query_weight, key_weight, value_weight,
        query_bias, value_bias, output_weight, output_bias, mlp_gain, mlp_shift, up_weight, up_bias,
        down_weight, down_bias, cot_tokens, cot_prefix,
    ):
        clock = Clock()

        def swap(array, which):
            return permute(array, swap_pairs(which))

        def gather_bits(array, order, ranked):
            taken = []
            current = array
            for which in order:
                other = swap(current, which)
                rank = ranked.index(which)
                place = sum(1 for t in taken if ranked.index(t) < rank)
                current = join(current, other, which, place)
                taken.append(which)
            return current.reshape((2 ** len(order),) + array.shape)

        def part_of(current, left, which, mine):
            return pick(current, side(which) if mine else 1 - side(which), left.index(which))

        def hop_scatter(current, left, which, last):
            other = swap(part_of(current, left, which, False).astype(BF16), which)
            total = part_of(current, left, which, True).astype(F32) + other.astype(F32)
            rest = [b for b in left if b != which]
            return (total if last else total.astype(BF16)), rest

        tok = tokens.shape[1]
        real = prefix.shape[1]
        pre = -(-real // 16) * 16
        width = pre + tok
        model = tokens.shape[2]
        heads = HEADS // n_seq
        span = heads * HEAD_DIM
        part = model // n_dev
        unit = up_bias.shape[0]
        hidden_here = groups * unit
        s_here = lax.axis_index("seq")
        z_here = s_here // 2
        c_here = s_here % 2
        near_here = side(near)
        lengths = seg_lengths[0]

        def rows_of(pre_part, tok_part):
            return jnp.concatenate([jnp.pad(pre_part, ((0, pre - real), (0, 0))), tok_part], axis=0)

        def device_rows(array, z, c):
            return lax.dynamic_slice_in_dim(array, (z * 2 + c) * width, width, 0)

        own = rows_of(prefix[0], tokens[0])
        row = jnp.arange(width, dtype=jnp.int32)
        position = row - pre + s_here * tok
        valid = jnp.where(row < pre, row < real, position < jnp.sum(lengths))
        validity = valid.astype(F32)[:, None]

        far_group = list(reversed(far_bits))
        n_far = groups // n_batch
        far_here = s_here // 4

        def afar(array, mask):
            return permute(array, ("seq", [(i, i ^ (mask * 4)) for i in range(n_seq)]))

        def batch_gather(array):
            return lax.all_gather(array, "batch", axis=0, tiled=True)

        def batch_sum(array):
            return lax.psum_scatter(array, "batch", scatter_dimension=0, tiled=True)

        def set_far(whole, blocks, index):
            blocks = blocks.reshape((n_batch, 1, -1) + blocks.shape[1:])
            return lax.dynamic_update_slice_in_dim(whole, blocks, index, 1)

        steps = [(permute(own, right_pairs(0, n_z - 1)), permute(own, left_pairs(1, n_z)))]
        small = jnp.concatenate(
            [attn_gain, attn_shift, query_bias, value_bias, output_bias, mlp_gain, mlp_shift, down_bias, up_bias]
        )
        small_bits = down_batch + [core]
        small = gather_bits(small, list(reversed(small_bits)), small_bits)
        down_gate, unused = lax.optimization_barrier((down_weight, small))
        down_own = batch_gather(down_gate)

        stacked = jnp.stack([query_weight, key_weight, value_weight], axis=1)
        stacked = stacked.reshape(part, 3, heads, n_z, 2, HEAD_DIM).transpose(3, 4, 0, 1, 2, 5)
        stacked = stacked.reshape(n_z, 2, part, 3 * span)
        mixed = join(pick(stacked, c_here, 1), swap(pick(stacked, 1 - c_here, 1), core), core, 1)
        mixed = mixed.reshape(n_z, 2 * part, 3 * span)
        flat = small.reshape(-1)
        small_rows = -(-flat.shape[0] // (3 * span * 16)) * 16
        flat = jnp.pad(flat, (0, small_rows * 3 * span - flat.shape[0]))
        flat = jnp.broadcast_to(flat.reshape(1, small_rows, 3 * span), (n_z, small_rows, 3 * span))
        mixed = jnp.concatenate([mixed, flat], axis=1)

        up_near = up_weight.reshape(part, groups, 2, 2, unit)
        up_near = join(pick(up_near, c_here, 3), swap(pick(up_near, 1 - c_here, 3), core), core, 0)

        clock.tick(*steps[0], up_near)

        def shift_out(choose):
            pieces = [choose((z_here + d) % n_z) for d in range(1, n_z)]
            pieces = clock.hold(*pieces) if len(pieces) > 1 else [clock.hold(*pieces)]
            got = [permute(piece, shift_pairs(d + 1)) for d, piece in enumerate(pieces)]
            return [(z_here, choose(z_here))] + [
                ((z_here - d - 1) % n_z, piece) for d, piece in enumerate(got)
            ]

        placed = shift_out(lambda z: pick(mixed, z, 0))
        ranked_o = far_group + [near]
        up_other = swap(clock.hold(pick(up_near, 1 - near_here, 3)), near)
        gathered_o = gather_bits(clock.hold(output_weight), far_bits, far_group)
        clock.tick(up_other, gathered_o, *[piece for unused, piece in placed[1:]])
        up_block = join(pick(up_near, near_here, 3), up_other, near, 0)
        up_block = up_block.reshape(4 * part, hidden_here)
        local = jnp.zeros((n_z, 2 * part, 3 * span), BF16)
        small_z = jnp.zeros((n_z, small_rows, 3 * span), BF16)
        for z, piece in placed:
            local = lax.dynamic_update_slice_in_dim(local, piece[None, : 2 * part], z, 0)
            small_z = lax.dynamic_update_slice_in_dim(small_z, piece[None, 2 * part :], z, 0)
        local, unused = lax.optimization_barrier((local, down_own))
        weight_qkv = batch_gather(local.reshape(n_z * 2 * part, 3 * span))
        small = small_z.reshape(n_z, -1)[:, : n_batch * 2 * (8 * part + unit)]
        small = small.reshape(n_z, n_batch, 2, 8 * part + unit).transpose(1, 0, 2, 3)
        small = small.reshape(n_dev, 8 * part + unit)
        vectors = [small[:, n * part : (n + 1) * part].reshape(model).astype(F32) for n in range(8)]
        gain_a, shift_a, bias_q, bias_v, bias_o, gain_m, shift_m, bias_down = vectors
        bias_up = pick(small[:, 8 * part :].reshape(groups, 4, unit), s_here % 4, 1)
        bias_up = bias_up.reshape(hidden_here).astype(F32)

        bias_qkv = jnp.concatenate(
            [
                pick(bias_q.reshape(heads, n_seq, HEAD_DIM), s_here, 1).reshape(span),
                jnp.zeros((span,), F32),
                pick(bias_v.reshape(heads, n_seq, HEAD_DIM), s_here, 1).reshape(span),
            ]
        )
        factor = jnp.concatenate(
            [jnp.full((span,), 1.0 / math.sqrt(HEAD_DIM), F32), jnp.ones((2 * span,), F32)]
        )

        def source(n):
            if n == 0:
                return z_here
            short = jnp.minimum(z_here, n_z - 1 - z_here)
            both = n <= 2 * short
            distance = jnp.where(both, (n + 1) // 2, n - short)
            left = jnp.where(both, n % 2 == 1, 2 * z_here >= n_z)
            return jnp.where(left, z_here - distance, z_here + distance)

        def rows_from(n):
            rows = own
            for d in range((n + 1) // 2, n + 1) if n else ():
                right, left = steps[d - 1]
                rows = jnp.where(source(n) == z_here - d, right, rows)
                rows = jnp.where(source(n) == z_here + d, left, rows)
            rows = jnp.concatenate([rows, swap(rows, core)], axis=0)
            hat, unused = normalize(rows.astype(F32))
            return (hat * gain_a + shift_a).astype(BF16)

        def qkv_of(rows):
            result = (contract(rows, weight_qkv, 1, 0) + bias_qkv).astype(BF16).astype(F32) * factor
            return result.astype(BF16)

        exact = part == HEAD_DIM and heads == n_batch
        normed = []
        for k in range(2, n_z):
            right, left = clock.hold(*steps[-1])
            steps.append(
                (permute(right, right_pairs(k - 1, n_z - 1)), permute(left, left_pairs(1, n_z - k + 1)))
            )
            normed.append(rows_from(k - 2))
            clock.tick(*steps[-1], normed[-1])
        up_gate, unused = lax.optimization_barrier((up_block, weight_qkv))
        up_own = batch_gather(up_gate)

        other = swap(clock.hold(gathered_o), near)
        gathered_o = join(gathered_o, other, near, 1)
        gathered_o, unused = lax.optimization_barrier((gathered_o, up_own))
        gathered_o = batch_gather(gathered_o.reshape(n_z * part, model))

        weight_o = gathered_o.reshape(n_batch, n_z, part, model)
        if exact:
            weight_o = weight_o.transpose(1, 0, 2, 3).reshape(n_z * span, model)
        else:
            weight_o = join(weight_o, swap(weight_o, core), core, 2)
            weight_o = weight_o.reshape(heads, n_z, 2, HEAD_DIM, model)
            weight_o = pick(weight_o, c_here, 2).transpose(1, 0, 2, 3).reshape(n_z * span, model)

        qkv = []
        for n in range(n_z):
            if n >= n_z - 2:
                normed.append(rows_from(n))
            qkv.append(qkv_of(normed[n]))
        shifted = [z_here] + [(z_here - d) % n_z for d in range(1, n_z)]
        spots = jnp.stack([c_here] + [source(n) for n in range(n_z)] + shifted).astype(jnp.int32)

        cot_rows = rows_of(cot_prefix[0], cot_tokens[0]).astype(F32)
        mlp_out_grad = (validity * cot_rows).astype(BF16)
        places, low, high = slot_labels(lengths, n_seq, pre, tok, real)
        clock.tick(other)
        *qkv, up_gate, grad_gate = clock.hold(*qkv, up_block, mlp_out_grad)
        up_far = [afar(up_gate, mask) for mask in range(1, n_far)]
        grad_far = swap(grad_gate, near)
        attended, attended_t, log_total = attention_forward(
            qkv, spots, places, low, high, n_seq, pre, tok, heads, HEAD_DIM
        )
        clock.tick(attended, grad_far, *up_far)
        up_blocks = [batch_gather(clock.hold(piece)) for piece in up_far]

        blocks = attended.reshape(n_z, 2 * width, span)
        placed = shift_out(lambda z: pick(blocks, z, 0))
        *normed, up_own, down_own, unused = lax.optimization_barrier(
            tuple(normed) + (up_own, down_own, attended)
        )
        weight_up = set_far(
            jnp.zeros((n_batch, n_far, 4 * part, hidden_here), BF16), up_own, far_here
        )
        weight_down = set_far(
            jnp.zeros((n_batch, n_far, unit, model), BF16), down_own, far_here
        )
        grad_rows = jnp.concatenate(
            [mlp_out_grad, swap(mlp_out_grad, core), grad_far, swap(grad_far, core)], axis=0
        )
        spread_o = [piece for unused, piece in placed[1:]]
        *spread_o, weight_up, weight_down, weight_o = lax.optimization_barrier(
            (*spread_o, weight_up, weight_down, weight_o)
        )
        placed = [placed[0]] + [(z, piece) for (z, unused), piece in zip(placed[1:], spread_o)]
        mixed_low = jnp.zeros((2 * width, n_z * span), BF16)
        for z, piece in placed:
            mixed_low = lax.dynamic_update_slice_in_dim(mixed_low, piece, z * span, 1)
        clock.tick(mixed_low, weight_up, weight_down)
        down_far = [afar(clock.hold(down_weight), mask) for mask in range(1, n_far)]
        mixed_held = clock.hold(mixed_low)
        branch_away = contract(mixed_held[width:], weight_o, 1, 0).astype(BF16)
        branch_away = swap(branch_away, core)
        branch = contract(mixed_held[:width], weight_o, 1, 0) + branch_away.astype(F32) + bias_o
        rows_in = own.astype(F32)
        resid = rows_in + validity * branch
        hat_m, inverse_m = normalize(resid)
        normed_own = (hat_m * gain_m + shift_m).astype(BF16)

        normed_near = swap(normed_own, core)
        normed_far = swap(normed_own, near)
        *down_far, unused = lax.optimization_barrier(tuple(down_far) + (normed_own,))
        down_blocks = [batch_gather(piece) for piece in down_far]
        *up_blocks, unused = lax.optimization_barrier(tuple(up_blocks) + (normed_own,))
        for mask, piece in enumerate(up_blocks):
            weight_up = set_far(weight_up, piece, far_here ^ (mask + 1))
        weight_up = weight_up.reshape(model, hidden_here)
        normed_far, weight_up = lax.optimization_barrier((normed_far, weight_up))
        normed_parts = [normed_own, normed_near, normed_far, swap(normed_far, core)]
        normed_rows = jnp.concatenate(normed_parts, axis=0)

        before = contract(normed_rows, weight_up, 1, 0) + bias_up
        cdf = 0.5 * (1.0 + lax.erf(before * (1.0 / math.sqrt(2.0))))
        hidden = (before * cdf).astype(BF16)
        slope = cdf + before * jnp.exp(-0.5 * before * before) * (1.0 / math.sqrt(2.0 * math.pi))
        *down_blocks, unused = lax.optimization_barrier(tuple(down_blocks) + (hidden,))
        for mask, piece in enumerate(down_blocks):
            weight_down = set_far(weight_down, piece, far_here ^ (mask + 1))
        weight_down = weight_down.reshape(hidden_here, model)
        grad_down = contract(hidden, grad_rows, 0, 0).astype(BF16)
        grad_down, grad_held = lax.optimization_barrier((grad_down, grad_rows))
        grad_down = batch_sum(grad_down)
        hidden_grad = contract(grad_held, weight_down, 1, 1)
        pre_grad = (hidden_grad * slope).astype(BF16)

        share_f = contract(pre_grad[2 * width :], weight_up, 1, 1).astype(BF16)
        back = swap(share_f[width:], core)
        back = (share_f[:width].astype(F32) + back.astype(F32)).astype(BF16)
        pre_held, hidden_held, back_held = lax.optimization_barrier((pre_grad, hidden, back))
        back = swap(back_held, near)
        share_n = matmul_low(pre_held[: 2 * width], weight_up, True)
        out_share = matmul_low(hidden_held, weight_down, False)
        *normed_late, unused = lax.optimization_barrier((*normed_parts, back_held))
        normed_late = jnp.concatenate(normed_late, axis=0)
        back, out_share, share_n, normed_late = lax.optimization_barrier(
            (back, out_share, share_n, normed_late)
        )
        here = swap(share_n[width:], core)
        normed_grad = share_n[:width].astype(F32) + here.astype(F32) + back.astype(F32)

        grad_up_bias = jnp.sum(pre_grad.astype(F32), axis=0)
        grad_down_bias = jnp.sum(mlp_out_grad.astype(F32), axis=0)
        grad_gain_m = jnp.sum(normed_grad * hat_m, axis=0)
        grad_shift_m = jnp.sum(normed_grad, axis=0)
        resid_grad = cot_rows + norm_backward(normed_grad, hat_m, inverse_m, gain_m)

        branch_grad = (validity * resid_grad).astype(BF16)
        grad_out_bias = jnp.sum(branch_grad.astype(F32), axis=0)
        branch_grad = jnp.concatenate([branch_grad, swap(branch_grad, core)], axis=0)
        mixed_grad = contract(branch_grad, weight_o, 1, 1).astype(BF16)
        clock.tick(mixed_grad)
        placed = shift_out(lambda z: lax.dynamic_slice_in_dim(mixed_grad, z * span, span, 1))
        grad_gate, branch_gate, mixed_gate, unused = lax.optimization_barrier(
            (pre_grad, branch_grad, mixed_low, mixed_grad)
        )
        grad_up = matmul_transposed(normed_late, grad_gate)
        grad_out = matmul_transposed(mixed_gate, branch_gate)
        if exact:
            grad_out = grad_out.reshape(n_z, n_batch, part, model).transpose(1, 0, 2, 3)
        else:
            full = jnp.zeros((heads, n_z, 2, HEAD_DIM, model), BF16)
            grad_out = grad_out.reshape(n_z, heads, 1, HEAD_DIM, model).transpose(1, 0, 2, 3, 4)
            grad_out = lax.dynamic_update_slice_in_dim(full, grad_out, c_here, 2)
            grad_out = grad_out.reshape(n_batch, n_z, 2, part, model)
            grad_out = pick(grad_out, c_here, 2).astype(F32) + swap(
                pick(grad_out, 1 - c_here, 2), core
            ).astype(F32)
            grad_out = grad_out.astype(BF16)
        rows_grad = [piece for unused, piece in placed]
        out_back = swap(out_share[3 * width :], core)
        out_back = (out_share[2 * width : 3 * width].astype(F32) + out_back.astype(F32)).astype(BF16)
        grad_up, grad_out, out_back, *rows_grad = lax.optimization_barrier(
            (grad_up, grad_out, out_back, *rows_grad)
        )
        grad_up = batch_sum(grad_up)
        grad_out = batch_sum(grad_out.reshape(n_batch * n_z * part, model))

        clock.tick(*rows_grad, grad_down, out_share)
        down_gate, out_away, *rows_grad = clock.hold(grad_down, out_back, *rows_grad)
        down_sum = down_gate.reshape((2,) * len(far_bits) + (unit, model))
        rest_down = list(far_group)
        for n, which in enumerate(far_bits):
            down_sum, rest_down = hop_scatter(
                down_sum, rest_down, which, n == len(far_bits) - 1
            )
        grad_down = down_sum
        out_back = swap(out_away, near)
        blocks = n_seq * width // BLOCK
        qkv_grad, relative = attention_backward(
            qkv, rows_grad, spots, attended_t, log_total, places, low, high,
            n_seq, pre, tok, heads, HEAD_DIM, 0, blocks, (), True,
        )
        qkv_grad, relative, grad_down, out_back = lax.optimization_barrier(
            (qkv_grad, relative, grad_down, out_back)
        )
        clock.tick(qkv_grad, grad_down, out_back)

        chunks = [None] * n_z
        aways = []
        order = []
        for k in range(1, n_z):
            for r in (n_z - k, k):
                if r not in order:
                    order.append(r)
        for r in order + [0]:
            z = (z_here + r) % n_z
            away = contract(device_rows(qkv_grad, z, 1), weight_qkv, 1, 1).astype(BF16)
            away = swap(away, core)
            aways.append(away)
            keep = contract(device_rows(qkv_grad, z, 0), weight_qkv, 1, 1)
            chunks[r] = keep + away.astype(F32)
        right = None
        left = None
        for k in range(1, n_z):
            going_r = jnp.where(z_here + n_z - k < n_z, chunks[n_z - k], 0.0)
            going_l = jnp.where(z_here - (n_z - k) >= 0, chunks[k], 0.0)
            if k > 1:
                going_r = going_r + right.astype(F32)
                going_l = going_l + left.astype(F32)
            going_r, going_l = clock.hold(going_r.astype(BF16), going_l.astype(BF16))
            right = permute(going_r, right_pairs(0, k))
            left = permute(going_l, left_pairs(n_z - k, n_z))
            started = [right, left]
            if k == 1:
                up_sum = clock.hold(grad_up).reshape((2,) * len(far_bits) + (4 * part, hidden_here))
                rest_up = list(far_group)
                for which in far_bits:
                    up_sum, rest_up = hop_scatter(up_sum, rest_up, which, False)
                relative, unused = lax.optimization_barrier((relative, going_r))
                grad_qkv = rows_product(normed, relative)
                grad_qkv, right, left, up_sum, grad_out, unused = lax.optimization_barrier(
                    (grad_qkv, right, left, up_sum, grad_out, tuple(aways[2:]))
                )
                grad_qkv = batch_sum(grad_qkv)
                started = [right, left, up_sum]
            if k == 2:
                grad_up = up_sum.reshape(2, 2, part, hidden_here)
                up_other = swap(clock.hold(pick(grad_up, 1 - near_here, 0)), near)
                grad_up = join(pick(grad_up, near_here, 0), up_other, near, 0)
                rest_o = list(ranked_o)
                grad_out = clock.hold(grad_out).reshape((2,) * len(ranked_o) + (part, model))
                grad_out, rest_o = hop_scatter(grad_out, rest_o, near, False)
                started += [up_other, grad_out]
            if k == n_z - 1:
                grad_qkv = grad_qkv.reshape(n_z, 2, part, 3 * span)
                grad_qkv = join(
                    pick(grad_qkv, c_here, 1), swap(pick(grad_qkv, 1 - c_here, 1), core), core, 1
                )
                placed = shift_out(lambda z: pick(grad_qkv, z, 0))
                out_share, out_back, grads_late = clock.hold(out_share, out_back, qkv_grad)
                out_here = swap(out_share[width : 2 * width], core)
                final = out_share[:width].astype(F32) + out_here.astype(F32) + out_back.astype(F32)
                final = resid + validity * (final + bias_down)
                out_rows = final.astype(BF16)
                bias_sums = jnp.sum(grads_late.astype(F32), axis=0)
                grad_out = clock.hold(grad_out)
                for n, which in enumerate(far_bits):
                    grad_out, rest_o = hop_scatter(grad_out, rest_o, which, n == len(far_bits) - 1)
            clock.tick(*started)
        right, left, unused = lax.optimization_barrier(
            (right, left, (out_rows, bias_sums, *[piece for unused, piece in placed[1:]]))
        )
        normed_back = chunks[0] + right.astype(F32) + left.astype(F32)

        grad_up = join(pick(grad_up, c_here, 1), swap(pick(grad_up, 1 - c_here, 1), core), core, 1)
        grad_up = grad_up.reshape(4, part, groups, unit).transpose(1, 2, 0, 3)
        grad_up = grad_up.reshape(part, n_dev * unit).astype(F32)


        shares = jnp.zeros((n_z, 2, part, 3 * span), BF16)
        for z, piece in placed:
            shares = lax.dynamic_update_slice_in_dim(shares, piece[None], z, 0)
        shares = shares.reshape(n_seq, part, 3, heads, HEAD_DIM)
        shares = [
            shares[:, :, n].transpose(1, 2, 0, 3).reshape(part, model).astype(F32) for n in range(3)
        ]

        hat_a, inverse_a = normalize(rows_in)
        grad_gain_a = jnp.sum(normed_back * hat_a, axis=0)
        grad_shift_a = jnp.sum(normed_back, axis=0)
        input_grad = resid_grad + norm_backward(normed_back, hat_a, inverse_a, gain_a)

        zero = jnp.zeros((heads, n_seq, HEAD_DIM), F32)

        def spread(sums):
            sums = sums.reshape(heads, 1, HEAD_DIM)
            return lax.dynamic_update_slice_in_dim(zero, sums, s_here, 1).reshape(model)

        full_up_bias = lax.dynamic_update_slice_in_dim(
            jnp.zeros((groups, 4, unit), F32), grad_up_bias.reshape(groups, 1, unit), s_here % 4, 1
        ).reshape(n_dev, unit)
        sums = jnp.concatenate(
            [
                vector.reshape(n_dev, part)
                for vector in (
                    grad_gain_a, grad_shift_a, spread(bias_sums[:span]), spread(bias_sums[2 * span :]),
                    grad_out_bias, grad_gain_m, grad_shift_m, grad_down_bias,
                )
            ]
            + [full_up_bias],
            axis=1,
        )
        sums, unused = lax.optimization_barrier((sums, tuple(shares)))
        current = jnp.sum(lax.all_to_all(sums, ("batch", "seq"), 0, 0, tiled=True), axis=0)
        small_grads = [current[n * part : (n + 1) * part] for n in range(8)]

        return (
            out_rows[pre:][None],
            out_rows[:real][None],
            input_grad[pre:][None],
            input_grad[:real][None],
            small_grads[0],
            small_grads[1],
            shares[0],
            shares[1],
            shares[2],
            small_grads[2],
            small_grads[3],
            grad_out,
            small_grads[4],
            small_grads[5],
            small_grads[6],
            grad_up,
            current[8 * part :],
            grad_down,
            small_grads[7],
        )

    return body


def solution(mesh):
    rows = P("batch", "seq", None)
    vector = P(("batch", "seq"))
    matrix = P(("batch", "seq"), None)
    return jax.shard_map(
        build(mesh.shape["batch"], mesh.shape["seq"]),
        mesh=mesh,
        in_specs=(
            rows, rows, P("batch", None), vector, vector, matrix, matrix, matrix, vector, vector,
            matrix, vector, vector, vector, matrix, vector, matrix, vector, rows, rows,
        ),
        out_specs=(
            rows, rows, rows, rows, vector, vector, matrix, matrix, matrix, vector, vector, matrix,
            vector, vector, vector, matrix, vector, matrix, vector,
        ),
        check_vma=False,
    )
```
